32 devices in a mesh: seq: 16 (over z, y, x), ch: 2 (over core).
Axes of the slice: x: 2, y: 2, z: 4, core: 2. Of those that a mesh axis runs over, the one named last changes fastest.
Arguments:
- stream_one: bfloat16 [2048, 2048], P('seq', 'ch'), may hold values from -6 to 6
- stream_two: bfloat16 [2048, 2048], P('seq', 'ch'), may hold values from -6 to 6
- stream_value: bfloat16 [2048, 2048], P('seq', 'ch'), may hold values from -6 to 6
- long_filter: bfloat16 [2048, 2048], P('seq', 'ch'), may hold values from -4 to 4
- short_taps: float32 [3, 3, 2048], P(None, None, 'ch'), may hold values from -3.5 to 3.5
- skip_gain: float32 [2048], P('ch'), may hold values from -1 to 1
- out_grad: bfloat16 [2048, 2048], P('seq', 'ch'), may hold values from -0.59765625 to 0.59765625
Outputs:
- mixed_out: bfloat16 [2048, 2048], P('seq', 'ch')
- grad_one: bfloat16 [2048, 2048], P('seq', 'ch')
- grad_two: bfloat16 [2048, 2048], P('seq', 'ch')
- grad_value: bfloat16 [2048, 2048], P('seq', 'ch')
- grad_filter: float32 [2048, 2048], P('seq', 'ch')
- grad_taps: float32 [3, 3, 2048], P(None, None, 'ch')
- grad_skip: float32 [2048], P('ch')
The draws below stay inside these ranges and needn't reach their ends.
All inputs are finite; a program needn't handle non-finite values.
Results may differ from the reference program's by a relative error of at most 0.0054.
Values may be sent and summed in bfloat16 or wider, within the bound.
No kernel may reach another device: no remote copies, remote signals or barrier semaphores. Data moves between devices by JAX's collectives and lax.ppermute only.
A program may use at most 128 MiB of HBM per device.

```python
import math
import jax
import jax.numpy as jnp
from jax import lax

HALF_MODEL_DIMS = 2048
TAPS = 3
STEP_COUNT = 2048
FFT_LEN = 4096


def draw_long_filter(key, part):
    key_noise = jax.random.fold_in(key, 11)
    key_rate = jax.random.fold_in(key, 12)
    placement_seed = jax.random.fold_in(key, 13)
    keeping_generator_start = jax.random.fold_in(key, 14)
    delay_ratio = jnp.arange(STEP_COUNT, dtype=jnp.float32)[:, None] / STEP_COUNT
    damping_rates = jnp.exp(jax.random.uniform(key_rate, (1, HALF_MODEL_DIMS), jnp.float32, math.log(0.02), math.log(200.0)))
    random_draws = jnp.clip(jax.random.normal(key_noise, (STEP_COUNT, HALF_MODEL_DIMS), jnp.float32), -4.0, 4.0)
    spike_shift_amount = jax.random.randint(placement_seed, (3, 1, HALF_MODEL_DIMS), 1, STEP_COUNT)
    spike_kept_mask = jax.random.uniform(keeping_generator_start, (3, 1, HALF_MODEL_DIMS), jnp.float32, 0.5, 0.8)
    chosen_slot_list = jnp.arange(STEP_COUNT, dtype=jnp.int32)[:, None]
    spike_shape_curve = jnp.ones((STEP_COUNT, HALF_MODEL_DIMS), jnp.float32)
    for spike_chooser in range(3):
        spike_shape_curve = spike_shape_curve * jnp.where(chosen_slot_list >= spike_shift_amount[spike_chooser], spike_kept_mask[spike_chooser], 1.0)
    magnitude_divisor = jnp.sqrt(2.0 * damping_rates / (STEP_COUNT * (1.0 - jnp.exp(-2.0 * damping_rates))))
    return (random_draws * jnp.exp(-damping_rates * delay_ratio) * spike_shape_curve * magnitude_divisor).astype(jnp.bfloat16)


def steps_of(own_key, dims, cuts, low, top_value):
    def one(axis_at, blocks):
        heights = jax.random.uniform(jax.random.fold_in(jax.random.fold_in(own_key, 6), axis_at), (blocks,), jnp.float32, low / len(cuts), top_value / len(cuts))
        return jnp.repeat(jnp.exp(heights), dims[axis_at] // blocks).reshape((-1,) + (1,) * (len(dims) - axis_at - 1))

    gain = one(*cuts[0])
    for cut in cuts[1:]:
        gain = gain * one(*cut)
    return gain


def gaussian(key, shape, width, limit, cuts=(), kind=jnp.bfloat16):
    drawn = width * jax.random.normal(key, shape, jnp.float32)
    if cuts:
        drawn = drawn * steps_of(key, shape, cuts, -0.22, 0.18)
    return jnp.clip(drawn, -limit, limit).astype(kind)


def setup_inputs(seed: int = 0) -> dict:
    keys = jax.random.split(jax.random.key(seed), 8)
    return {
        "stream_one": gaussian(keys[0], (STEP_COUNT, HALF_MODEL_DIMS), 1.0, 6.0, ((0, 16), (1, 2))),
        "stream_two": gaussian(keys[1], (STEP_COUNT, HALF_MODEL_DIMS), 1.0, 6.0, ((0, 16), (1, 2))),
        "stream_value": gaussian(keys[2], (STEP_COUNT, HALF_MODEL_DIMS), 1.0, 6.0, ((0, 16), (1, 2))),
        "long_filter": draw_long_filter(jax.random.fold_in(keys[7], 71), 0),
        "short_taps": gaussian(keys[4], (3, TAPS, HALF_MODEL_DIMS), TAPS ** -0.5, 3.5, ((2, 2),), jnp.float32),
        "skip_gain": jnp.clip(jax.random.uniform(keys[5], (HALF_MODEL_DIMS,), jnp.float32, -1.0, 1.0) * steps_of(keys[5], (HALF_MODEL_DIMS,), ((0, 2),), -0.4, 0.0), -1.0, 1.0),
        "out_grad": gaussian(keys[6], (STEP_COUNT, HALF_MODEL_DIMS), 0.1, 0.59765625, ((0, 16), (1, 2))),
    }


def short_filter(streams, short_taps):
    tap_count = short_taps.shape[1]
    padded = jnp.pad(streams, ((0, 0), (tap_count - 1, 0), (0, 0)))
    summed = jnp.zeros_like(streams)
    for offset in range(tap_count):
        first_row = tap_count - 1 - offset
        summed = summed + short_taps[:, offset, None, :] * padded[:, first_row:first_row + STEP_COUNT]
    return summed, padded


def causal_mix(signal, kernel):
    product = jnp.fft.rfft(signal, n=FFT_LEN, axis=0) * jnp.fft.rfft(kernel, n=FFT_LEN, axis=0)
    return jnp.fft.irfft(product, n=FFT_LEN, axis=0)[:STEP_COUNT].astype(jnp.float32)


def causal_match(signal, kernel):
    product = jnp.fft.rfft(signal, n=FFT_LEN, axis=0) * jnp.conj(jnp.fft.rfft(kernel, n=FFT_LEN, axis=0))
    return jnp.fft.irfft(product, n=FFT_LEN, axis=0)[:STEP_COUNT].astype(jnp.float32)


def reference(stream_one, stream_two, stream_value, long_filter, short_taps, skip_gain, out_grad):
    streams = jnp.stack([stream_one, stream_two, stream_value]).astype(jnp.float32)
    convolved, padded = short_filter(streams, short_taps)
    gate_out, gate_in, value_conv = convolved[0], convolved[1], convolved[2]
    cotangent = out_grad.astype(jnp.float32)
    mixed_in = lax.optimization_barrier((gate_in * value_conv).astype(jnp.bfloat16)).astype(jnp.float32)
    back_grad = lax.optimization_barrier((cotangent * gate_out).astype(jnp.bfloat16)).astype(jnp.float32)
    filter_wide = long_filter.astype(jnp.float32)
    long_out = causal_mix(mixed_in, filter_wide) + skip_gain * mixed_in
    mixed_out = (gate_out * long_out).astype(jnp.bfloat16)
    grad_filter = causal_match(back_grad, mixed_in)
    grad_mixed_in = causal_match(back_grad, filter_wide) + skip_gain * back_grad
    grad_skip = jnp.sum(back_grad * mixed_in, axis=0)
    conv_grads = jnp.stack([cotangent * long_out, grad_mixed_in * value_conv, grad_mixed_in * gate_in])
    tap_count = short_taps.shape[1]
    taps_list = []
    for offset in range(tap_count):
        first_row = tap_count - 1 - offset
        taps_list.append(jnp.sum(conv_grads * padded[:, first_row:first_row + STEP_COUNT], axis=1))
    grad_taps = jnp.stack(taps_list, axis=1)
    trailing = jnp.pad(conv_grads, ((0, 0), (0, tap_count - 1), (0, 0)))
    grad_streams = jnp.zeros_like(conv_grads)
    for offset in range(tap_count):
        grad_streams = grad_streams + short_taps[:, offset, None, :] * trailing[:, offset:offset + STEP_COUNT]
    grad_streams = grad_streams.astype(jnp.bfloat16)
    return (mixed_out, grad_streams[0], grad_streams[1], grad_streams[2], grad_filter, grad_taps, grad_skip)
```

```python
import math

import jax
import jax.numpy as jnp
import ml_dtypes
import numpy as np
from jax import lax
from jax.experimental import pallas as pl
from jax.experimental.pallas import tpu as pltpu
from jax.sharding import PartitionSpec as P

HALF = 64
LANES = 2 * HALF
EXTRA = 16


def root(top, bottom):
    angle = math.pi * top / bottom
    return math.cos(angle), math.sin(angle)


def padded_dft(xs):
    m = len(xs)
    if m == 1:
        return [(xs[0], None), (xs[0], None)]
    even, odd = padded_dft(xs[0::2]), padded_dft(xs[1::2])
    out = [None] * (m + 1)
    for k in range(m // 2 + 1):
        (ar, ai), (br, bi) = even[k], odd[k]
        if k == 0:
            out[0], out[m] = (ar + br, None), (ar - br, None)
        elif 2 * k == m:
            out[k] = (ar, -br)
        else:
            c, s = root(k, m)
            if bi is None:
                tr, ti = br * c, br * -s
            else:
                tr, ti = br * c + bi * s, bi * c - br * s
            out[k] = (ar + tr, ti if ai is None else ai + ti)
            out[m - k] = (ar - tr, ti if ai is None else ti - ai)
    return out


def folded_sum(ys):
    m = len(ys) - 1
    if m == 1:
        return [ys[0][0] + ys[1][0]]
    even, odd = [], []
    for k in range(m // 2 + 1):
        (ar, ai), (br, bi) = ys[k], ys[m - k]
        if k == 0:
            even.append((ar + br, None))
            odd.append((ar - br, None))
        elif 2 * k == m:
            even.append((ar, None))
            odd.append((-ai, None))
        else:
            c, s = root(k, m)
            dr, di = ar - br, ai + bi
            even.append((ar + br, ai - bi))
            odd.append((dr * c - di * s, dr * s + di * c))
    out = [None] * m
    out[0::2], out[1::2] = folded_sum(even), folded_sum(odd)
    return out


def split_pair(values):
    high = values.astype(ml_dtypes.bfloat16)
    low = (values - high.astype(np.float64)).astype(ml_dtypes.bfloat16)
    return np.concatenate([high, low], axis=-1)


def dft_tables(blocks, tokens):
    period = 2 * blocks * tokens
    k1 = np.arange(blocks + 1)[:, None, None]
    k2 = np.arange(tokens)[None, :, None]
    place = np.arange(tokens)[None, None, :]
    angle = (2.0 * math.pi / period) * ((place * (k1 + 2 * blocks * k2)) % period)
    c, s = np.cos(angle), np.sin(angle)
    weight = np.where((k1 == 0) | (k1 == blocks), 1.0, 2.0) / period
    forward = np.concatenate([c, s], 2)
    inverse = np.concatenate([c.transpose(0, 2, 1), -s.transpose(0, 2, 1)], 2) * weight
    return split_pair(forward), split_pair(inverse)


def halves_swapped(values):
    return pltpu.roll(values, HALF, 1)


def interleave(first, second):
    low = lax.broadcasted_iota(jnp.int32, first.shape, 1) < HALF
    return (
        jnp.where(low, first, halves_swapped(second)),
        jnp.where(low, halves_swapped(first), second),
    )


def pack_kernel(one, two, value, filt, grad, out):
    tokens = one.shape[0]
    half = tokens // 2
    for pair in range(one.shape[1] // LANES):
        cols = slice(pair * LANES, (pair + 1) * LANES)
        tile = [ref[:, cols].astype(jnp.float32) for ref in (two, one, value, grad, filt)]
        parts = (
            (0, tokens, tile[0], tile[1]),
            (tokens, tokens, tile[2], tile[3]),
            (2 * tokens, half, tile[4][:half], tile[4][half:]),
        )
        for start, rows, first, second in parts:
            for side, piece in enumerate(interleave(first, second)):
                out[2 * pair + side, start : start + rows] = piece.astype(out.dtype)


def window_conv(window, weights, tokens):
    total = weights[0] * window[8 : 8 + tokens]
    for j in (1, 2):
        total = total + weights[j] * window[8 - j : 8 - j + tokens]
    return total


def owner_kernel(blocks, chunk, weights, ftab, itab, out, ug_ref, spec_ref, lg_ref, gf_ref, acc_ref):
    step = pl.program_id(0)
    tokens = ftab.shape[1]
    half = tokens // 2
    f32 = jnp.float32

    def block_rows(a, start):
        return chunk[a, start : start + tokens].astype(f32)

    def window(a, start):
        before = chunk[jnp.maximum(a - 1, 0), start + tokens - 16 : start + tokens].astype(f32)[8:]
        return jnp.concatenate([jnp.where(a > 0, before, 0.0), block_rows(a, start)], axis=0)

    w1 = [weights[j : j + 1] for j in range(3)]
    w2 = [weights[3 + j : 4 + j] for j in range(3)]

    @pl.when(step == 0)
    def _():
        @pl.loop(0, blocks)
        def _(a):
            c1 = window_conv(window(a, 0), w1, tokens)
            c2 = window_conv(window(a, tokens), w2, tokens)
            ug_ref[a] = (c1 * c2).astype(jnp.bfloat16).astype(f32)

        @pl.loop(0, tokens // 8)
        def _(r):
            at = pl.multiple_of(r * 8, 8)
            spectrum = padded_dft([ug_ref[a, pl.ds(at, 8)] for a in range(blocks)])
            for k, (real, imag) in enumerate(spectrum):
                spec_ref[k, pl.ds(at, 8), :LANES] = real
                spec_ref[k, pl.ds(tokens + at, 8), :LANES] = (
                    jnp.zeros_like(real) if imag is None else imag
                )

        @pl.loop(0, half // 16)
        def _(r):
            at = pl.multiple_of(r * 16, 16)
            tiles = [chunk[a, pl.ds(2 * tokens + at, 16)].astype(f32) for a in range(blocks)]
            low = lax.broadcasted_iota(jnp.int32, (8, LANES), 1) < HALF
            for sub in range(2):
                spectrum = padded_dft([t[8 * sub : 8 * sub + 8] for t in tiles])
                for k, pair in enumerate(spectrum):
                    for place, part in enumerate(pair):
                        part = jnp.zeros_like(pair[0]) if part is None else part
                        turned = halves_swapped(part)
                        row = place * tokens + at + 8 * sub
                        spec_ref[k, pl.ds(row, 8), LANES:] = jnp.where(low, part, turned)
                        spec_ref[k, pl.ds(row + half, 8), LANES:] = jnp.where(low, turned, part)

    def transform(table, values):
        high = values.astype(jnp.bfloat16)
        rest = (values - high.astype(f32)).astype(jnp.bfloat16)
        cos_high, sin_high, cos_low, sin_low = [
            table[0, :, i * tokens : (i + 1) * tokens] for i in range(4)
        ]
        left = jnp.concatenate(
            [
                jnp.concatenate([cos_high, sin_high, cos_low, sin_low], 1),
                jnp.concatenate([-sin_high, cos_high, -sin_low, cos_low], 1),
            ],
            0,
        )
        return jnp.dot(
            left, jnp.concatenate([high, high], 0), preferred_element_type=f32
        ) + jnp.dot(left[:, : 2 * tokens], rest, preferred_element_type=f32)

    spectral = transform(ftab, spec_ref[step])
    sign = jnp.where(lax.broadcasted_iota(jnp.int32, (tokens, LANES), 1) < HALF, 1.0, -1.0)
    ur, ui = spectral[:tokens, :LANES], spectral[tokens:, :LANES]
    hr, hi = spectral[:tokens, LANES:], spectral[tokens:, LANES:] * sign
    vr, vi = halves_swapped(ur), halves_swapped(ui)
    products = jnp.concatenate(
        [
            jnp.concatenate([ur * hr - ui * hi, ur * vr + ui * vi], 1),
            jnp.concatenate([ui * hr + ur * hi, vi * ur - vr * ui], 1),
        ],
        0,
    )
    spec_ref[step] = transform(itab, products)

    @pl.when(step == blocks)
    def _():
        skip = weights[6:7]
        low = lax.broadcasted_iota(jnp.int32, (8, LANES), 1) < HALF

        @pl.loop(0, tokens // 8)
        def _(r):
            at = pl.multiple_of(r * 8, 8)
            ys = [
                (spec_ref[k, pl.ds(at, 8), :LANES], spec_ref[k, pl.ds(tokens + at, 8), :LANES])
                for k in range(blocks + 1)
            ]
            for a, total in enumerate(folded_sum(ys)):
                lg_ref[a, pl.ds(at, 8)] = total + skip * ug_ref[a, pl.ds(at, 8)]

        @pl.loop(0, half // 8)
        def _(r):
            at = pl.multiple_of(r * 8, 8)
            ys = []
            for k in range(blocks + 1):
                pair = []
                for place in range(2):
                    row = place * tokens + at
                    top = spec_ref[k, pl.ds(row, 8), LANES:]
                    bottom = spec_ref[k, pl.ds(row + half, 8), LANES:]
                    pair.append(jnp.where(low, top, halves_swapped(bottom)))
                ys.append(tuple(pair))
            for a, total in enumerate(folded_sum(ys)):
                gf_ref[a, pl.ds(at, 8)] = total

        acc_ref[...] = jnp.zeros_like(acc_ref)

        def folded(values):
            total = values[:8]
            for r in range(1, tokens // 8):
                total = total + values[8 * r : 8 * r + 8]
            return total

        @pl.loop(0, blocks)
        def _(i):
            a = blocks - 1 - i
            one, two = window(a, 0), window(a, tokens)
            c1, c2 = window_conv(one, w1, tokens), window_conv(two, w2, tokens)
            lg = lg_ref[a]
            turned = halves_swapped(lg)
            x1, x2 = c2 * turned, c1 * turned
            ug = ug_ref[a]
            for j in range(3):
                acc_ref[j] += folded(x1 * one[8 - j : 8 - j + tokens])
                acc_ref[3 + j] += folded(x2 * two[8 - j : 8 - j + tokens])
            acc_ref[6] += folded(ug * halves_swapped(ug))
            after = acc_ref[7]
            out[a, :tokens] = lg.astype(out.dtype)
            out[a, tokens : tokens + half] = gf_ref[a].astype(out.dtype)
            out[a, tokens + half :] = jnp.concatenate(
                [after[:4], one[6:8], two[6:8], jnp.zeros((8, LANES), f32)], 0
            ).astype(out.dtype)
            acc_ref[7] = jnp.concatenate([x1[:2], x2[:2], jnp.zeros((4, LANES), f32)], 0)

        lower = lax.broadcasted_iota(jnp.int32, (1, LANES), 1) < HALF
        sums = [jnp.sum(acc_ref[j], axis=0, keepdims=True) for j in range(7)]
        sums[3] = jnp.where(lower, sums[3], sums[6])
        tail = jnp.concatenate(sums[:6] + [jnp.zeros((2, LANES), f32)], 0)

        @pl.loop(0, blocks)
        def _(a):
            rows = out[a, tokens + half :].astype(f32)
            out[a, tokens + half :] = jnp.concatenate([rows[:8], tail], 0).astype(out.dtype)


def finish(streams, cotangent, weights, low, high):
    tokens = streams[0].shape[0]
    half = tokens // 2
    at = tokens + half
    long_out, grad_mixed = low[:tokens], high[:tokens]
    grad_filter = jnp.concatenate([low[tokens:at], high[tokens:at]], 0)
    before = (high[at + 4 : at + 6], low[at + 4 : at + 6], low[at + 6 : at + 8])
    after = (high[at : at + 2], low[at : at + 2], low[at + 2 : at + 4])
    gates = []
    for s in range(3):
        window = jnp.concatenate([jnp.zeros_like(low[:6]), before[s], streams[s]], 0)
        gates.append(window_conv(window, [weights[3 * s + j] for j in range(3)], tokens))
    mixed_out = gates[0] * long_out
    conv_grads = (cotangent * long_out, grad_mixed * gates[2], grad_mixed * gates[1])
    grads = []
    for s in range(3):
        trailing = jnp.concatenate([conv_grads[s], after[s], jnp.zeros_like(low[:6])], 0)
        total = weights[3 * s] * trailing[:tokens]
        for j in (1, 2):
            total = total + weights[3 * s + j] * trailing[j : j + tokens]
        grads.append(total)
    sums = jnp.concatenate(
        [high[at + 8 : at + 11], low[at + 8 : at + 11], low[at + 11 : at + 14], high[at + 11 : at + 12]], 0
    )
    return [mixed_out] + grads + [grad_filter, sums]


def finish_kernel(one, two, value, grad, weights, back, *outs):
    rows = back.shape[1]
    for pair in range(one.shape[1] // LANES):
        cols = slice(pair * LANES, (pair + 1) * LANES)
        low, high = interleave(
            back[2 * pair].astype(jnp.float32), back[2 * pair + 1].astype(jnp.float32)
        )
        streams = [ref[:, cols].astype(jnp.float32) for ref in (one, two, value)]
        results = finish(
            streams,
            grad[:, cols].astype(jnp.float32),
            [weights[i : i + 1, cols] for i in range(9)],
            low,
            high,
        )
        for ref, result in zip(outs, results):
            ref[:, cols] = result.astype(ref.dtype)


VMEM = pl.BlockSpec(memory_space=pltpu.VMEM)


def per_device(stream_one, stream_two, stream_value, long_filter, short_taps, skip_gain, out_grad):
    blocks = lax.axis_size("seq")
    me = lax.axis_index("seq")
    tokens, channels = stream_one.shape
    half = tokens // 2
    owned = channels // blocks
    exact = owned == HALF
    bf16, f32 = jnp.bfloat16, jnp.float32
    rows_in = 2 * tokens + half
    rows_out = tokens + half + EXTRA
    taps_flat = short_taps.reshape(9, channels)

    def by_owner(array):
        split = array.reshape(array.shape[0], blocks, owned).transpose(1, 0, 2)
        return jnp.pad(split, ((0, 0), (0, 0), (0, HALF - owned)))

    def side_by_side(first, second):
        return jnp.concatenate([by_owner(first), by_owner(second)], 2)

    if exact:
        packed = pl.pallas_call(
            pack_kernel,
            out_shape=jax.ShapeDtypeStruct((blocks, rows_in, LANES), bf16),
            in_specs=[VMEM] * 5,
            out_specs=VMEM,
            name="pack",
        )(stream_one, stream_two, stream_value, long_filter, out_grad)
    else:
        packed = jnp.concatenate(
            [
                side_by_side(stream_two, stream_one),
                side_by_side(stream_value, out_grad),
                side_by_side(long_filter[:half], long_filter[half:]),
            ],
            1,
        )

    unit = jnp.zeros((3, channels), f32).at[0].set(1.0)
    lower = jnp.concatenate([taps_flat[3:9], skip_gain[None], skip_gain[None]], 0)
    upper = jnp.concatenate([taps_flat[:3], unit, skip_gain[None], skip_gain[None]], 0)
    weights = lax.dynamic_index_in_dim(side_by_side(lower, upper), me, 0, keepdims=False)

    owned_chunk = lax.all_to_all(packed, "seq", 0, 0, tiled=True)

    forward, inverse = dft_tables(blocks, tokens)
    size = 2 * tokens
    table_spec = pl.BlockSpec((1, tokens, 2 * size), lambda k: (k, 0, 0))

    def owner(*refs):
        owner_kernel(blocks, *refs)

    returned = pl.pallas_call(
        owner,
        out_shape=jax.ShapeDtypeStruct((blocks, rows_out, LANES), bf16),
        grid=(blocks + 1,),
        in_specs=[
            VMEM,
            VMEM,
            table_spec,
            table_spec,
        ],
        out_specs=VMEM,
        scratch_shapes=[
            pltpu.VMEM((blocks, tokens, LANES), f32),
            pltpu.VMEM((blocks + 1, size, 2 * LANES), f32),
            pltpu.VMEM((blocks, tokens, LANES), f32),
            pltpu.VMEM((blocks, half, LANES), f32),
            pltpu.VMEM((8, 8, LANES), f32),
        ],
        compiler_params=pltpu.CompilerParams(vmem_limit_bytes=58 * 1024 * 1024),
        name="owner",
    )(owned_chunk, weights, jnp.asarray(forward), jnp.asarray(inverse))

    back = lax.all_to_all(returned, "seq", 0, 0, tiled=True)

    if exact:
        shape = (tokens, channels)
        results = pl.pallas_call(
            finish_kernel,
            out_shape=[jax.ShapeDtypeStruct(shape, bf16)] * 4
            + [jax.ShapeDtypeStruct(shape, f32), jax.ShapeDtypeStruct((10, channels), f32)],
            in_specs=[VMEM] * 6,
            out_specs=[VMEM] * 6,
            name="finish",
        )(stream_one, stream_two, stream_value, out_grad, taps_flat, back)
    else:
        wide = back.astype(f32)

        def joined(part):
            return part[:, :, :owned].transpose(1, 0, 2).reshape(rows_out, channels)

        results = finish(
            [s.astype(f32) for s in (stream_one, stream_two, stream_value)],
            out_grad.astype(f32),
            [taps_flat[i : i + 1] for i in range(9)],
            joined(wide[:, :, :HALF]),
            joined(wide[:, :, HALF:]),
        )
        results = [r.astype(bf16) for r in results[:4]] + results[4:]
    mixed_out, grad_one, grad_two, grad_value, grad_filter, sums = results
    grad_taps = sums[:9].reshape(3, 3, channels)
    return (mixed_out, grad_one, grad_two, grad_value, grad_filter, grad_taps, sums[9])


def solution(mesh):
    rows = P("seq", "ch")
    return jax.shard_map(
        per_device,
        mesh=mesh,
        in_specs=(rows, rows, rows, rows, P(None, None, "ch"), P("ch"), rows),
        out_specs=(rows, rows, rows, rows, rows, P(None, None, "ch"), P("ch")),
        check_vma=False,
    )
```

```python
import math

import jax
import jax.numpy as jnp
import ml_dtypes
import numpy as np
from jax import lax
from jax.experimental import pallas as pl
from jax.experimental.pallas import tpu as pltpu
from jax.sharding import PartitionSpec as P

HALF = 64
LANES = 2 * HALF
EXTRA = 16


def root(top, bottom):
    angle = math.pi * top / bottom
    return math.cos(angle), math.sin(angle)


def padded_dft(xs):
    m = len(xs)
    if m == 1:
        return [(xs[0], None), (xs[0], None)]
    even, odd = padded_dft(xs[0::2]), padded_dft(xs[1::2])
    out = [None] * (m + 1)
    for k in range(m // 2 + 1):
        (ar, ai), (br, bi) = even[k], odd[k]
        if k == 0:
            out[0], out[m] = (ar + br, None), (ar - br, None)
        elif 2 * k == m:
            out[k] = (ar, -br)
        else:
            c, s = root(k, m)
            if bi is None:
                tr, ti = br * c, br * -s
            else:
                tr, ti = br * c + bi * s, bi * c - br * s
            out[k] = (ar + tr, ti if ai is None else ai + ti)
            out[m - k] = (ar - tr, ti if ai is None else ti - ai)
    return out


def folded_sum(ys):
    m = len(ys) - 1
    if m == 1:
        return [ys[0][0] + ys[1][0]]
    even, odd = [], []
    for k in range(m // 2 + 1):
        (ar, ai), (br, bi) = ys[k], ys[m - k]
        if k == 0:
            even.append((ar + br, None))
            odd.append((ar - br, None))
        elif 2 * k == m:
            even.append((ar, None))
            odd.append((-ai, None))
        else:
            c, s = root(k, m)
            dr, di = ar - br, ai + bi
            even.append((ar + br, ai - bi))
            odd.append((dr * c - di * s, dr * s + di * c))
    out = [None] * m
    out[0::2], out[1::2] = folded_sum(even), folded_sum(odd)
    return out


def split_pair(values):
    high = values.astype(ml_dtypes.bfloat16)
    low = (values - high.astype(np.float64)).astype(ml_dtypes.bfloat16)
    return np.concatenate([high, low], axis=-1)


def dft_tables(blocks, tokens):
    period = 2 * blocks * tokens
    k1 = np.arange(blocks + 1)[:, None, None]
    k2 = np.arange(tokens)[None, :, None]
    place = np.arange(tokens)[None, None, :]
    angle = (2.0 * math.pi / period) * ((place * (k1 + 2 * blocks * k2)) % period)
    c, s = np.cos(angle), np.sin(angle)
    weight = np.where((k1 == 0) | (k1 == blocks), 1.0, 2.0) / period
    forward = np.concatenate([c, s], 2)
    inverse = np.concatenate([c.transpose(0, 2, 1), -s.transpose(0, 2, 1)], 2) * weight
    return split_pair(forward), split_pair(inverse)


def full_tables(tables):
    parts = []
    for pair in np.split(tables, 2, axis=-1):
        cos, sin = np.split(pair, 2, axis=-1)
        parts.append(np.concatenate([pair, np.concatenate([-sin, cos], -1)], -2))
    return np.concatenate(parts, -1)


def halves_swapped(values):
    return pltpu.roll(values, HALF, 1)


def interleave(first, second):
    low = lax.broadcasted_iota(jnp.int32, first.shape, 1) < HALF
    return (
        jnp.where(low, first, halves_swapped(second)),
        jnp.where(low, halves_swapped(first), second),
    )


def pack_kernel(one, two, value, filt, grad, out):
    tokens = one.shape[0]
    half = tokens // 2
    for pair in range(one.shape[1] // LANES):
        cols = slice(pair * LANES, (pair + 1) * LANES)
        tile = [ref[:, cols].astype(jnp.float32) for ref in (two, one, value, grad, filt)]
        parts = (
            (0, tokens, tile[0], tile[1]),
            (tokens, tokens, tile[2], tile[3]),
            (2 * tokens, half, tile[4][:half], tile[4][half:]),
        )
        for start, rows, first, second in parts:
            for side, piece in enumerate(interleave(first, second)):
                out[2 * pair + side, start : start + rows] = piece.astype(out.dtype)


def window_conv(window, weights, tokens):
    total = weights[0] * window[8 : 8 + tokens]
    for j in (1, 2):
        total = total + weights[j] * window[8 - j : 8 - j + tokens]
    return total


def owner_kernel(blocks, chunk, weights, ftab, itab, out, ug_ref, spec_ref, lg_ref, gf_ref, acc_ref):
    step = pl.program_id(0)
    tokens = ftab.shape[1]
    half = tokens // 2
    f32 = jnp.float32

    def block_rows(a, start):
        return chunk[a, start : start + tokens].astype(f32)

    def window(a, start):
        before = chunk[jnp.maximum(a - 1, 0), start + tokens - 16 : start + tokens].astype(f32)[8:]
        return jnp.concatenate([jnp.where(a > 0, before, 0.0), block_rows(a, start)], axis=0)

    w1 = [weights[j : j + 1] for j in range(3)]
    w2 = [weights[3 + j : 4 + j] for j in range(3)]

    @pl.when(step == 0)
    def _():
        @pl.loop(0, blocks)
        def _(a):
            c1 = window_conv(window(a, 0), w1, tokens)
            c2 = window_conv(window(a, tokens), w2, tokens)
            ug_ref[a] = (c1 * c2).astype(jnp.bfloat16).astype(f32)

        @pl.loop(0, tokens // 8)
        def _(r):
            at = pl.multiple_of(r * 8, 8)
            spectrum = padded_dft([ug_ref[a, pl.ds(at, 8)] for a in range(blocks)])
            for k, (real, imag) in enumerate(spectrum):
                spec_ref[k, pl.ds(at, 8), :LANES] = real
                spec_ref[k, pl.ds(tokens + at, 8), :LANES] = (
                    jnp.zeros_like(real) if imag is None else imag
                )

        @pl.loop(0, half // 16)
        def _(r):
            at = pl.multiple_of(r * 16, 16)
            tiles = [chunk[a, pl.ds(2 * tokens + at, 16)].astype(f32) for a in range(blocks)]
            low = lax.broadcasted_iota(jnp.int32, (8, LANES), 1) < HALF
            for sub in range(2):
                spectrum = padded_dft([t[8 * sub : 8 * sub + 8] for t in tiles])
                for k, pair in enumerate(spectrum):
                    for place, part in enumerate(pair):
                        part = jnp.zeros_like(pair[0]) if part is None else part
                        turned = halves_swapped(part)
                        row = place * tokens + at + 8 * sub
                        spec_ref[k, pl.ds(row, 8), LANES:] = jnp.where(low, part, turned)
                        spec_ref[k, pl.ds(row + half, 8), LANES:] = jnp.where(low, turned, part)

    def transform(table, values):
        high = values.astype(jnp.bfloat16)
        rest = (values - high.astype(f32)).astype(jnp.bfloat16)
        cos_high, sin_high, cos_low, sin_low = [
            table[0, :, i * tokens : (i + 1) * tokens] for i in range(4)
        ]
        left = jnp.concatenate(
            [
                jnp.concatenate([cos_high, sin_high, cos_low, sin_low], 1),
                jnp.concatenate([-sin_high, cos_high, -sin_low, cos_low], 1),
            ],
            0,
        )
        return jnp.dot(
            left, jnp.concatenate([high, high], 0), preferred_element_type=f32
        ) + jnp.dot(left[:, : 2 * tokens], rest, preferred_element_type=f32)

    spectral = transform(ftab, spec_ref[step])
    sign = jnp.where(lax.broadcasted_iota(jnp.int32, (tokens, LANES), 1) < HALF, 1.0, -1.0)
    ur, ui = spectral[:tokens, :LANES], spectral[tokens:, :LANES]
    hr, hi = spectral[:tokens, LANES:], spectral[tokens:, LANES:] * sign
    vr, vi = halves_swapped(ur), halves_swapped(ui)
    products = jnp.concatenate(
        [
            jnp.concatenate([ur * hr - ui * hi, ur * vr + ui * vi], 1),
            jnp.concatenate([ui * hr + ur * hi, vi * ur - vr * ui], 1),
        ],
        0,
    )
    spec_ref[step] = transform(itab, products)

    @pl.when(step == blocks)
    def _():
        skip = weights[6:7]
        low = lax.broadcasted_iota(jnp.int32, (8, LANES), 1) < HALF

        @pl.loop(0, tokens // 8)
        def _(r):
            at = pl.multiple_of(r * 8, 8)
            ys = [
                (spec_ref[k, pl.ds(at, 8), :LANES], spec_ref[k, pl.ds(tokens + at, 8), :LANES])
                for k in range(blocks + 1)
            ]
            for a, total in enumerate(folded_sum(ys)):
                lg_ref[a, pl.ds(at, 8)] = total + skip * ug_ref[a, pl.ds(at, 8)]

        @pl.loop(0, half // 8)
        def _(r):
            at = pl.multiple_of(r * 8, 8)
            ys = []
            for k in range(blocks + 1):
                pair = []
                for place in range(2):
                    row = place * tokens + at
                    top = spec_ref[k, pl.ds(row, 8), LANES:]
                    bottom = spec_ref[k, pl.ds(row + half, 8), LANES:]
                    pair.append(jnp.where(low, top, halves_swapped(bottom)))
                ys.append(tuple(pair))
            for a, total in enumerate(folded_sum(ys)):
                gf_ref[a, pl.ds(at, 8)] = total

        acc_ref[...] = jnp.zeros_like(acc_ref)

        def folded(values):
            total = values[:8]
            for r in range(1, tokens // 8):
                total = total + values[8 * r : 8 * r + 8]
            return total

        @pl.loop(0, blocks)
        def _(i):
            a = blocks - 1 - i
            one, two = window(a, 0), window(a, tokens)
            c1, c2 = window_conv(one, w1, tokens), window_conv(two, w2, tokens)
            lg = lg_ref[a]
            turned = halves_swapped(lg)
            x1, x2 = c2 * turned, c1 * turned
            ug = ug_ref[a]
            for j in range(3):
                acc_ref[j] += folded(x1 * one[8 - j : 8 - j + tokens])
                acc_ref[3 + j] += folded(x2 * two[8 - j : 8 - j + tokens])
            acc_ref[6] += folded(ug * halves_swapped(ug))
            after = acc_ref[7]
            out[a, :tokens] = lg.astype(out.dtype)
            out[a, tokens : tokens + half] = gf_ref[a].astype(out.dtype)
            out[a, tokens + half :] = jnp.concatenate(
                [after[:4], one[6:8], two[6:8], jnp.zeros((8, LANES), f32)], 0
            ).astype(out.dtype)
            acc_ref[7] = jnp.concatenate([x1[:2], x2[:2], jnp.zeros((4, LANES), f32)], 0)

        lower = lax.broadcasted_iota(jnp.int32, (1, LANES), 1) < HALF
        sums = [jnp.sum(acc_ref[j], axis=0, keepdims=True) for j in range(7)]
        sums[3] = jnp.where(lower, sums[3], sums[6])
        tail = jnp.concatenate(sums[:6] + [jnp.zeros((2, LANES), f32)], 0)

        @pl.loop(0, blocks)
        def _(a):
            rows = out[a, tokens + half :].astype(f32)
            out[a, tokens + half :] = jnp.concatenate([rows[:8], tail], 0).astype(out.dtype)


def resident_kernel(
    blocks, chunk_hbm, weights, ftab_hbm, itab_hbm, out_hbm,
    chunk, ftab, itab, high_ref, low_ref, zh_ref, zl_ref, spec_ref,
    c1_ref, c2_ref, ug_ref, lg_ref, gf_ref, acc_ref, out, in_sems, tab_sems, out_sem,
):
    tokens = ftab.shape[1] // 2
    size = 2 * tokens
    half = tokens // 2
    f32, bf16 = jnp.float32, jnp.bfloat16
    pieces = in_sems.shape[0]
    per = blocks // pieces

    def piece_copy(p):
        part = pl.ds(p * per, per)
        return pltpu.make_async_copy(chunk_hbm.at[part], chunk.at[part], in_sems.at[p])

    table_copies = [
        pltpu.make_async_copy(ftab_hbm, ftab, tab_sems.at[0]),
        pltpu.make_async_copy(itab_hbm, itab, tab_sems.at[1]),
    ]
    for p in range(pieces):
        piece_copy(p).start()
    for copy in table_copies:
        copy.start()

    def window(a, start):
        before = chunk[jnp.maximum(a - 1, 0), start + tokens - 16 : start + tokens].astype(f32)[8:]
        body = chunk[a, start : start + tokens].astype(f32)
        return jnp.concatenate([jnp.where(a > 0, before, 0.0), body], axis=0)

    w1 = [weights[j : j + 1] for j in range(3)]
    w2 = [weights[3 + j : 4 + j] for j in range(3)]

    for p in range(pieces):
        piece_copy(p).wait()

        @pl.loop(p * per, (p + 1) * per)
        def _(a):
            c1 = window_conv(window(a, 0), w1, tokens)
            c2 = window_conv(window(a, tokens), w2, tokens)
            c1_ref[a], c2_ref[a] = c1, c2
            ug_ref[a] = (c1 * c2).astype(bf16)

    def put(k, row, cols, values):
        high = values.astype(bf16)
        high_ref[k, pl.ds(row, 16), cols] = high
        low_ref[k, pl.ds(row, 16), cols] = (values - high.astype(f32)).astype(bf16)

    left, right = slice(0, LANES), slice(LANES, 2 * LANES)

    @pl.loop(0, tokens // 16)
    def _(r):
        at = pl.multiple_of(r * 16, 16)
        spectrum = padded_dft([ug_ref[a, pl.ds(at, 16)].astype(f32) for a in range(blocks)])
        for k, (real, imag) in enumerate(spectrum):
            put(k, at, left, real)
            put(k, tokens + at, left, jnp.zeros_like(real) if imag is None else imag)

    @pl.loop(0, half // 16)
    def _(r):
        at = pl.multiple_of(r * 16, 16)
        low = lax.broadcasted_iota(jnp.int32, (16, LANES), 1) < HALF
        spectrum = padded_dft(
            [chunk[a, pl.ds(2 * tokens + at, 16)].astype(f32) for a in range(blocks)]
        )
        for k, pair in enumerate(spectrum):
            for place, part in enumerate(pair):
                part = jnp.zeros_like(pair[0]) if part is None else part
                turned = halves_swapped(part)
                put(k, place * tokens + at, right, jnp.where(low, part, turned))
                put(k, place * tokens + half + at, right, jnp.where(low, turned, part))

    for copy in table_copies:
        copy.wait()

    def apply(table, k, high, rest):
        first = table[k, :, :size]
        total = jnp.dot(first, high, preferred_element_type=f32)
        total = total + jnp.dot(table[k, :, size:], high, preferred_element_type=f32)
        return total + jnp.dot(first, rest, preferred_element_type=f32)

    sign = jnp.where(lax.broadcasted_iota(jnp.int32, (1, LANES), 1) < HALF, 1.0, -1.0)

    def into_products(k, slot):
        spectral = apply(ftab, k, high_ref[k], low_ref[k])
        ur, ui = spectral[:tokens, :LANES], spectral[tokens:, :LANES]
        hr, hi = spectral[:tokens, LANES:], spectral[tokens:, LANES:] * sign
        vr, vi = halves_swapped(ur), halves_swapped(ui)
        for place, cols, values in (
            (0, left, ur * hr - ui * hi),
            (1, left, ui * hr + ur * hi),
            (0, right, ur * vr + ui * vi),
            (1, right, vi * ur - vr * ui),
        ):
            rows = slice(place * tokens, (place + 1) * tokens)
            high = values.astype(bf16)
            zh_ref[slot, rows, cols] = high
            zl_ref[slot, rows, cols] = (values - high.astype(f32)).astype(bf16)

    def out_of_products(k, slot):
        spec_ref[k] = apply(itab, k, zh_ref[slot], zl_ref[slot])

    into_products(0, 0)

    @pl.loop(1, blocks + 1)
    def _(k):
        slot = lax.rem(k, 2)
        out_of_products(k - 1, 1 - slot)
        into_products(k, slot)

    out_of_products(blocks, blocks % 2)

    skip = weights[6:7]
    low8 = lax.broadcasted_iota(jnp.int32, (8, LANES), 1) < HALF

    @pl.loop(0, tokens // 16)
    def _(r):
        at = pl.multiple_of(r * 16, 16)
        ug = [ug_ref[a, pl.ds(at, 16)].astype(f32) for a in range(blocks)]
        for sub in range(2):
            row = pl.multiple_of(at + 8 * sub, 8)
            ys = [
                (spec_ref[k, pl.ds(row, 8), left], spec_ref[k, pl.ds(tokens + row, 8), left])
                for k in range(blocks + 1)
            ]
            for a, total in enumerate(folded_sum(ys)):
                lg_ref[a, pl.ds(row, 8)] = total + skip * ug[a][8 * sub : 8 * sub + 8]

    @pl.loop(0, half // 8)
    def _(r):
        at = pl.multiple_of(r * 8, 8)
        ys = []
        for k in range(blocks + 1):
            pair = []
            for place in range(2):
                row = place * tokens + at
                top = spec_ref[k, pl.ds(row, 8), right]
                bottom = spec_ref[k, pl.ds(row + half, 8), right]
                pair.append(jnp.where(low8, top, halves_swapped(bottom)))
            ys.append(tuple(pair))
        for a, total in enumerate(folded_sum(ys)):
            gf_ref[a, pl.ds(at, 8)] = total

    acc_ref[...] = jnp.zeros_like(acc_ref)

    def folded(values):
        total = values[:8]
        for r in range(1, tokens // 8):
            total = total + values[8 * r : 8 * r + 8]
        return total

    @pl.loop(0, blocks)
    def _(i):
        a = blocks - 1 - i
        one, two = window(a, 0), window(a, tokens)
        lg = lg_ref[a]
        turned = halves_swapped(lg)
        x1, x2 = c2_ref[a] * turned, c1_ref[a] * turned
        ug = ug_ref[a].astype(f32)
        for j in range(3):
            acc_ref[j] += folded(x1 * one[8 - j : 8 - j + tokens])
            acc_ref[3 + j] += folded(x2 * two[8 - j : 8 - j + tokens])
        acc_ref[6] += folded(ug * halves_swapped(ug))
        after = acc_ref[7]
        out[a, :tokens] = lg.astype(out.dtype)
        out[a, tokens : tokens + half] = gf_ref[a].astype(out.dtype)
        out[a, tokens + half :] = jnp.concatenate(
            [after[:4], one[6:8], two[6:8], jnp.zeros((8, LANES), f32)], 0
        ).astype(out.dtype)
        acc_ref[7] = jnp.concatenate([x1[:2], x2[:2], jnp.zeros((4, LANES), f32)], 0)

    lower = lax.broadcasted_iota(jnp.int32, (1, LANES), 1) < HALF
    sums = [jnp.sum(acc_ref[j], axis=0, keepdims=True) for j in range(7)]
    sums[3] = jnp.where(lower, sums[3], sums[6])
    tail = jnp.concatenate(sums[:6] + [jnp.zeros((2, LANES), f32)], 0)

    @pl.loop(0, blocks)
    def _(a):
        rows = out[a, tokens + half :].astype(f32)
        out[a, tokens + half :] = jnp.concatenate([rows[:8], tail], 0).astype(out.dtype)

    copy = pltpu.make_async_copy(out, out_hbm, out_sem)
    copy.start()
    copy.wait()


def finish(streams, cotangent, weights, low, high):
    tokens = streams[0].shape[0]
    half = tokens // 2
    at = tokens + half
    long_out, grad_mixed = low[:tokens], high[:tokens]
    grad_filter = jnp.concatenate([low[tokens:at], high[tokens:at]], 0)
    before = (high[at + 4 : at + 6], low[at + 4 : at + 6], low[at + 6 : at + 8])
    after = (high[at : at + 2], low[at : at + 2], low[at + 2 : at + 4])
    gates = []
    for s in range(3):
        window = jnp.concatenate([jnp.zeros_like(low[:6]), before[s], streams[s]], 0)
        gates.append(window_conv(window, [weights[3 * s + j] for j in range(3)], tokens))
    mixed_out = gates[0] * long_out
    conv_grads = (cotangent * long_out, grad_mixed * gates[2], grad_mixed * gates[1])
    grads = []
    for s in range(3):
        trailing = jnp.concatenate([conv_grads[s], after[s], jnp.zeros_like(low[:6])], 0)
        total = weights[3 * s] * trailing[:tokens]
        for j in (1, 2):
            total = total + weights[3 * s + j] * trailing[j : j + tokens]
        grads.append(total)
    taps = [high[at + 8 : at + 11], low[at + 8 : at + 11], low[at + 11 : at + 14]]
    return [mixed_out] + grads + [grad_filter] + taps + [high[at + 11 : at + 12]]


def finish_kernel(one, two, value, grad, weights, back, *outs):
    for pair in range(one.shape[1] // LANES):
        cols = slice(pair * LANES, (pair + 1) * LANES)
        low, high = interleave(
            back[2 * pair].astype(jnp.float32), back[2 * pair + 1].astype(jnp.float32)
        )
        streams = [ref[:, cols].astype(jnp.float32) for ref in (one, two, value)]
        results = finish(
            streams,
            grad[:, cols].astype(jnp.float32),
            [weights[i // 3, i % 3 : i % 3 + 1, cols] for i in range(9)],
            low,
            high,
        )
        for ref, result in zip(outs[:5], results[:5]):
            ref[:, cols] = result.astype(ref.dtype)
        for s in range(3):
            outs[5][s, :, cols] = results[5 + s]
        outs[6][:, cols] = results[8]


VMEM = pl.BlockSpec(memory_space=pltpu.VMEM)
ANY = pl.BlockSpec(memory_space=pl.ANY)


def per_device(stream_one, stream_two, stream_value, long_filter, short_taps, skip_gain, out_grad):
    blocks = lax.axis_size("seq")
    me = lax.axis_index("seq")
    tokens, channels = stream_one.shape
    half = tokens // 2
    owned = channels // blocks
    exact = owned == HALF
    bf16, f32 = jnp.bfloat16, jnp.float32
    rows_in = 2 * tokens + half
    rows_out = tokens + half + EXTRA
    taps_flat = short_taps.reshape(9, channels)

    def by_owner(array):
        split = array.reshape(array.shape[0], blocks, owned).transpose(1, 0, 2)
        return jnp.pad(split, ((0, 0), (0, 0), (0, HALF - owned)))

    def side_by_side(first, second):
        return jnp.concatenate([by_owner(first), by_owner(second)], 2)

    steps = max(1, channels // 256)
    by_columns = pl.BlockSpec((tokens, channels // steps), lambda i: (0, i))

    if exact:
        packed = pl.pallas_call(
            pack_kernel,
            out_shape=jax.ShapeDtypeStruct((blocks, rows_in, LANES), bf16),
            grid=(steps,),
            in_specs=[by_columns] * 5,
            out_specs=pl.BlockSpec((blocks // steps, rows_in, LANES), lambda i: (i, 0, 0)),
            name="pack",
        )(stream_one, stream_two, stream_value, long_filter, out_grad)
    else:
        packed = jnp.concatenate(
            [
                side_by_side(stream_two, stream_one),
                side_by_side(stream_value, out_grad),
                side_by_side(long_filter[:half], long_filter[half:]),
            ],
            1,
        )

    unit = jnp.zeros((3, channels), f32).at[0].set(1.0)
    lower = jnp.concatenate([taps_flat[3:9], skip_gain[None], skip_gain[None]], 0)
    upper = jnp.concatenate([taps_flat[:3], unit, skip_gain[None], skip_gain[None]], 0)
    weights = lax.dynamic_index_in_dim(side_by_side(lower, upper), me, 0, keepdims=False)

    owned_chunk = lax.all_to_all(packed, "seq", 0, 0, tiled=True)

    forward, inverse = dft_tables(blocks, tokens)
    size = 2 * tokens
    table_spec = pl.BlockSpec((1, tokens, 2 * size), lambda k: (k, 0, 0))

    if exact and blocks <= 16:
        pieces = 4 if blocks % 4 == 0 else 1

        def resident(*refs):
            resident_kernel(blocks, *refs)

        returned = pl.pallas_call(
            resident,
            out_shape=jax.ShapeDtypeStruct((blocks, rows_out, LANES), bf16),
            in_specs=[ANY, VMEM, ANY, ANY],
            out_specs=ANY,
            scratch_shapes=[
                pltpu.VMEM((blocks, rows_in, LANES), bf16),
                pltpu.VMEM((blocks + 1, size, 2 * size), bf16),
                pltpu.VMEM((blocks + 1, size, 2 * size), bf16),
                pltpu.VMEM((blocks + 1, size, 2 * LANES), bf16),
                pltpu.VMEM((blocks + 1, size, 2 * LANES), bf16),
                pltpu.VMEM((2, size, 2 * LANES), bf16),
                pltpu.VMEM((2, size, 2 * LANES), bf16),
                pltpu.VMEM((blocks + 1, size, 2 * LANES), f32),
                pltpu.VMEM((blocks, tokens, LANES), f32),
                pltpu.VMEM((blocks, tokens, LANES), f32),
                pltpu.VMEM((blocks, tokens, LANES), bf16),
                pltpu.VMEM((blocks, tokens, LANES), f32),
                pltpu.VMEM((blocks, half, LANES), f32),
                pltpu.VMEM((8, 8, LANES), f32),
                pltpu.VMEM((blocks, rows_out, LANES), bf16),
                pltpu.SemaphoreType.DMA((pieces,)),
                pltpu.SemaphoreType.DMA((2,)),
                pltpu.SemaphoreType.DMA,
            ],
            compiler_params=pltpu.CompilerParams(vmem_limit_bytes=48 * 1024 * 1024),
            name="owner",
        )(
            owned_chunk,
            weights,
            jnp.asarray(full_tables(forward)),
            jnp.asarray(full_tables(inverse)),
        )
    else:

        def owner(*refs):
            owner_kernel(blocks, *refs)

        returned = pl.pallas_call(
            owner,
            out_shape=jax.ShapeDtypeStruct((blocks, rows_out, LANES), bf16),
            grid=(blocks + 1,),
            in_specs=[VMEM, VMEM, table_spec, table_spec],
            out_specs=VMEM,
            scratch_shapes=[
                pltpu.VMEM((blocks, tokens, LANES), f32),
                pltpu.VMEM((blocks + 1, size, 2 * LANES), f32),
                pltpu.VMEM((blocks, tokens, LANES), f32),
                pltpu.VMEM((blocks, half, LANES), f32),
                pltpu.VMEM((8, 8, LANES), f32),
            ],
            compiler_params=pltpu.CompilerParams(vmem_limit_bytes=58 * 1024 * 1024),
            name="owner",
        )(owned_chunk, weights, jnp.asarray(forward), jnp.asarray(inverse))

    back = lax.all_to_all(returned, "seq", 0, 0, tiled=True)

    if exact:
        shape = (tokens, channels)
        taps_spec = pl.BlockSpec((3, 3, channels // steps), lambda i: (0, 0, i))
        results = pl.pallas_call(
            finish_kernel,
            out_shape=[jax.ShapeDtypeStruct(shape, bf16)] * 4
            + [
                jax.ShapeDtypeStruct(shape, f32),
                jax.ShapeDtypeStruct(short_taps.shape, f32),
                jax.ShapeDtypeStruct((1, channels), f32),
            ],
            grid=(steps,),
            in_specs=[by_columns] * 4
            + [taps_spec, pl.BlockSpec((blocks // steps, rows_out, LANES), lambda i: (i, 0, 0))],
            out_specs=[by_columns] * 5 + [taps_spec, pl.BlockSpec((1, channels // steps), lambda i: (0, i))],
            name="finish",
        )(stream_one, stream_two, stream_value, out_grad, short_taps, back)
    else:
        wide = back.astype(f32)

        def joined(part):
            return part[:, :, :owned].transpose(1, 0, 2).reshape(rows_out, channels)

        results = finish(
            [s.astype(f32) for s in (stream_one, stream_two, stream_value)],
            out_grad.astype(f32),
            [taps_flat[i : i + 1] for i in range(9)],
            joined(wide[:, :, :HALF]),
            joined(wide[:, :, HALF:]),
        )
        results = [r.astype(bf16) for r in results[:4]] + [
            results[4],
            jnp.stack(results[5:8]),
            results[8],
        ]
    return tuple(results[:6]) + (results[6].reshape(channels),)


def solution(mesh):
    rows = P("seq", "ch")
    return jax.shard_map(
        per_device,
        mesh=mesh,
        in_specs=(rows, rows, rows, rows, P(None, None, "ch"), P("ch"), rows),
        out_specs=(rows, rows, rows, rows, rows, P(None, None, "ch"), P("ch")),
        check_vma=False,
    )
```

```python
import math

import jax
import jax.numpy as jnp
import ml_dtypes
import numpy as np
from jax import lax
from jax.experimental import pallas as pl
from jax.experimental.pallas import tpu as pltpu
from jax.sharding import PartitionSpec as P

HALF = 64
LANES = 2 * HALF
EXTRA = 16


def root(top, bottom):
    angle = math.pi * top / bottom
    return math.cos(angle), math.sin(angle)


def padded_dft(xs):
    m = len(xs)
    if m == 1:
        return [(xs[0], None), (xs[0], None)]
    even, odd = padded_dft(xs[0::2]), padded_dft(xs[1::2])
    out = [None] * (m + 1)
    for k in range(m // 2 + 1):
        (ar, ai), (br, bi) = even[k], odd[k]
        if k == 0:
            out[0], out[m] = (ar + br, None), (ar - br, None)
        elif 2 * k == m:
            out[k] = (ar, -br)
        else:
            c, s = root(k, m)
            if bi is None:
                tr, ti = br * c, br * -s
            else:
                tr, ti = br * c + bi * s, bi * c - br * s
            out[k] = (ar + tr, ti if ai is None else ai + ti)
            out[m - k] = (ar - tr, ti if ai is None else ti - ai)
    return out


def folded_sum(ys):
    m = len(ys) - 1
    if m == 1:
        return [ys[0][0] + ys[1][0]]
    even, odd = [], []
    for k in range(m // 2 + 1):
        (ar, ai), (br, bi) = ys[k], ys[m - k]
        if k == 0:
            even.append((ar + br, None))
            odd.append((ar - br, None))
        elif 2 * k == m:
            even.append((ar, None))
            odd.append((-ai, None))
        else:
            c, s = root(k, m)
            dr, di = ar - br, ai + bi
            even.append((ar + br, ai - bi))
            odd.append((dr * c - di * s, dr * s + di * c))
    out = [None] * m
    out[0::2], out[1::2] = folded_sum(even), folded_sum(odd)
    return out


def split_pair(values):
    high = values.astype(ml_dtypes.bfloat16)
    low = (values - high.astype(np.float64)).astype(ml_dtypes.bfloat16)
    return np.concatenate([high, low], axis=-1)


def dft_tables(blocks, tokens):
    period = 2 * blocks * tokens
    k1 = np.arange(blocks + 1)[:, None, None]
    k2 = np.arange(tokens)[None, :, None]
    place = np.arange(tokens)[None, None, :]
    angle = (2.0 * math.pi / period) * ((place * (k1 + 2 * blocks * k2)) % period)
    c, s = np.cos(angle), np.sin(angle)
    weight = np.where((k1 == 0) | (k1 == blocks), 1.0, 2.0) / period
    forward = np.concatenate([c, s], 2)
    inverse = np.concatenate([c.transpose(0, 2, 1), -s.transpose(0, 2, 1)], 2) * weight
    return split_pair(forward), split_pair(inverse)


def halves_swapped(values):
    return pltpu.roll(values, HALF, 1)


def interleave(first, second):
    low = lax.broadcasted_iota(jnp.int32, first.shape, 1) < HALF
    return (
        jnp.where(low, first, halves_swapped(second)),
        jnp.where(low, halves_swapped(first), second),
    )


def pack_kernel(one, two, value, filt, grad, out):
    tokens = one.shape[0]
    half = tokens // 2
    for pair in range(one.shape[1] // LANES):
        cols = slice(pair * LANES, (pair + 1) * LANES)
        tile = [ref[:, cols].astype(jnp.float32) for ref in (two, one, value, grad, filt)]
        parts = (
            (0, tokens, tile[0], tile[1]),
            (tokens, tokens, tile[2], tile[3]),
            (2 * tokens, half, tile[4][:half], tile[4][half:]),
        )
        for start, rows, first, second in parts:
            for side, piece in enumerate(interleave(first, second)):
                out[2 * pair + side, start : start + rows] = piece.astype(out.dtype)


def window_conv(window, weights, tokens):
    total = weights[0] * window[8 : 8 + tokens]
    for j in (1, 2):
        total = total + weights[j] * window[8 - j : 8 - j + tokens]
    return total


def owner_kernel(blocks, chunk, weights, ftab, itab, out, ug_ref, spec_ref, lg_ref, gf_ref, acc_ref):
    step = pl.program_id(0)
    tokens = ftab.shape[1]
    half = tokens // 2
    f32 = jnp.float32

    def block_rows(a, start):
        return chunk[a, start : start + tokens].astype(f32)

    def window(a, start):
        before = chunk[jnp.maximum(a - 1, 0), start + tokens - 16 : start + tokens].astype(f32)[8:]
        return jnp.concatenate([jnp.where(a > 0, before, 0.0), block_rows(a, start)], axis=0)

    w1 = [weights[j : j + 1] for j in range(3)]
    w2 = [weights[3 + j : 4 + j] for j in range(3)]

    @pl.when(step == 0)
    def _():
        @pl.loop(0, blocks)
        def _(a):
            c1 = window_conv(window(a, 0), w1, tokens)
            c2 = window_conv(window(a, tokens), w2, tokens)
            ug_ref[a] = (c1 * c2).astype(jnp.bfloat16).astype(f32)

        @pl.loop(0, tokens // 8)
        def _(r):
            at = pl.multiple_of(r * 8, 8)
            spectrum = padded_dft([ug_ref[a, pl.ds(at, 8)] for a in range(blocks)])
            for k, (real, imag) in enumerate(spectrum):
                spec_ref[k, pl.ds(at, 8), :LANES] = real
                spec_ref[k, pl.ds(tokens + at, 8), :LANES] = (
                    jnp.zeros_like(real) if imag is None else imag
                )

        @pl.loop(0, half // 16)
        def _(r):
            at = pl.multiple_of(r * 16, 16)
            tiles = [chunk[a, pl.ds(2 * tokens + at, 16)].astype(f32) for a in range(blocks)]
            low = lax.broadcasted_iota(jnp.int32, (8, LANES), 1) < HALF
            for sub in range(2):
                spectrum = padded_dft([t[8 * sub : 8 * sub + 8] for t in tiles])
                for k, pair in enumerate(spectrum):
                    for place, part in enumerate(pair):
                        part = jnp.zeros_like(pair[0]) if part is None else part
                        turned = halves_swapped(part)
                        row = place * tokens + at + 8 * sub
                        spec_ref[k, pl.ds(row, 8), LANES:] = jnp.where(low, part, turned)
                        spec_ref[k, pl.ds(row + half, 8), LANES:] = jnp.where(low, turned, part)

    def transform(table, values):
        high = values.astype(jnp.bfloat16)
        rest = (values - high.astype(f32)).astype(jnp.bfloat16)
        cos_high, sin_high, cos_low, sin_low = [
            table[0, :, i * tokens : (i + 1) * tokens] for i in range(4)
        ]
        left = jnp.concatenate(
            [
                jnp.concatenate([cos_high, sin_high, cos_low, sin_low], 1),
                jnp.concatenate([-sin_high, cos_high, -sin_low, cos_low], 1),
            ],
            0,
        )
        return jnp.dot(
            left, jnp.concatenate([high, high], 0), preferred_element_type=f32
        ) + jnp.dot(left[:, : 2 * tokens], rest, preferred_element_type=f32)

    spectral = transform(ftab, spec_ref[step])
    sign = jnp.where(lax.broadcasted_iota(jnp.int32, (tokens, LANES), 1) < HALF, 1.0, -1.0)
    ur, ui = spectral[:tokens, :LANES], spectral[tokens:, :LANES]
    hr, hi = spectral[:tokens, LANES:], spectral[tokens:, LANES:] * sign
    vr, vi = halves_swapped(ur), halves_swapped(ui)
    products = jnp.concatenate(
        [
            jnp.concatenate([ur * hr - ui * hi, ur * vr + ui * vi], 1),
            jnp.concatenate([ui * hr + ur * hi, vi * ur - vr * ui], 1),
        ],
        0,
    )
    spec_ref[step] = transform(itab, products)

    @pl.when(step == blocks)
    def _():
        skip = weights[6:7]
        low = lax.broadcasted_iota(jnp.int32, (8, LANES), 1) < HALF

        @pl.loop(0, tokens // 8)
        def _(r):
            at = pl.multiple_of(r * 8, 8)
            ys = [
                (spec_ref[k, pl.ds(at, 8), :LANES], spec_ref[k, pl.ds(tokens + at, 8), :LANES])
                for k in range(blocks + 1)
            ]
            for a, total in enumerate(folded_sum(ys)):
                lg_ref[a, pl.ds(at, 8)] = total + skip * ug_ref[a, pl.ds(at, 8)]

        @pl.loop(0, half // 8)
        def _(r):
            at = pl.multiple_of(r * 8, 8)
            ys = []
            for k in range(blocks + 1):
                pair = []
                for place in range(2):
                    row = place * tokens + at
                    top = spec_ref[k, pl.ds(row, 8), LANES:]
                    bottom = spec_ref[k, pl.ds(row + half, 8), LANES:]
                    pair.append(jnp.where(low, top, halves_swapped(bottom)))
                ys.append(tuple(pair))
            for a, total in enumerate(folded_sum(ys)):
                gf_ref[a, pl.ds(at, 8)] = total

        acc_ref[...] = jnp.zeros_like(acc_ref)

        def folded(values):
            total = values[:8]
            for r in range(1, tokens // 8):
                total = total + values[8 * r : 8 * r + 8]
            return total

        @pl.loop(0, blocks)
        def _(i):
            a = blocks - 1 - i
            one, two = window(a, 0), window(a, tokens)
            c1, c2 = window_conv(one, w1, tokens), window_conv(two, w2, tokens)
            lg = lg_ref[a]
            turned = halves_swapped(lg)
            x1, x2 = c2 * turned, c1 * turned
            ug = ug_ref[a]
            for j in range(3):
                acc_ref[j] += folded(x1 * one[8 - j : 8 - j + tokens])
                acc_ref[3 + j] += folded(x2 * two[8 - j : 8 - j + tokens])
            acc_ref[6] += folded(ug * halves_swapped(ug))
            after = acc_ref[7]
            out[a, :tokens] = lg.astype(out.dtype)
            out[a, tokens : tokens + half] = gf_ref[a].astype(out.dtype)
            out[a, tokens + half :] = jnp.concatenate(
                [after[:4], one[6:8], two[6:8], jnp.zeros((8, LANES), f32)], 0
            ).astype(out.dtype)
            acc_ref[7] = jnp.concatenate([x1[:2], x2[:2], jnp.zeros((4, LANES), f32)], 0)

        lower = lax.broadcasted_iota(jnp.int32, (1, LANES), 1) < HALF
        sums = [jnp.sum(acc_ref[j], axis=0, keepdims=True) for j in range(7)]
        sums[3] = jnp.where(lower, sums[3], sums[6])
        tail = jnp.concatenate(sums[:6] + [jnp.zeros((2, LANES), f32)], 0)

        @pl.loop(0, blocks)
        def _(a):
            rows = out[a, tokens + half :].astype(f32)
            out[a, tokens + half :] = jnp.concatenate([rows[:8], tail], 0).astype(out.dtype)


def resident_kernel(
    blocks, chunk, weights, tables_hbm, out,
    tables, high_ref, low_ref, zh_ref, zl_ref, spec_ref,
    c1_ref, c2_ref, ug_ref, lg_ref, gf_ref, acc_ref, sems,
):
    tokens = tables.shape[2]
    size = 2 * tokens
    half = tokens // 2
    f32, bf16 = jnp.float32, jnp.bfloat16
    copies = [
        pltpu.make_async_copy(tables_hbm.at[i], tables.at[i], sems.at[i]) for i in range(2)
    ]
    for copy in copies:
        copy.start()

    def window(a, start):
        before = chunk[jnp.maximum(a - 1, 0), start + tokens - 16 : start + tokens].astype(f32)[8:]
        body = chunk[a, start : start + tokens].astype(f32)
        return jnp.concatenate([jnp.where(a > 0, before, 0.0), body], axis=0)

    w1 = [weights[j : j + 1] for j in range(3)]
    w2 = [weights[3 + j : 4 + j] for j in range(3)]

    @pl.loop(0, blocks)
    def _(a):
        c1 = window_conv(window(a, 0), w1, tokens)
        c2 = window_conv(window(a, tokens), w2, tokens)
        c1_ref[a], c2_ref[a] = c1, c2
        ug_ref[a] = (c1 * c2).astype(bf16)

    def put(k, row, cols, values):
        high = values.astype(bf16)
        high_ref[k, pl.ds(row, 16), cols] = high
        low_ref[k, pl.ds(row, 16), cols] = (values - high.astype(f32)).astype(bf16)

    left, right = slice(0, LANES), slice(LANES, 2 * LANES)

    @pl.loop(0, tokens // 16)
    def _(r):
        at = pl.multiple_of(r * 16, 16)
        spectrum = padded_dft([ug_ref[a, pl.ds(at, 16)].astype(f32) for a in range(blocks)])
        for k, (real, imag) in enumerate(spectrum):
            put(k, at, left, real)
            put(k, tokens + at, left, jnp.zeros_like(real) if imag is None else imag)

    @pl.loop(0, half // 16)
    def _(r):
        at = pl.multiple_of(r * 16, 16)
        low = lax.broadcasted_iota(jnp.int32, (16, LANES), 1) < HALF
        spectrum = padded_dft(
            [chunk[a, pl.ds(2 * tokens + at, 16)].astype(f32) for a in range(blocks)]
        )
        for k, pair in enumerate(spectrum):
            for place, part in enumerate(pair):
                part = jnp.zeros_like(pair[0]) if part is None else part
                turned = halves_swapped(part)
                put(k, place * tokens + at, right, jnp.where(low, part, turned))
                put(k, place * tokens + half + at, right, jnp.where(low, turned, part))

    def whole_map(table, k, start):
        pair = tables[table, k, :, start : start + size]
        return jnp.concatenate(
            [pair, jnp.concatenate([-pair[:, tokens:], pair[:, :tokens]], 1)], 0
        )

    def apply(table, k, high, rest):
        first = whole_map(table, k, 0)
        total = jnp.dot(first, high, preferred_element_type=f32)
        total = total + jnp.dot(whole_map(table, k, size), high, preferred_element_type=f32)
        return total + jnp.dot(first, rest, preferred_element_type=f32)

    sign = jnp.where(lax.broadcasted_iota(jnp.int32, (1, LANES), 1) < HALF, 1.0, -1.0)

    def into_products(k, slot):
        spectral = apply(0, k, high_ref[k], low_ref[k])
        ur, ui = spectral[:tokens, :LANES], spectral[tokens:, :LANES]
        hr, hi = spectral[:tokens, LANES:], spectral[tokens:, LANES:] * sign
        vr, vi = halves_swapped(ur), halves_swapped(ui)
        for place, cols, values in (
            (0, left, ur * hr - ui * hi),
            (1, left, ui * hr + ur * hi),
            (0, right, ur * vr + ui * vi),
            (1, right, vi * ur - vr * ui),
        ):
            rows = slice(place * tokens, (place + 1) * tokens)
            high = values.astype(bf16)
            zh_ref[slot, rows, cols] = high
            zl_ref[slot, rows, cols] = (values - high.astype(f32)).astype(bf16)

    def out_of_products(k, slot):
        spec_ref[k] = apply(1, k, zh_ref[slot], zl_ref[slot])

    for copy in copies:
        copy.wait()

    group = zh_ref.shape[0] // 2
    whole = (blocks + 1) // group
    rest = range(whole * group, blocks + 1)
    for j in range(group):
        into_products(j, j)

    @pl.loop(1, whole)
    def _(i):
        now = lax.rem(i, 2) * group
        for j in range(group):
            out_of_products((i - 1) * group + j, group - now + j)
        for j in range(group):
            into_products(i * group + j, now + j)

    last = (whole - 1) % 2 * group
    for j, k in enumerate(rest):
        into_products(k, group - last + j)
    for j in range(group):
        out_of_products((whole - 1) * group + j, last + j)
    for j, k in enumerate(rest):
        out_of_products(k, group - last + j)

    skip = weights[6:7]
    low8 = lax.broadcasted_iota(jnp.int32, (8, LANES), 1) < HALF

    @pl.loop(0, tokens // 16)
    def _(r):
        at = pl.multiple_of(r * 16, 16)
        ug = [ug_ref[a, pl.ds(at, 16)].astype(f32) for a in range(blocks)]
        for sub in range(2):
            row = pl.multiple_of(at + 8 * sub, 8)
            ys = [
                (spec_ref[k, pl.ds(row, 8), left], spec_ref[k, pl.ds(tokens + row, 8), left])
                for k in range(blocks + 1)
            ]
            for a, total in enumerate(folded_sum(ys)):
                lg_ref[a, pl.ds(row, 8)] = total + skip * ug[a][8 * sub : 8 * sub + 8]

    @pl.loop(0, half // 8)
    def _(r):
        at = pl.multiple_of(r * 8, 8)
        ys = []
        for k in range(blocks + 1):
            pair = []
            for place in range(2):
                row = place * tokens + at
                top = spec_ref[k, pl.ds(row, 8), right]
                bottom = spec_ref[k, pl.ds(row + half, 8), right]
                pair.append(jnp.where(low8, top, halves_swapped(bottom)))
            ys.append(tuple(pair))
        for a, total in enumerate(folded_sum(ys)):
            gf_ref[a, pl.ds(at, 8)] = total

    acc_ref[...] = jnp.zeros_like(acc_ref)

    def folded(values):
        total = values[:8]
        for r in range(1, tokens // 8):
            total = total + values[8 * r : 8 * r + 8]
        return total

    @pl.loop(0, blocks)
    def _(i):
        a = blocks - 1 - i
        one, two = window(a, 0), window(a, tokens)
        lg = lg_ref[a]
        turned = halves_swapped(lg)
        x1, x2 = c2_ref[a] * turned, c1_ref[a] * turned
        for j in range(3):
            acc_ref[j] += folded(x1 * one[8 - j : 8 - j + tokens])
            acc_ref[3 + j] += folded(x2 * two[8 - j : 8 - j + tokens])
        after = acc_ref[7]
        out[a, :tokens] = lg.astype(out.dtype)
        out[a, tokens : tokens + half] = gf_ref[a].astype(out.dtype)
        out[a, tokens + half :] = jnp.concatenate(
            [after[:4], one[6:8], two[6:8], jnp.zeros((8, LANES), f32)], 0
        ).astype(out.dtype)
        acc_ref[7] = jnp.concatenate([x1[:2], x2[:2], jnp.zeros((4, LANES), f32)], 0)

    lower = lax.broadcasted_iota(jnp.int32, (1, LANES), 1) < HALF
    sums = [jnp.sum(acc_ref[j], axis=0, keepdims=True) for j in range(6)]
    sums[3] = jnp.where(lower, sums[3], halves_swapped(gf_ref[0, :8])[:1])
    tail = jnp.concatenate(sums + [jnp.zeros((2, LANES), f32)], 0)

    @pl.loop(0, blocks)
    def _(a):
        rows = out[a, tokens + half :].astype(f32)
        out[a, tokens + half :] = jnp.concatenate([rows[:8], tail], 0).astype(out.dtype)


def local_gates(streams, weights):
    tokens = streams[0].shape[0]
    gates = []
    for s, stream in enumerate(streams):
        window = jnp.concatenate([jnp.zeros_like(stream[:8]), stream], 0)
        gates.append(window_conv(window, weights[3 * s : 3 * s + 3], tokens))
    return gates


def finish(gates, cotangent, weights, low, high):
    tokens = cotangent.shape[0]
    half = tokens // 2
    at = tokens + half
    long_out, grad_mixed = low[:tokens], high[:tokens]
    grad_filter = jnp.concatenate([low[tokens:at], high[tokens:at]], 0)
    before = (high[at + 4 : at + 6], low[at + 4 : at + 6], low[at + 6 : at + 8])
    after = (high[at : at + 2], low[at : at + 2], low[at + 2 : at + 4])
    whole = []
    for s in range(3):
        older, newer = before[s][:1], before[s][1:]
        w1, w2 = weights[3 * s + 1], weights[3 * s + 2]
        missing = jnp.concatenate(
            [w1 * newer + w2 * older, w2 * newer, jnp.zeros((6, older.shape[1]), jnp.float32)], 0
        )
        whole.append(jnp.concatenate([gates[s][:8] + missing, gates[s][8:]], 0))
    mixed_out = whole[0] * long_out
    conv_grads = (cotangent * long_out, grad_mixed * whole[2], grad_mixed * whole[1])
    grads = []
    for s in range(3):
        trailing = jnp.concatenate([conv_grads[s], after[s], jnp.zeros_like(low[:6])], 0)
        total = weights[3 * s] * trailing[:tokens]
        for j in (1, 2):
            total = total + weights[3 * s + j] * trailing[j : j + tokens]
        grads.append(total)
    taps = [high[at + 8 : at + 11], low[at + 8 : at + 11], low[at + 11 : at + 14]]
    return [mixed_out] + grads + [grad_filter] + taps + [high[at + 11 : at + 12]]


def gates_kernel(one, two, value, weights, after, gates):
    del after
    for pair in range(one.shape[1] // LANES):
        cols = slice(pair * LANES, (pair + 1) * LANES)
        results = local_gates(
            [ref[:, cols].astype(jnp.float32) for ref in (one, two, value)],
            [weights[i // 3, i % 3 : i % 3 + 1, cols] for i in range(9)],
        )
        for s, result in enumerate(results):
            gates[s, :, cols] = result


def finish_kernel(gates, grad, weights, back, *refs):
    targets, grad_taps, grad_skip = refs[:5], refs[5], refs[6]
    buffers, sems = refs[7:12], refs[12]
    pieces = sems.shape[1]
    width = grad.shape[1] // pieces

    def copy(i, piece):
        cols = pl.ds(piece * width, width)
        return pltpu.make_async_copy(buffers[i].at[:, cols], targets[i].at[:, cols], sems.at[i, piece])

    for piece in range(pieces):
        for start in range(piece * width, (piece + 1) * width, LANES):
            cols = slice(start, start + LANES)
            owner = start // HALF
            low, high = interleave(
                back[owner].astype(jnp.float32), back[owner + 1].astype(jnp.float32)
            )
            results = finish(
                [gates[s, :, cols] for s in range(3)],
                grad[:, cols].astype(jnp.float32),
                [weights[i // 3, i % 3 : i % 3 + 1, cols] for i in range(9)],
                low,
                high,
            )
            for ref, result in zip(buffers, results[:5]):
                ref[:, cols] = result.astype(ref.dtype)
            for s in range(3):
                grad_taps[s, :, cols] = results[5 + s]
            grad_skip[:, cols] = results[8]
        for i in range(5):
            copy(i, piece).start()
    for piece in range(pieces):
        for i in range(5):
            copy(i, piece).wait()


VMEM = pl.BlockSpec(memory_space=pltpu.VMEM)
ANY = pl.BlockSpec(memory_space=pl.ANY)
HBM = pl.BlockSpec(memory_space=pltpu.HBM)


def per_device(stream_one, stream_two, stream_value, long_filter, short_taps, skip_gain, out_grad):
    blocks = lax.axis_size("seq")
    me = lax.axis_index("seq")
    tokens, channels = stream_one.shape
    half = tokens // 2
    owned = channels // blocks
    exact = owned == HALF
    bf16, f32 = jnp.bfloat16, jnp.float32
    rows_in = 2 * tokens + half
    rows_out = tokens + half + EXTRA
    taps_flat = short_taps.reshape(9, channels)

    def by_owner(array):
        split = array.reshape(array.shape[0], blocks, owned).transpose(1, 0, 2)
        return jnp.pad(split, ((0, 0), (0, 0), (0, HALF - owned)))

    def side_by_side(first, second):
        return jnp.concatenate([by_owner(first), by_owner(second)], 2)

    small = pltpu.CompilerParams(vmem_limit_bytes=16 * 1024 * 1024)
    steps = 2 if channels % 512 == 0 else 1
    by_columns = pl.BlockSpec((tokens, channels // steps), lambda i: (0, i))

    if exact:
        packed = pl.pallas_call(
            pack_kernel,
            out_shape=jax.ShapeDtypeStruct((blocks, rows_in, LANES), bf16),
            grid=(steps,),
            in_specs=[by_columns] * 5,
            out_specs=pl.BlockSpec((blocks // steps, rows_in, LANES), lambda i: (i, 0, 0)),
            name="pack",
        )(stream_one, stream_two, stream_value, long_filter, out_grad)
    else:
        packed = jnp.concatenate(
            [
                side_by_side(stream_two, stream_one),
                side_by_side(stream_value, out_grad),
                side_by_side(long_filter[:half], long_filter[half:]),
            ],
            1,
        )

    unit = jnp.zeros((3, channels), f32).at[0].set(1.0)
    lower = jnp.concatenate([taps_flat[3:9], skip_gain[None], skip_gain[None]], 0)
    upper = jnp.concatenate([taps_flat[:3], unit, skip_gain[None], skip_gain[None]], 0)
    weights = lax.dynamic_index_in_dim(side_by_side(lower, upper), me, 0, keepdims=False)

    owned_chunk = lax.all_to_all(packed, "seq", 0, 0, tiled=True)

    forward, inverse = dft_tables(blocks, tokens)
    size = 2 * tokens
    table_spec = pl.BlockSpec((1, tokens, 2 * size), lambda k: (k, 0, 0))

    if exact and blocks <= 16:
        group = 4

        def resident(*refs):
            resident_kernel(blocks, *refs)

        returned = pl.pallas_call(
            resident,
            out_shape=jax.ShapeDtypeStruct((blocks, rows_out, LANES), bf16),
            in_specs=[VMEM, VMEM, HBM],
            out_specs=VMEM,
            scratch_shapes=[
                pltpu.VMEM((2, blocks + 1, tokens, 2 * size), bf16),
                pltpu.VMEM((blocks + 1, size, 2 * LANES), bf16),
                pltpu.VMEM((blocks + 1, size, 2 * LANES), bf16),
                pltpu.VMEM((2 * group, size, 2 * LANES), bf16),
                pltpu.VMEM((2 * group, size, 2 * LANES), bf16),
                pltpu.VMEM((blocks + 1, size, 2 * LANES), f32),
                pltpu.VMEM((blocks, tokens, LANES), f32),
                pltpu.VMEM((blocks, tokens, LANES), f32),
                pltpu.VMEM((blocks, tokens, LANES), bf16),
                pltpu.VMEM((blocks, tokens, LANES), f32),
                pltpu.VMEM((blocks, half, LANES), f32),
                pltpu.VMEM((8, 8, LANES), f32),
                pltpu.SemaphoreType.DMA((2,)),
            ],
            compiler_params=pltpu.CompilerParams(vmem_limit_bytes=48 * 1024 * 1024),
            name="owner",
        )(owned_chunk, weights, jnp.asarray(np.stack([forward, inverse])))
    else:

        def owner(*refs):
            owner_kernel(blocks, *refs)

        returned = pl.pallas_call(
            owner,
            out_shape=jax.ShapeDtypeStruct((blocks, rows_out, LANES), bf16),
            grid=(blocks + 1,),
            in_specs=[VMEM, VMEM, table_spec, table_spec],
            out_specs=VMEM,
            scratch_shapes=[
                pltpu.VMEM((blocks, tokens, LANES), f32),
                pltpu.VMEM((blocks + 1, size, 2 * LANES), f32),
                pltpu.VMEM((blocks, tokens, LANES), f32),
                pltpu.VMEM((blocks, half, LANES), f32),
                pltpu.VMEM((8, 8, LANES), f32),
            ],
            compiler_params=pltpu.CompilerParams(vmem_limit_bytes=58 * 1024 * 1024),
            name="owner",
        )(owned_chunk, weights, jnp.asarray(forward), jnp.asarray(inverse))

    back = lax.all_to_all(returned, "seq", 0, 0, tiled=True)

    if exact:
        shape = (tokens, channels)
        taps_spec = pl.BlockSpec((3, 3, channels // steps), lambda i: (0, 0, i))
        gates_spec = pl.BlockSpec((3, tokens, channels // steps), lambda i: (0, 0, i))
        gates = pl.pallas_call(
            gates_kernel,
            out_shape=jax.ShapeDtypeStruct((3,) + shape, f32),
            grid=(steps,),
            in_specs=[by_columns] * 3 + [taps_spec, ANY],
            out_specs=gates_spec,
            compiler_params=small,
            name="gates",
        )(stream_one, stream_two, stream_value, short_taps, returned)
        results = pl.pallas_call(
            finish_kernel,
            out_shape=[jax.ShapeDtypeStruct(shape, bf16)] * 4
            + [
                jax.ShapeDtypeStruct(shape, f32),
                jax.ShapeDtypeStruct(short_taps.shape, f32),
                jax.ShapeDtypeStruct((1, channels), f32),
            ],
            in_specs=[VMEM] * 4,
            out_specs=[ANY] * 5 + [VMEM] * 2,
            scratch_shapes=[pltpu.VMEM(shape, bf16)] * 4
            + [pltpu.VMEM(shape, f32), pltpu.SemaphoreType.DMA((5, 4))],
            compiler_params=small,
            name="finish",
        )(gates, out_grad, short_taps, back)
    else:
        wide = back.astype(f32)

        def joined(part):
            return part[:, :, :owned].transpose(1, 0, 2).reshape(rows_out, channels)

        rows = [taps_flat[i : i + 1] for i in range(9)]
        streams = [s.astype(f32) for s in (stream_one, stream_two, stream_value)]
        results = finish(
            local_gates(streams, rows),
            out_grad.astype(f32),
            rows,
            joined(wide[:, :, :HALF]),
            joined(wide[:, :, HALF:]),
        )
        results = [r.astype(bf16) for r in results[:4]] + [
            results[4],
            jnp.stack(results[5:8]),
            results[8],
        ]
    return tuple(results[:6]) + (results[6].reshape(channels),)


def solution(mesh):
    rows = P("seq", "ch")
    return jax.shard_map(
        per_device,
        mesh=mesh,
        in_specs=(rows, rows, rows, rows, P(None, None, "ch"), P("ch"), rows),
        out_specs=(rows, rows, rows, rows, rows, P(None, None, "ch"), P("ch")),
        check_vma=False,
    )
```

```python
import math

import jax
import jax.numpy as jnp
import ml_dtypes
import numpy as np
from jax import lax
from jax.experimental import pallas as pl
from jax.experimental.pallas import tpu as pltpu
from jax.sharding import PartitionSpec as P

HALF = 64
LANES = 2 * HALF
EXTRA = 16


def root(top, bottom):
    angle = math.pi * top / bottom
    return math.cos(angle), math.sin(angle)


def padded_dft(xs):
    m = len(xs)
    if m == 1:
        return [(xs[0], None), (xs[0], None)]
    even, odd = padded_dft(xs[0::2]), padded_dft(xs[1::2])
    out = [None] * (m + 1)
    for k in range(m // 2 + 1):
        (ar, ai), (br, bi) = even[k], odd[k]
        if k == 0:
            out[0], out[m] = (ar + br, None), (ar - br, None)
        elif 2 * k == m:
            out[k] = (ar, -br)
        else:
            c, s = root(k, m)
            if bi is None:
                tr, ti = br * c, br * -s
            else:
                tr, ti = br * c + bi * s, bi * c - br * s
            out[k] = (ar + tr, ti if ai is None else ai + ti)
            out[m - k] = (ar - tr, ti if ai is None else ti - ai)
    return out


def folded_sum(ys):
    m = len(ys) - 1
    if m == 1:
        return [ys[0][0] + ys[1][0]]
    even, odd = [], []
    for k in range(m // 2 + 1):
        (ar, ai), (br, bi) = ys[k], ys[m - k]
        if k == 0:
            even.append((ar + br, None))
            odd.append((ar - br, None))
        elif 2 * k == m:
            even.append((ar, None))
            odd.append((-ai, None))
        else:
            c, s = root(k, m)
            dr, di = ar - br, ai + bi
            even.append((ar + br, ai - bi))
            odd.append((dr * c - di * s, dr * s + di * c))
    out = [None] * m
    out[0::2], out[1::2] = folded_sum(even), folded_sum(odd)
    return out


def split_pair(values):
    high = values.astype(ml_dtypes.bfloat16)
    low = (values - high.astype(np.float64)).astype(ml_dtypes.bfloat16)
    return np.concatenate([high, low], axis=-1)


def dft_tables(blocks, tokens):
    period = 2 * blocks * tokens
    k1 = np.arange(blocks + 1)[:, None, None]
    k2 = np.arange(tokens)[None, :, None]
    place = np.arange(tokens)[None, None, :]
    angle = (2.0 * math.pi / period) * ((place * (k1 + 2 * blocks * k2)) % period)
    c, s = np.cos(angle), np.sin(angle)
    weight = np.where((k1 == 0) | (k1 == blocks), 1.0, 2.0) / period
    forward = np.concatenate([c, s], 2)
    inverse = np.concatenate([c.transpose(0, 2, 1), -s.transpose(0, 2, 1)], 2) * weight
    return split_pair(forward), split_pair(inverse)


def halves_swapped(values):
    return pltpu.roll(values, HALF, 1)


def interleave(first, second):
    low = lax.broadcasted_iota(jnp.int32, first.shape, 1) < HALF
    return (
        jnp.where(low, first, halves_swapped(second)),
        jnp.where(low, halves_swapped(first), second),
    )


def pack_kernel(one, two, value, filt, grad, out):
    tokens = one.shape[0]
    half = tokens // 2
    for pair in range(one.shape[1] // LANES):
        cols = slice(pair * LANES, (pair + 1) * LANES)
        tile = [ref[:, cols] for ref in (two, one, value, grad, filt)]
        parts = (
            (0, tokens, tile[0], tile[1]),
            (tokens, tokens, tile[2], tile[3]),
            (2 * tokens, half, tile[4][:half], tile[4][half:]),
        )
        for start, rows, first, second in parts:
            for side, piece in enumerate(interleave(first, second)):
                out[2 * pair + side, start : start + rows] = piece.astype(out.dtype)


def window_conv(window, weights, tokens):
    total = weights[0] * window[8 : 8 + tokens]
    for j in (1, 2):
        total = total + weights[j] * window[8 - j : 8 - j + tokens]
    return total


def owner_kernel(blocks, chunk, weights, ftab, itab, out, ug_ref, spec_ref, lg_ref, gf_ref, acc_ref):
    step = pl.program_id(0)
    tokens = ftab.shape[1]
    half = tokens // 2
    f32 = jnp.float32

    def block_rows(a, start):
        return chunk[a, start : start + tokens].astype(f32)

    def window(a, start):
        before = chunk[jnp.maximum(a - 1, 0), start + tokens - 16 : start + tokens].astype(f32)[8:]
        return jnp.concatenate([jnp.where(a > 0, before, 0.0), block_rows(a, start)], axis=0)

    w1 = [weights[j : j + 1] for j in range(3)]
    w2 = [weights[3 + j : 4 + j] for j in range(3)]

    @pl.when(step == 0)
    def _():
        @pl.loop(0, blocks)
        def _(a):
            c1 = window_conv(window(a, 0), w1, tokens)
            c2 = window_conv(window(a, tokens), w2, tokens)
            ug_ref[a] = (c1 * c2).astype(jnp.bfloat16).astype(f32)

        @pl.loop(0, tokens // 8)
        def _(r):
            at = pl.multiple_of(r * 8, 8)
            spectrum = padded_dft([ug_ref[a, pl.ds(at, 8)] for a in range(blocks)])
            for k, (real, imag) in enumerate(spectrum):
                spec_ref[k, pl.ds(at, 8), :LANES] = real
                spec_ref[k, pl.ds(tokens + at, 8), :LANES] = (
                    jnp.zeros_like(real) if imag is None else imag
                )

        @pl.loop(0, half // 16)
        def _(r):
            at = pl.multiple_of(r * 16, 16)
            tiles = [chunk[a, pl.ds(2 * tokens + at, 16)].astype(f32) for a in range(blocks)]
            low = lax.broadcasted_iota(jnp.int32, (8, LANES), 1) < HALF
            for sub in range(2):
                spectrum = padded_dft([t[8 * sub : 8 * sub + 8] for t in tiles])
                for k, pair in enumerate(spectrum):
                    for place, part in enumerate(pair):
                        part = jnp.zeros_like(pair[0]) if part is None else part
                        turned = halves_swapped(part)
                        row = place * tokens + at + 8 * sub
                        spec_ref[k, pl.ds(row, 8), LANES:] = jnp.where(low, part, turned)
                        spec_ref[k, pl.ds(row + half, 8), LANES:] = jnp.where(low, turned, part)

    def transform(table, values):
        high = values.astype(jnp.bfloat16)
        rest = (values - high.astype(f32)).astype(jnp.bfloat16)
        cos_high, sin_high, cos_low, sin_low = [
            table[0, :, i * tokens : (i + 1) * tokens] for i in range(4)
        ]
        left = jnp.concatenate(
            [
                jnp.concatenate([cos_high, sin_high, cos_low, sin_low], 1),
                jnp.concatenate([-sin_high, cos_high, -sin_low, cos_low], 1),
            ],
            0,
        )
        return jnp.dot(
            left, jnp.concatenate([high, high], 0), preferred_element_type=f32
        ) + jnp.dot(left[:, : 2 * tokens], rest, preferred_element_type=f32)

    spectral = transform(ftab, spec_ref[step])
    sign = jnp.where(lax.broadcasted_iota(jnp.int32, (tokens, LANES), 1) < HALF, 1.0, -1.0)
    ur, ui = spectral[:tokens, :LANES], spectral[tokens:, :LANES]
    hr, hi = spectral[:tokens, LANES:], spectral[tokens:, LANES:] * sign
    vr, vi = halves_swapped(ur), halves_swapped(ui)
    products = jnp.concatenate(
        [
            jnp.concatenate([ur * hr - ui * hi, ur * vr + ui * vi], 1),
            jnp.concatenate([ui * hr + ur * hi, vi * ur - vr * ui], 1),
        ],
        0,
    )
    spec_ref[step] = transform(itab, products)

    @pl.when(step == blocks)
    def _():
        skip = weights[6:7]
        low = lax.broadcasted_iota(jnp.int32, (8, LANES), 1) < HALF

        @pl.loop(0, tokens // 8)
        def _(r):
            at = pl.multiple_of(r * 8, 8)
            ys = [
                (spec_ref[k, pl.ds(at, 8), :LANES], spec_ref[k, pl.ds(tokens + at, 8), :LANES])
                for k in range(blocks + 1)
            ]
            for a, total in enumerate(folded_sum(ys)):
                lg_ref[a, pl.ds(at, 8)] = total + skip * ug_ref[a, pl.ds(at, 8)]

        @pl.loop(0, half // 8)
        def _(r):
            at = pl.multiple_of(r * 8, 8)
            ys = []
            for k in range(blocks + 1):
                pair = []
                for place in range(2):
                    row = place * tokens + at
                    top = spec_ref[k, pl.ds(row, 8), LANES:]
                    bottom = spec_ref[k, pl.ds(row + half, 8), LANES:]
                    pair.append(jnp.where(low, top, halves_swapped(bottom)))
                ys.append(tuple(pair))
            for a, total in enumerate(folded_sum(ys)):
                gf_ref[a, pl.ds(at, 8)] = total

        acc_ref[...] = jnp.zeros_like(acc_ref)

        def folded(values):
            total = values[:8]
            for r in range(1, tokens // 8):
                total = total + values[8 * r : 8 * r + 8]
            return total

        @pl.loop(0, blocks)
        def _(i):
            a = blocks - 1 - i
            one, two = window(a, 0), window(a, tokens)
            c1, c2 = window_conv(one, w1, tokens), window_conv(two, w2, tokens)
            lg = lg_ref[a]
            turned = halves_swapped(lg)
            x1, x2 = c2 * turned, c1 * turned
            ug = ug_ref[a]
            for j in range(3):
                acc_ref[j] += folded(x1 * one[8 - j : 8 - j + tokens])
                acc_ref[3 + j] += folded(x2 * two[8 - j : 8 - j + tokens])
            acc_ref[6] += folded(ug * halves_swapped(ug))
            after = acc_ref[7]
            out[a, :tokens] = lg.astype(out.dtype)
            out[a, tokens : tokens + half] = gf_ref[a].astype(out.dtype)
            out[a, tokens + half :] = jnp.concatenate(
                [after[:4], one[6:8], two[6:8], jnp.zeros((8, LANES), f32)], 0
            ).astype(out.dtype)
            acc_ref[7] = jnp.concatenate([x1[:2], x2[:2], jnp.zeros((4, LANES), f32)], 0)

        lower = lax.broadcasted_iota(jnp.int32, (1, LANES), 1) < HALF
        sums = [jnp.sum(acc_ref[j], axis=0, keepdims=True) for j in range(7)]
        sums[3] = jnp.where(lower, sums[3], sums[6])
        tail = jnp.concatenate(sums[:6] + [jnp.zeros((2, LANES), f32)], 0)

        @pl.loop(0, blocks)
        def _(a):
            rows = out[a, tokens + half :].astype(f32)
            out[a, tokens + half :] = jnp.concatenate([rows[:8], tail], 0).astype(out.dtype)


def resident_kernel(
    blocks, chunk, weights, tables_hbm, out,
    tables, high_ref, low_ref, zh_ref, zl_ref, spec_ref,
    c1_ref, c2_ref, ug_ref, lg_ref, gf_ref, acc_ref, sems,
):
    tokens = tables.shape[2]
    size = 2 * tokens
    half = tokens // 2
    f32, bf16 = jnp.float32, jnp.bfloat16
    copies = [
        pltpu.make_async_copy(tables_hbm.at[i], tables.at[i], sems.at[i]) for i in range(2)
    ]
    for copy in copies:
        copy.start()

    def window(a, start):
        before = chunk[jnp.maximum(a - 1, 0), start + tokens - 16 : start + tokens].astype(f32)[8:]
        body = chunk[a, start : start + tokens].astype(f32)
        return jnp.concatenate([jnp.where(a > 0, before, 0.0), body], axis=0)

    w1 = [weights[j : j + 1] for j in range(3)]
    w2 = [weights[3 + j : 4 + j] for j in range(3)]

    @pl.loop(0, blocks)
    def _(a):
        c1 = window_conv(window(a, 0), w1, tokens)
        c2 = window_conv(window(a, tokens), w2, tokens)
        c1_ref[a], c2_ref[a] = c1, c2
        ug_ref[a] = (c1 * c2).astype(bf16)

    def put(k, row, cols, values):
        high = values.astype(bf16)
        high_ref[k, pl.ds(row, 16), cols] = high
        low_ref[k, pl.ds(row, 16), cols] = (values - high.astype(f32)).astype(bf16)

    left, right = slice(0, LANES), slice(LANES, 2 * LANES)

    @pl.loop(0, tokens // 16, unroll=2)
    def _(r):
        at = pl.multiple_of(r * 16, 16)
        spectrum = padded_dft([ug_ref[a, pl.ds(at, 16)].astype(f32) for a in range(blocks)])
        for k, (real, imag) in enumerate(spectrum):
            put(k, at, left, real)
            put(k, tokens + at, left, jnp.zeros_like(real) if imag is None else imag)

    @pl.loop(0, half // 16, unroll=2)
    def _(r):
        at = pl.multiple_of(r * 16, 16)
        low = lax.broadcasted_iota(jnp.int32, (16, LANES), 1) < HALF
        spectrum = padded_dft(
            [chunk[a, pl.ds(2 * tokens + at, 16)].astype(f32) for a in range(blocks)]
        )
        for k, pair in enumerate(spectrum):
            for place, part in enumerate(pair):
                part = jnp.zeros_like(pair[0]) if part is None else part
                turned = halves_swapped(part)
                put(k, place * tokens + at, right, jnp.where(low, part, turned))
                put(k, place * tokens + half + at, right, jnp.where(low, turned, part))

    def whole_map(table, k, start):
        pair = tables[table, k, :, start : start + size]
        return jnp.concatenate(
            [pair, jnp.concatenate([-pair[:, tokens:], pair[:, :tokens]], 1)], 0
        )

    def apply(table, k, high, rest):
        first = whole_map(table, k, 0)
        total = jnp.dot(first, high, preferred_element_type=f32)
        total = total + jnp.dot(whole_map(table, k, size), high, preferred_element_type=f32)
        return total + jnp.dot(first, rest, preferred_element_type=f32)

    sign = jnp.where(lax.broadcasted_iota(jnp.int32, (1, LANES), 1) < HALF, 1.0, -1.0)

    def into_products(k, slot):
        spectral = apply(0, k, high_ref[k], low_ref[k])
        ur, ui = spectral[:tokens, :LANES], spectral[tokens:, :LANES]
        hr, hi = spectral[:tokens, LANES:], spectral[tokens:, LANES:] * sign
        vr, vi = halves_swapped(ur), halves_swapped(ui)
        for place, cols, values in (
            (0, left, ur * hr - ui * hi),
            (1, left, ui * hr + ur * hi),
            (0, right, ur * vr + ui * vi),
            (1, right, vi * ur - vr * ui),
        ):
            rows = slice(place * tokens, (place + 1) * tokens)
            high = values.astype(bf16)
            zh_ref[slot, rows, cols] = high
            zl_ref[slot, rows, cols] = (values - high.astype(f32)).astype(bf16)

    def out_of_products(k, slot):
        spec_ref[k] = apply(1, k, zh_ref[slot], zl_ref[slot])

    copies[0].wait()

    group = zh_ref.shape[0] // 2
    whole = (blocks + 1) // group
    rest = range(whole * group, blocks + 1)
    for j in range(group):
        into_products(j, j)
    copies[1].wait()

    @pl.loop(1, whole)
    def _(i):
        now = lax.rem(i, 2) * group
        for j in range(group):
            out_of_products((i - 1) * group + j, group - now + j)
        for j in range(group):
            into_products(i * group + j, now + j)

    last = (whole - 1) % 2 * group
    for j, k in enumerate(rest):
        into_products(k, group - last + j)
    for j in range(group):
        out_of_products((whole - 1) * group + j, last + j)
    for j, k in enumerate(rest):
        out_of_products(k, group - last + j)

    skip = weights[6:7]
    low8 = lax.broadcasted_iota(jnp.int32, (8, LANES), 1) < HALF

    @pl.loop(0, tokens // 16)
    def _(r):
        at = pl.multiple_of(r * 16, 16)
        ug = [ug_ref[a, pl.ds(at, 16)].astype(f32) for a in range(blocks)]
        for sub in range(2):
            row = pl.multiple_of(at + 8 * sub, 8)
            ys = [
                (spec_ref[k, pl.ds(row, 8), left], spec_ref[k, pl.ds(tokens + row, 8), left])
                for k in range(blocks + 1)
            ]
            for a, total in enumerate(folded_sum(ys)):
                lg_ref[a, pl.ds(row, 8)] = total + skip * ug[a][8 * sub : 8 * sub + 8]

    @pl.loop(0, half // 8, unroll=2)
    def _(r):
        at = pl.multiple_of(r * 8, 8)
        ys = []
        for k in range(blocks + 1):
            pair = []
            for place in range(2):
                row = place * tokens + at
                top = spec_ref[k, pl.ds(row, 8), right]
                bottom = spec_ref[k, pl.ds(row + half, 8), right]
                pair.append(jnp.where(low8, top, halves_swapped(bottom)))
            ys.append(tuple(pair))
        for a, total in enumerate(folded_sum(ys)):
            gf_ref[a, pl.ds(at, 8)] = total

    acc_ref[...] = jnp.zeros_like(acc_ref)

    def folded(values):
        total = values[:8]
        for r in range(1, tokens // 8):
            total = total + values[8 * r : 8 * r + 8]
        return total

    @pl.loop(0, blocks, unroll=4)
    def _(i):
        a = blocks - 1 - i
        one, two = window(a, 0), window(a, tokens)
        lg = lg_ref[a]
        turned = halves_swapped(lg)
        x1, x2 = c2_ref[a] * turned, c1_ref[a] * turned
        for j in range(3):
            acc_ref[j] += folded(x1 * one[8 - j : 8 - j + tokens])
            acc_ref[3 + j] += folded(x2 * two[8 - j : 8 - j + tokens])
        after = acc_ref[7]
        out[a, :tokens] = lg.astype(out.dtype)
        out[a, tokens : tokens + half] = gf_ref[a].astype(out.dtype)
        out[a, tokens + half :] = jnp.concatenate(
            [after[:4], one[6:8], two[6:8], jnp.zeros((8, LANES), f32)], 0
        ).astype(out.dtype)
        acc_ref[7] = jnp.concatenate([x1[:2], x2[:2], jnp.zeros((4, LANES), f32)], 0)

    lower = lax.broadcasted_iota(jnp.int32, (1, LANES), 1) < HALF
    sums = [jnp.sum(acc_ref[j], axis=0, keepdims=True) for j in range(6)]
    sums[3] = jnp.where(lower, sums[3], halves_swapped(gf_ref[0, :8])[:1])
    tail = jnp.concatenate(sums + [jnp.zeros((2, LANES), f32)], 0)

    @pl.loop(0, blocks, unroll=4)
    def _(a):
        rows = out[a, tokens + half :].astype(f32)
        out[a, tokens + half :] = jnp.concatenate([rows[:8], tail], 0).astype(out.dtype)


def local_gates(streams, weights):
    tokens = streams[0].shape[0]
    gates = []
    for s, stream in enumerate(streams):
        window = jnp.concatenate([jnp.zeros_like(stream[:8]), stream], 0)
        gates.append(window_conv(window, weights[3 * s : 3 * s + 3], tokens))
    return gates


def finish(gates, cotangent, weights, low, high):
    tokens = cotangent.shape[0]
    half = tokens // 2
    at = tokens + half
    long_out, grad_mixed = low[:tokens], high[:tokens]
    grad_filter = jnp.concatenate([low[tokens:at], high[tokens:at]], 0)
    before = (high[at + 4 : at + 6], low[at + 4 : at + 6], low[at + 6 : at + 8])
    after = (high[at : at + 2], low[at : at + 2], low[at + 2 : at + 4])
    whole = []
    for s in range(3):
        older, newer = before[s][:1], before[s][1:]
        w1, w2 = weights[3 * s + 1], weights[3 * s + 2]
        missing = jnp.concatenate(
            [w1 * newer + w2 * older, w2 * newer, jnp.zeros((6, older.shape[1]), jnp.float32)], 0
        )
        whole.append(jnp.concatenate([gates[s][:8] + missing, gates[s][8:]], 0))
    mixed_out = whole[0] * long_out
    conv_grads = (cotangent * long_out, grad_mixed * whole[2], grad_mixed * whole[1])
    grads = []
    for s in range(3):
        trailing = jnp.concatenate([conv_grads[s], after[s], jnp.zeros_like(low[:6])], 0)
        total = weights[3 * s] * trailing[:tokens]
        for j in (1, 2):
            total = total + weights[3 * s + j] * trailing[j : j + tokens]
        grads.append(total)
    taps = [high[at + 8 : at + 11], low[at + 8 : at + 11], low[at + 11 : at + 14]]
    return [mixed_out] + grads + [grad_filter] + taps + [high[at + 11 : at + 12]]


def gates_kernel(one, two, value, weights, after, gates):
    del after
    for pair in range(one.shape[1] // LANES):
        cols = slice(pair * LANES, (pair + 1) * LANES)
        results = local_gates(
            [ref[:, cols].astype(jnp.float32) for ref in (one, two, value)],
            [weights[i // 3, i % 3 : i % 3 + 1, cols] for i in range(9)],
        )
        for s, result in enumerate(results):
            gates[s, :, cols] = result


def finish_kernel(gates, grad, weights, back, *refs):
    targets, grad_taps, grad_skip = refs[:5], refs[5], refs[6]
    buffers, sems = refs[7:12], refs[12]
    pieces = sems.shape[1]
    width = grad.shape[1] // pieces

    def copy(i, piece):
        cols = pl.ds(piece * width, width)
        return pltpu.make_async_copy(buffers[i].at[:, cols], targets[i].at[:, cols], sems.at[i, piece])

    for piece in range(pieces):
        for start in range(piece * width, (piece + 1) * width, LANES):
            cols = slice(start, start + LANES)
            owner = start // HALF
            low, high = interleave(
                back[owner].astype(jnp.float32), back[owner + 1].astype(jnp.float32)
            )
            results = finish(
                [gates[s, :, cols] for s in range(3)],
                grad[:, cols].astype(jnp.float32),
                [weights[i // 3, i % 3 : i % 3 + 1, cols] for i in range(9)],
                low,
                high,
            )
            for ref, result in zip(buffers, results[:5]):
                ref[:, cols] = result.astype(ref.dtype)
            for s in range(3):
                grad_taps[s, :, cols] = results[5 + s]
            grad_skip[:, cols] = results[8]
        for i in range(5):
            copy(i, piece).start()
    for piece in range(pieces):
        for i in range(5):
            copy(i, piece).wait()


VMEM = pl.BlockSpec(memory_space=pltpu.VMEM)
ANY = pl.BlockSpec(memory_space=pl.ANY)
HBM = pl.BlockSpec(memory_space=pltpu.HBM)


def per_device(stream_one, stream_two, stream_value, long_filter, short_taps, skip_gain, out_grad):
    blocks = lax.axis_size("seq")
    me = lax.axis_index("seq")
    tokens, channels = stream_one.shape
    half = tokens // 2
    owned = channels // blocks
    exact = owned == HALF
    bf16, f32 = jnp.bfloat16, jnp.float32
    rows_in = 2 * tokens + half
    rows_out = tokens + half + EXTRA
    taps_flat = short_taps.reshape(9, channels)

    def by_owner(array):
        split = array.reshape(array.shape[0], blocks, owned).transpose(1, 0, 2)
        return jnp.pad(split, ((0, 0), (0, 0), (0, HALF - owned)))

    def side_by_side(first, second):
        return jnp.concatenate([by_owner(first), by_owner(second)], 2)

    small = pltpu.CompilerParams(vmem_limit_bytes=16 * 1024 * 1024)
    steps = 2 if channels % 512 == 0 else 1
    by_columns = pl.BlockSpec((tokens, channels // steps), lambda i: (0, i))

    if exact:
        packed = pl.pallas_call(
            pack_kernel,
            out_shape=jax.ShapeDtypeStruct((blocks, rows_in, LANES), bf16),
            grid=(steps,),
            in_specs=[by_columns] * 5,
            out_specs=pl.BlockSpec((blocks // steps, rows_in, LANES), lambda i: (i, 0, 0)),
            name="pack",
        )(stream_one, stream_two, stream_value, long_filter, out_grad)
    else:
        packed = jnp.concatenate(
            [
                side_by_side(stream_two, stream_one),
                side_by_side(stream_value, out_grad),
                side_by_side(long_filter[:half], long_filter[half:]),
            ],
            1,
        )

    unit = jnp.zeros((3, channels), f32).at[0].set(1.0)
    lower = jnp.concatenate([taps_flat[3:9], skip_gain[None], skip_gain[None]], 0)
    upper = jnp.concatenate([taps_flat[:3], unit, skip_gain[None], skip_gain[None]], 0)
    weights = lax.dynamic_index_in_dim(side_by_side(lower, upper), me, 0, keepdims=False)

    owned_chunk = lax.all_to_all(packed, "seq", 0, 0, tiled=True)

    forward, inverse = dft_tables(blocks, tokens)
    size = 2 * tokens
    table_spec = pl.BlockSpec((1, tokens, 2 * size), lambda k: (k, 0, 0))

    if exact and blocks <= 16:
        group = 6

        def resident(*refs):
            resident_kernel(blocks, *refs)

        returned = pl.pallas_call(
            resident,
            out_shape=jax.ShapeDtypeStruct((blocks, rows_out, LANES), bf16),
            in_specs=[VMEM, VMEM, HBM],
            out_specs=VMEM,
            scratch_shapes=[
                pltpu.VMEM((2, blocks + 1, tokens, 2 * size), bf16),
                pltpu.VMEM((blocks + 1, size, 2 * LANES), bf16),
                pltpu.VMEM((blocks + 1, size, 2 * LANES), bf16),
                pltpu.VMEM((2 * group, size, 2 * LANES), bf16),
                pltpu.VMEM((2 * group, size, 2 * LANES), bf16),
                pltpu.VMEM((blocks + 1, size, 2 * LANES), f32),
                pltpu.VMEM((blocks, tokens, LANES), f32),
                pltpu.VMEM((blocks, tokens, LANES), f32),
                pltpu.VMEM((blocks, tokens, LANES), bf16),
                pltpu.VMEM((blocks, tokens, LANES), f32),
                pltpu.VMEM((blocks, half, LANES), f32),
                pltpu.VMEM((8, 8, LANES), f32),
                pltpu.SemaphoreType.DMA((2,)),
            ],
            compiler_params=pltpu.CompilerParams(vmem_limit_bytes=48 * 1024 * 1024),
            name="owner",
        )(owned_chunk, weights, jnp.asarray(np.stack([forward, inverse])))
    else:

        def owner(*refs):
            owner_kernel(blocks, *refs)

        returned = pl.pallas_call(
            owner,
            out_shape=jax.ShapeDtypeStruct((blocks, rows_out, LANES), bf16),
            grid=(blocks + 1,),
            in_specs=[VMEM, VMEM, table_spec, table_spec],
            out_specs=VMEM,
            scratch_shapes=[
                pltpu.VMEM((blocks, tokens, LANES), f32),
                pltpu.VMEM((blocks + 1, size, 2 * LANES), f32),
                pltpu.VMEM((blocks, tokens, LANES), f32),
                pltpu.VMEM((blocks, half, LANES), f32),
                pltpu.VMEM((8, 8, LANES), f32),
            ],
            compiler_params=pltpu.CompilerParams(vmem_limit_bytes=58 * 1024 * 1024),
            name="owner",
        )(owned_chunk, weights, jnp.asarray(forward), jnp.asarray(inverse))

    back = lax.all_to_all(returned, "seq", 0, 0, tiled=True)

    if exact:
        shape = (tokens, channels)
        taps_spec = pl.BlockSpec((3, 3, channels // steps), lambda i: (0, 0, i))
        gates_spec = pl.BlockSpec((3, tokens, channels // steps), lambda i: (0, 0, i))
        gates = pl.pallas_call(
            gates_kernel,
            out_shape=jax.ShapeDtypeStruct((3,) + shape, f32),
            grid=(steps,),
            in_specs=[by_columns] * 3 + [taps_spec, ANY],
            out_specs=gates_spec,
            compiler_params=small,
            name="gates",
        )(stream_one, stream_two, stream_value, short_taps, returned)
        results = pl.pallas_call(
            finish_kernel,
            out_shape=[jax.ShapeDtypeStruct(shape, bf16)] * 4
            + [
                jax.ShapeDtypeStruct(shape, f32),
                jax.ShapeDtypeStruct(short_taps.shape, f32),
                jax.ShapeDtypeStruct((1, channels), f32),
            ],
            in_specs=[VMEM] * 4,
            out_specs=[ANY] * 5 + [VMEM] * 2,
            scratch_shapes=[pltpu.VMEM(shape, bf16)] * 4
            + [pltpu.VMEM(shape, f32), pltpu.SemaphoreType.DMA((5, 4))],
            compiler_params=small,
            name="finish",
        )(gates, out_grad, short_taps, back)
    else:
        wide = back.astype(f32)

        def joined(part):
            return part[:, :, :owned].transpose(1, 0, 2).reshape(rows_out, channels)

        rows = [taps_flat[i : i + 1] for i in range(9)]
        streams = [s.astype(f32) for s in (stream_one, stream_two, stream_value)]
        results = finish(
            local_gates(streams, rows),
            out_grad.astype(f32),
            rows,
            joined(wide[:, :, :HALF]),
            joined(wide[:, :, HALF:]),
        )
        results = [r.astype(bf16) for r in results[:4]] + [
            results[4],
            jnp.stack(results[5:8]),
            results[8],
        ]
    return tuple(results[:6]) + (results[6].reshape(channels),)


def solution(mesh):
    rows = P("seq", "ch")
    return jax.shard_map(
        per_device,
        mesh=mesh,
        in_specs=(rows, rows, rows, rows, P(None, None, "ch"), P("ch"), rows),
        out_specs=(rows, rows, rows, rows, rows, P(None, None, "ch"), P("ch")),
        check_vma=False,
    )
```

```python
import math

import jax
import jax.numpy as jnp
import ml_dtypes
import numpy as np
from jax import lax
from jax.experimental import pallas as pl
from jax.experimental.pallas import tpu as pltpu
from jax.sharding import PartitionSpec as P

HALF = 64
LANES = 2 * HALF
EXTRA = 16


def root(top, bottom):
    angle = math.pi * top / bottom
    return math.cos(angle), math.sin(angle)


def padded_dft(xs):
    m = len(xs)
    if m == 1:
        return [(xs[0], None), (xs[0], None)]
    even, odd = padded_dft(xs[0::2]), padded_dft(xs[1::2])
    out = [None] * (m + 1)
    for k in range(m // 2 + 1):
        (ar, ai), (br, bi) = even[k], odd[k]
        if k == 0:
            out[0], out[m] = (ar + br, None), (ar - br, None)
        elif 2 * k == m:
            out[k] = (ar, -br)
        else:
            c, s = root(k, m)
            if bi is None:
                tr, ti = br * c, br * -s
            else:
                tr, ti = br * c + bi * s, bi * c - br * s
            out[k] = (ar + tr, ti if ai is None else ai + ti)
            out[m - k] = (ar - tr, ti if ai is None else ti - ai)
    return out


def folded_sum(ys):
    m = len(ys) - 1
    if m == 1:
        return [ys[0][0] + ys[1][0]]
    even, odd = [], []
    for k in range(m // 2 + 1):
        (ar, ai), (br, bi) = ys[k], ys[m - k]
        if k == 0:
            even.append((ar + br, None))
            odd.append((ar - br, None))
        elif 2 * k == m:
            even.append((ar, None))
            odd.append((-ai, None))
        else:
            c, s = root(k, m)
            dr, di = ar - br, ai + bi
            even.append((ar + br, ai - bi))
            odd.append((dr * c - di * s, dr * s + di * c))
    out = [None] * m
    out[0::2], out[1::2] = folded_sum(even), folded_sum(odd)
    return out


def split_pair(values):
    high = values.astype(ml_dtypes.bfloat16)
    low = (values - high.astype(np.float64)).astype(ml_dtypes.bfloat16)
    return np.concatenate([high, low], axis=-1)


def dft_tables(blocks, tokens):
    period = 2 * blocks * tokens
    k1 = np.arange(blocks + 1)[:, None, None]
    k2 = np.arange(tokens)[None, :, None]
    place = np.arange(tokens)[None, None, :]
    angle = (2.0 * math.pi / period) * ((place * (k1 + 2 * blocks * k2)) % period)
    c, s = np.cos(angle), np.sin(angle)
    weight = np.where((k1 == 0) | (k1 == blocks), 1.0, 2.0) / period
    forward = np.concatenate([c, s], 2)
    inverse = np.concatenate([c.transpose(0, 2, 1), -s.transpose(0, 2, 1)], 2) * weight
    return split_pair(forward), split_pair(inverse)


def halves_swapped(values):
    return pltpu.roll(values, HALF, 1)


def interleave(first, second):
    low = lax.broadcasted_iota(jnp.int32, first.shape, 1) < HALF
    return (
        jnp.where(low, first, halves_swapped(second)),
        jnp.where(low, halves_swapped(first), second),
    )


def pack_kernel(one, two, value, filt, grad, out):
    tokens = one.shape[0]
    half = tokens // 2
    for pair in range(one.shape[1] // LANES):
        cols = slice(pair * LANES, (pair + 1) * LANES)
        tile = [ref[:, cols] for ref in (two, one, value, grad, filt)]
        parts = (
            (0, tokens, tile[0], tile[1]),
            (tokens, tokens, tile[2], tile[3]),
            (2 * tokens, half, tile[4][:half], tile[4][half:]),
        )
        for start, rows, first, second in parts:
            for side, piece in enumerate(interleave(first, second)):
                out[2 * pair + side, start : start + rows] = piece.astype(out.dtype)


def window_conv(window, weights, tokens):
    total = weights[0] * window[8 : 8 + tokens]
    for j in (1, 2):
        total = total + weights[j] * window[8 - j : 8 - j + tokens]
    return total


def owner_kernel(blocks, chunk, weights, ftab, itab, out, ug_ref, spec_ref, lg_ref, gf_ref, acc_ref):
    step = pl.program_id(0)
    tokens = ftab.shape[1]
    half = tokens // 2
    f32 = jnp.float32

    def block_rows(a, start):
        return chunk[a, start : start + tokens].astype(f32)

    def window(a, start):
        before = chunk[jnp.maximum(a - 1, 0), start + tokens - 16 : start + tokens].astype(f32)[8:]
        return jnp.concatenate([jnp.where(a > 0, before, 0.0), block_rows(a, start)], axis=0)

    w1 = [weights[j : j + 1] for j in range(3)]
    w2 = [weights[3 + j : 4 + j] for j in range(3)]

    @pl.when(step == 0)
    def _():
        @pl.loop(0, blocks)
        def _(a):
            c1 = window_conv(window(a, 0), w1, tokens)
            c2 = window_conv(window(a, tokens), w2, tokens)
            ug_ref[a] = (c1 * c2).astype(jnp.bfloat16).astype(f32)

        @pl.loop(0, tokens // 8)
        def _(r):
            at = pl.multiple_of(r * 8, 8)
            spectrum = padded_dft([ug_ref[a, pl.ds(at, 8)] for a in range(blocks)])
            for k, (real, imag) in enumerate(spectrum):
                spec_ref[k, pl.ds(at, 8), :LANES] = real
                spec_ref[k, pl.ds(tokens + at, 8), :LANES] = (
                    jnp.zeros_like(real) if imag is None else imag
                )

        @pl.loop(0, half // 16)
        def _(r):
            at = pl.multiple_of(r * 16, 16)
            tiles = [chunk[a, pl.ds(2 * tokens + at, 16)].astype(f32) for a in range(blocks)]
            low = lax.broadcasted_iota(jnp.int32, (8, LANES), 1) < HALF
            for sub in range(2):
                spectrum = padded_dft([t[8 * sub : 8 * sub + 8] for t in tiles])
                for k, pair in enumerate(spectrum):
                    for place, part in enumerate(pair):
                        part = jnp.zeros_like(pair[0]) if part is None else part
                        turned = halves_swapped(part)
                        row = place * tokens + at + 8 * sub
                        spec_ref[k, pl.ds(row, 8), LANES:] = jnp.where(low, part, turned)
                        spec_ref[k, pl.ds(row + half, 8), LANES:] = jnp.where(low, turned, part)

    def transform(table, values):
        high = values.astype(jnp.bfloat16)
        rest = (values - high.astype(f32)).astype(jnp.bfloat16)
        cos_high, sin_high, cos_low, sin_low = [
            table[0, :, i * tokens : (i + 1) * tokens] for i in range(4)
        ]
        left = jnp.concatenate(
            [
                jnp.concatenate([cos_high, sin_high, cos_low, sin_low], 1),
                jnp.concatenate([-sin_high, cos_high, -sin_low, cos_low], 1),
            ],
            0,
        )
        return jnp.dot(
            left, jnp.concatenate([high, high], 0), preferred_element_type=f32
        ) + jnp.dot(left[:, : 2 * tokens], rest, preferred_element_type=f32)

    spectral = transform(ftab, spec_ref[step])
    sign = jnp.where(lax.broadcasted_iota(jnp.int32, (tokens, LANES), 1) < HALF, 1.0, -1.0)
    ur, ui = spectral[:tokens, :LANES], spectral[tokens:, :LANES]
    hr, hi = spectral[:tokens, LANES:], spectral[tokens:, LANES:] * sign
    vr, vi = halves_swapped(ur), halves_swapped(ui)
    products = jnp.concatenate(
        [
            jnp.concatenate([ur * hr - ui * hi, ur * vr + ui * vi], 1),
            jnp.concatenate([ui * hr + ur * hi, vi * ur - vr * ui], 1),
        ],
        0,
    )
    spec_ref[step] = transform(itab, products)

    @pl.when(step == blocks)
    def _():
        skip = weights[6:7]
        low = lax.broadcasted_iota(jnp.int32, (8, LANES), 1) < HALF

        @pl.loop(0, tokens // 8)
        def _(r):
            at = pl.multiple_of(r * 8, 8)
            ys = [
                (spec_ref[k, pl.ds(at, 8), :LANES], spec_ref[k, pl.ds(tokens + at, 8), :LANES])
                for k in range(blocks + 1)
            ]
            for a, total in enumerate(folded_sum(ys)):
                lg_ref[a, pl.ds(at, 8)] = total + skip * ug_ref[a, pl.ds(at, 8)]

        @pl.loop(0, half // 8)
        def _(r):
            at = pl.multiple_of(r * 8, 8)
            ys = []
            for k in range(blocks + 1):
                pair = []
                for place in range(2):
                    row = place * tokens + at
                    top = spec_ref[k, pl.ds(row, 8), LANES:]
                    bottom = spec_ref[k, pl.ds(row + half, 8), LANES:]
                    pair.append(jnp.where(low, top, halves_swapped(bottom)))
                ys.append(tuple(pair))
            for a, total in enumerate(folded_sum(ys)):
                gf_ref[a, pl.ds(at, 8)] = total

        acc_ref[...] = jnp.zeros_like(acc_ref)

        def folded(values):
            total = values[:8]
            for r in range(1, tokens // 8):
                total = total + values[8 * r : 8 * r + 8]
            return total

        @pl.loop(0, blocks)
        def _(i):
            a = blocks - 1 - i
            one, two = window(a, 0), window(a, tokens)
            c1, c2 = window_conv(one, w1, tokens), window_conv(two, w2, tokens)
            lg = lg_ref[a]
            turned = halves_swapped(lg)
            x1, x2 = c2 * turned, c1 * turned
            ug = ug_ref[a]
            for j in range(3):
                acc_ref[j] += folded(x1 * one[8 - j : 8 - j + tokens])
                acc_ref[3 + j] += folded(x2 * two[8 - j : 8 - j + tokens])
            acc_ref[6] += folded(ug * halves_swapped(ug))
            after = acc_ref[7]
            out[a, :tokens] = lg.astype(out.dtype)
            out[a, tokens : tokens + half] = gf_ref[a].astype(out.dtype)
            out[a, tokens + half :] = jnp.concatenate(
                [after[:4], one[6:8], two[6:8], jnp.zeros((8, LANES), f32)], 0
            ).astype(out.dtype)
            acc_ref[7] = jnp.concatenate([x1[:2], x2[:2], jnp.zeros((4, LANES), f32)], 0)

        lower = lax.broadcasted_iota(jnp.int32, (1, LANES), 1) < HALF
        sums = [jnp.sum(acc_ref[j], axis=0, keepdims=True) for j in range(7)]
        sums[3] = jnp.where(lower, sums[3], sums[6])
        tail = jnp.concatenate(sums[:6] + [jnp.zeros((2, LANES), f32)], 0)

        @pl.loop(0, blocks)
        def _(a):
            rows = out[a, tokens + half :].astype(f32)
            out[a, tokens + half :] = jnp.concatenate([rows[:8], tail], 0).astype(out.dtype)


def resident_kernel(
    blocks, chunk, weights, tables_hbm, out,
    tables, high_ref, low_ref, zh_ref, zl_ref, spec_ref,
    s1_ref, s2_ref, c1_ref, c2_ref, ug_ref, lg_ref, gf_ref, acc_ref, sems,
):
    tokens = tables.shape[2]
    size = 2 * tokens
    half = tokens // 2
    f32, bf16 = jnp.float32, jnp.bfloat16
    copies = [
        pltpu.make_async_copy(tables_hbm.at[i], tables.at[i], sems.at[i]) for i in range(2)
    ]
    for copy in copies:
        copy.start()

    w1 = [weights[j : j + 1] for j in range(3)]
    w2 = [weights[3 + j : 4 + j] for j in range(3)]

    s1_ref[:8] = jnp.zeros((8, LANES), f32)
    s2_ref[:8] = jnp.zeros((8, LANES), f32)

    def earlier(ref, a, j):
        return ref[pl.ds(a * tokens + (8 - j), tokens)]

    def conv(ref, a, own, w):
        return w[0] * own + w[1] * earlier(ref, a, 1) + w[2] * earlier(ref, a, 2)

    @pl.loop(0, blocks)
    def _(a):
        at = pl.multiple_of(a * tokens + 8, 8)
        one, two = chunk[a, :tokens].astype(f32), chunk[a, tokens : 2 * tokens].astype(f32)
        s1_ref[pl.ds(at, tokens)], s2_ref[pl.ds(at, tokens)] = one, two
        c1, c2 = conv(s1_ref, a, one, w1), conv(s2_ref, a, two, w2)
        c1_ref[a], c2_ref[a] = c1, c2
        ug_ref[a] = (c1 * c2).astype(bf16)

    def put(k, row, cols, values):
        high = values.astype(bf16)
        high_ref[k, pl.ds(row, 16), cols] = high
        low_ref[k, pl.ds(row, 16), cols] = (values - high.astype(f32)).astype(bf16)

    left, right = slice(0, LANES), slice(LANES, 2 * LANES)

    @pl.loop(0, tokens // 16, unroll=2)
    def _(r):
        at = pl.multiple_of(r * 16, 16)
        spectrum = padded_dft([ug_ref[a, pl.ds(at, 16)].astype(f32) for a in range(blocks)])
        for k, (real, imag) in enumerate(spectrum):
            put(k, at, left, real)
            put(k, tokens + at, left, jnp.zeros_like(real) if imag is None else imag)

    @pl.loop(0, half // 16, unroll=2)
    def _(r):
        at = pl.multiple_of(r * 16, 16)
        low = lax.broadcasted_iota(jnp.int32, (16, LANES), 1) < HALF
        spectrum = padded_dft(
            [chunk[a, pl.ds(2 * tokens + at, 16)].astype(f32) for a in range(blocks)]
        )
        for k, pair in enumerate(spectrum):
            for place, part in enumerate(pair):
                part = jnp.zeros_like(pair[0]) if part is None else part
                turned = halves_swapped(part)
                put(k, place * tokens + at, right, jnp.where(low, part, turned))
                put(k, place * tokens + half + at, right, jnp.where(low, turned, part))

    def whole_map(table, k, start):
        pair = tables[table, k, :, start : start + size]
        return jnp.concatenate(
            [pair, jnp.concatenate([-pair[:, tokens:], pair[:, :tokens]], 1)], 0
        )

    def apply(table, k, high, rest):
        first = whole_map(table, k, 0)
        total = jnp.dot(first, high, preferred_element_type=f32)
        total = total + jnp.dot(whole_map(table, k, size), high, preferred_element_type=f32)
        return total + jnp.dot(first, rest, preferred_element_type=f32)

    sign = jnp.where(lax.broadcasted_iota(jnp.int32, (1, LANES), 1) < HALF, 1.0, -1.0)

    def into_products(k, slot):
        spectral = apply(0, k, high_ref[k], low_ref[k])
        ur, ui = spectral[:tokens, :LANES], spectral[tokens:, :LANES]
        hr, hi = spectral[:tokens, LANES:], spectral[tokens:, LANES:] * sign
        vr, vi = halves_swapped(ur), halves_swapped(ui)
        for place, cols, values in (
            (0, left, ur * hr - ui * hi),
            (1, left, ui * hr + ur * hi),
            (0, right, ur * vr + ui * vi),
            (1, right, vi * ur - vr * ui),
        ):
            rows = slice(place * tokens, (place + 1) * tokens)
            high = values.astype(bf16)
            zh_ref[slot, rows, cols] = high
            zl_ref[slot, rows, cols] = (values - high.astype(f32)).astype(bf16)

    def out_of_products(k, slot):
        spec_ref[k] = apply(1, k, zh_ref[slot], zl_ref[slot])

    copies[0].wait()

    group = zh_ref.shape[0] // 2
    whole = (blocks + 1) // group
    rest = range(whole * group, blocks + 1)
    for j in range(group):
        into_products(j, j)
    copies[1].wait()

    @pl.loop(1, whole)
    def _(i):
        now = lax.rem(i, 2) * group
        for j in range(group):
            out_of_products((i - 1) * group + j, group - now + j)
        for j in range(group):
            into_products(i * group + j, now + j)

    last = (whole - 1) % 2 * group
    for j, k in enumerate(rest):
        into_products(k, group - last + j)
    for j in range(group):
        out_of_products((whole - 1) * group + j, last + j)
    for j, k in enumerate(rest):
        out_of_products(k, group - last + j)

    skip = weights[6:7]
    low8 = lax.broadcasted_iota(jnp.int32, (8, LANES), 1) < HALF

    @pl.loop(0, tokens // 16)
    def _(r):
        at = pl.multiple_of(r * 16, 16)
        ug = [ug_ref[a, pl.ds(at, 16)].astype(f32) for a in range(blocks)]
        for sub in range(2):
            row = pl.multiple_of(at + 8 * sub, 8)
            ys = [
                (spec_ref[k, pl.ds(row, 8), left], spec_ref[k, pl.ds(tokens + row, 8), left])
                for k in range(blocks + 1)
            ]
            for a, total in enumerate(folded_sum(ys)):
                lg_ref[a, pl.ds(row, 8)] = total + skip * ug[a][8 * sub : 8 * sub + 8]

    @pl.loop(0, half // 8, unroll=2)
    def _(r):
        at = pl.multiple_of(r * 8, 8)
        ys = []
        for k in range(blocks + 1):
            pair = []
            for place in range(2):
                row = place * tokens + at
                top = spec_ref[k, pl.ds(row, 8), right]
                bottom = spec_ref[k, pl.ds(row + half, 8), right]
                pair.append(jnp.where(low8, top, halves_swapped(bottom)))
            ys.append(tuple(pair))
        for a, total in enumerate(folded_sum(ys)):
            gf_ref[a, pl.ds(at, 8)] = total

    acc_ref[...] = jnp.zeros_like(acc_ref)

    def folded(values):
        total = values[:8]
        for r in range(1, tokens // 8):
            total = total + values[8 * r : 8 * r + 8]
        return total

    @pl.loop(0, blocks, unroll=4)
    def _(i):
        a = blocks - 1 - i
        lg = lg_ref[a]
        turned = halves_swapped(lg)
        x1, x2 = c2_ref[a] * turned, c1_ref[a] * turned
        for j in range(3):
            acc_ref[j] += folded(x1 * earlier(s1_ref, a, j))
            acc_ref[3 + j] += folded(x2 * earlier(s2_ref, a, j))
        after = acc_ref[7]
        before = pl.multiple_of(a * tokens, 8)
        out[a, :tokens] = lg.astype(out.dtype)
        out[a, tokens : tokens + half] = gf_ref[a].astype(out.dtype)
        out[a, tokens + half :] = jnp.concatenate(
            [after[:4], s1_ref[pl.ds(before, 8)][6:], s2_ref[pl.ds(before, 8)][6:], jnp.zeros((8, LANES), f32)], 0
        ).astype(out.dtype)
        acc_ref[7] = jnp.concatenate([x1[:2], x2[:2], jnp.zeros((4, LANES), f32)], 0)

    lower = lax.broadcasted_iota(jnp.int32, (1, LANES), 1) < HALF
    sums = [jnp.sum(acc_ref[j], axis=0, keepdims=True) for j in range(6)]
    sums[3] = jnp.where(lower, sums[3], halves_swapped(gf_ref[0, :8])[:1])
    tail = jnp.concatenate(sums + [jnp.zeros((2, LANES), f32)], 0)

    @pl.loop(0, blocks, unroll=4)
    def _(a):
        rows = out[a, tokens + half :].astype(f32)
        out[a, tokens + half :] = jnp.concatenate([rows[:8], tail], 0).astype(out.dtype)


def local_gates(streams, weights):
    tokens = streams[0].shape[0]
    gates = []
    for s, stream in enumerate(streams):
        window = jnp.concatenate([jnp.zeros_like(stream[:8]), stream], 0)
        gates.append(window_conv(window, weights[3 * s : 3 * s + 3], tokens))
    return gates


def finish(gates, cotangent, weights, low, high):
    tokens = cotangent.shape[0]
    half = tokens // 2
    at = tokens + half
    long_out, grad_mixed = low[:tokens], high[:tokens]
    grad_filter = jnp.concatenate([low[tokens:at], high[tokens:at]], 0)
    before = (high[at + 4 : at + 6], low[at + 4 : at + 6], low[at + 6 : at + 8])
    after = (high[at : at + 2], low[at : at + 2], low[at + 2 : at + 4])
    whole = []
    for s in range(3):
        older, newer = before[s][:1], before[s][1:]
        w1, w2 = weights[3 * s + 1], weights[3 * s + 2]
        missing = jnp.concatenate(
            [w1 * newer + w2 * older, w2 * newer, jnp.zeros((6, older.shape[1]), jnp.float32)], 0
        )
        whole.append(jnp.concatenate([gates[s][:8] + missing, gates[s][8:]], 0))
    mixed_out = whole[0] * long_out
    conv_grads = (cotangent * long_out, grad_mixed * whole[2], grad_mixed * whole[1])
    grads = []
    for s in range(3):
        trailing = jnp.concatenate([conv_grads[s], after[s], jnp.zeros_like(low[:6])], 0)
        total = weights[3 * s] * trailing[:tokens]
        for j in (1, 2):
            total = total + weights[3 * s + j] * trailing[j : j + tokens]
        grads.append(total)
    return [mixed_out] + grads + [grad_filter]


def token_sums(low, high):
    return [high[:3], low[:3], low[3:6], high[3:4]]


def gates_kernel(one, two, value, weights, after, gates):
    del after
    for pair in range(one.shape[1] // LANES):
        cols = slice(pair * LANES, (pair + 1) * LANES)
        results = local_gates(
            [ref[:, cols].astype(jnp.float32) for ref in (one, two, value)],
            [weights[i // 3, i % 3 : i % 3 + 1, cols] for i in range(9)],
        )
        for s, result in enumerate(results):
            gates[s, :, cols] = result


def finish_kernel(gates, grad, weights, back, *refs):
    targets, buffers, sems, sum_sems = refs[:7], refs[7:14], refs[14], refs[15]
    grad_taps, grad_skip = buffers[5:]
    pieces = sems.shape[1]
    width = grad.shape[1] // pieces

    def copy(i, piece):
        cols = pl.ds(piece * width, width)
        return pltpu.make_async_copy(buffers[i].at[:, cols], targets[i].at[:, cols], sems.at[i, piece])

    for owner in range(0, back.shape[0], 2):
        cols = slice(owner * HALF, (owner + 2) * HALF)
        last = [back[owner + side, -16:].astype(jnp.float32)[8:] for side in range(2)]
        totals = token_sums(*interleave(*last))
        for s in range(3):
            grad_taps[s, :, cols] = totals[s]
        grad_skip[:, cols] = totals[3]
    sum_copies = [
        pltpu.make_async_copy(buffers[5 + i], targets[5 + i], sum_sems.at[i]) for i in range(2)
    ]
    for small_copy in sum_copies:
        small_copy.start()

    for piece in range(pieces):
        for start in range(piece * width, (piece + 1) * width, LANES):
            cols = slice(start, start + LANES)
            owner = start // HALF
            low, high = interleave(
                back[owner].astype(jnp.float32), back[owner + 1].astype(jnp.float32)
            )
            results = finish(
                [gates[s, :, cols] for s in range(3)],
                grad[:, cols].astype(jnp.float32),
                [weights[i // 3, i % 3 : i % 3 + 1, cols] for i in range(9)],
                low,
                high,
            )
            for ref, result in zip(buffers, results[:5]):
                ref[:, cols] = result.astype(ref.dtype)
        for i in range(5):
            copy(i, piece).start()
    for piece in range(pieces):
        for i in range(5):
            copy(i, piece).wait()
    for small_copy in sum_copies:
        small_copy.wait()


VMEM = pl.BlockSpec(memory_space=pltpu.VMEM)
ANY = pl.BlockSpec(memory_space=pl.ANY)
HBM = pl.BlockSpec(memory_space=pltpu.HBM)


def per_device(stream_one, stream_two, stream_value, long_filter, short_taps, skip_gain, out_grad):
    blocks = lax.axis_size("seq")
    me = lax.axis_index("seq")
    tokens, channels = stream_one.shape
    half = tokens // 2
    owned = channels // blocks
    exact = owned == HALF
    bf16, f32 = jnp.bfloat16, jnp.float32
    rows_in = 2 * tokens + half
    rows_out = tokens + half + EXTRA
    taps_flat = short_taps.reshape(9, channels)

    def by_owner(array):
        split = array.reshape(array.shape[0], blocks, owned).transpose(1, 0, 2)
        return jnp.pad(split, ((0, 0), (0, 0), (0, HALF - owned)))

    def side_by_side(first, second):
        return jnp.concatenate([by_owner(first), by_owner(second)], 2)

    small = pltpu.CompilerParams(vmem_limit_bytes=16 * 1024 * 1024)
    steps = 2 if channels % 512 == 0 else 1
    by_columns = pl.BlockSpec((tokens, channels // steps), lambda i: (0, i))

    if exact:
        packed = pl.pallas_call(
            pack_kernel,
            out_shape=jax.ShapeDtypeStruct((blocks, rows_in, LANES), bf16),
            grid=(steps,),
            in_specs=[by_columns] * 5,
            out_specs=pl.BlockSpec((blocks // steps, rows_in, LANES), lambda i: (i, 0, 0)),
            name="pack",
        )(stream_one, stream_two, stream_value, long_filter, out_grad)
    else:
        packed = jnp.concatenate(
            [
                side_by_side(stream_two, stream_one),
                side_by_side(stream_value, out_grad),
                side_by_side(long_filter[:half], long_filter[half:]),
            ],
            1,
        )

    unit = jnp.zeros((3, channels), f32).at[0].set(1.0)
    lower = jnp.concatenate([taps_flat[3:9], skip_gain[None], skip_gain[None]], 0)
    upper = jnp.concatenate([taps_flat[:3], unit, skip_gain[None], skip_gain[None]], 0)
    weights = lax.dynamic_index_in_dim(side_by_side(lower, upper), me, 0, keepdims=False)

    owned_chunk = lax.all_to_all(packed, "seq", 0, 0, tiled=True)

    forward, inverse = dft_tables(blocks, tokens)
    size = 2 * tokens
    table_spec = pl.BlockSpec((1, tokens, 2 * size), lambda k: (k, 0, 0))

    if exact and blocks <= 16:
        group = 6

        def resident(*refs):
            resident_kernel(blocks, *refs)

        returned = pl.pallas_call(
            resident,
            out_shape=jax.ShapeDtypeStruct((blocks, rows_out, LANES), bf16),
            in_specs=[VMEM, VMEM, HBM],
            out_specs=VMEM,
            scratch_shapes=[
                pltpu.VMEM((2, blocks + 1, tokens, 2 * size), bf16),
                pltpu.VMEM((blocks + 1, size, 2 * LANES), bf16),
                pltpu.VMEM((blocks + 1, size, 2 * LANES), bf16),
                pltpu.VMEM((2 * group, size, 2 * LANES), bf16),
                pltpu.VMEM((2 * group, size, 2 * LANES), bf16),
                pltpu.VMEM((blocks + 1, size, 2 * LANES), f32),
                pltpu.VMEM((blocks * tokens + 8, LANES), f32),
                pltpu.VMEM((blocks * tokens + 8, LANES), f32),
                pltpu.VMEM((blocks, tokens, LANES), f32),
                pltpu.VMEM((blocks, tokens, LANES), f32),
                pltpu.VMEM((blocks, tokens, LANES), bf16),
                pltpu.VMEM((blocks, tokens, LANES), f32),
                pltpu.VMEM((blocks, half, LANES), f32),
                pltpu.VMEM((8, 8, LANES), f32),
                pltpu.SemaphoreType.DMA((2,)),
            ],
            compiler_params=pltpu.CompilerParams(vmem_limit_bytes=48 * 1024 * 1024),
            name="owner",
        )(owned_chunk, weights, jnp.asarray(np.stack([forward, inverse])))
    else:

        def owner(*refs):
            owner_kernel(blocks, *refs)

        returned = pl.pallas_call(
            owner,
            out_shape=jax.ShapeDtypeStruct((blocks, rows_out, LANES), bf16),
            grid=(blocks + 1,),
            in_specs=[VMEM, VMEM, table_spec, table_spec],
            out_specs=VMEM,
            scratch_shapes=[
                pltpu.VMEM((blocks, tokens, LANES), f32),
                pltpu.VMEM((blocks + 1, size, 2 * LANES), f32),
                pltpu.VMEM((blocks, tokens, LANES), f32),
                pltpu.VMEM((blocks, half, LANES), f32),
                pltpu.VMEM((8, 8, LANES), f32),
            ],
            compiler_params=pltpu.CompilerParams(vmem_limit_bytes=58 * 1024 * 1024),
            name="owner",
        )(owned_chunk, weights, jnp.asarray(forward), jnp.asarray(inverse))

    back = lax.all_to_all(returned, "seq", 0, 0, tiled=True)

    if exact:
        shape = (tokens, channels)
        taps_spec = pl.BlockSpec((3, 3, channels // steps), lambda i: (0, 0, i))
        gates_spec = pl.BlockSpec((3, tokens, channels // steps), lambda i: (0, 0, i))
        gates = pl.pallas_call(
            gates_kernel,
            out_shape=jax.ShapeDtypeStruct((3,) + shape, f32),
            grid=(steps,),
            in_specs=[by_columns] * 3 + [taps_spec, ANY],
            out_specs=gates_spec,
            compiler_params=small,
            name="gates",
        )(stream_one, stream_two, stream_value, short_taps, returned)
        results = pl.pallas_call(
            finish_kernel,
            out_shape=[jax.ShapeDtypeStruct(shape, bf16)] * 4
            + [
                jax.ShapeDtypeStruct(shape, f32),
                jax.ShapeDtypeStruct(short_taps.shape, f32),
                jax.ShapeDtypeStruct((1, channels), f32),
            ],
            in_specs=[VMEM] * 4,
            out_specs=[ANY] * 7,
            scratch_shapes=[pltpu.VMEM(shape, bf16)] * 4
            + [
                pltpu.VMEM(shape, f32),
                pltpu.VMEM(short_taps.shape, f32),
                pltpu.VMEM((1, channels), f32),
                pltpu.SemaphoreType.DMA((5, 4)),
                pltpu.SemaphoreType.DMA((2,)),
            ],
            compiler_params=small,
            name="finish",
        )(gates, out_grad, short_taps, back)
    else:
        wide = back.astype(f32)

        def joined(part):
            return part[:, :, :owned].transpose(1, 0, 2).reshape(rows_out, channels)

        low, high = joined(wide[:, :, :HALF]), joined(wide[:, :, HALF:])
        rows = [taps_flat[i : i + 1] for i in range(9)]
        streams = [s.astype(f32) for s in (stream_one, stream_two, stream_value)]
        results = finish(local_gates(streams, rows), out_grad.astype(f32), rows, low, high)
        totals = token_sums(low[-8:], high[-8:])
        results = [r.astype(bf16) for r in results[:4]] + [
            results[4],
            jnp.stack(totals[:3]),
            totals[3],
        ]
    return tuple(results[:6]) + (results[6].reshape(channels),)


def solution(mesh):
    rows = P("seq", "ch")
    return jax.shard_map(
        per_device,
        mesh=mesh,
        in_specs=(rows, rows, rows, rows, P(None, None, "ch"), P("ch"), rows),
        out_specs=(rows, rows, rows, rows, rows, P(None, None, "ch"), P("ch")),
        check_vma=False,
    )
```

```python
import math

import jax
import jax.numpy as jnp
import ml_dtypes
import numpy as np
from jax import lax
from jax.experimental import pallas as pl
from jax.experimental.pallas import tpu as pltpu
from jax.sharding import PartitionSpec as P

HALF = 64
LANES = 2 * HALF
EXTRA = 16


def root(top, bottom):
    angle = math.pi * top / bottom
    return math.cos(angle), math.sin(angle)


def padded_dft(xs):
    m = len(xs)
    if m == 1:
        return [(xs[0], None), (xs[0], None)]
    even, odd = padded_dft(xs[0::2]), padded_dft(xs[1::2])
    out = [None] * (m + 1)
    for k in range(m // 2 + 1):
        (ar, ai), (br, bi) = even[k], odd[k]
        if k == 0:
            out[0], out[m] = (ar + br, None), (ar - br, None)
        elif 2 * k == m:
            out[k] = (ar, -br)
        else:
            c, s = root(k, m)
            if bi is None:
                tr, ti = br * c, br * -s
            else:
                tr, ti = br * c + bi * s, bi * c - br * s
            out[k] = (ar + tr, ti if ai is None else ai + ti)
            out[m - k] = (ar - tr, ti if ai is None else ti - ai)
    return out


def folded_sum(ys):
    m = len(ys) - 1
    if m == 1:
        return [ys[0][0] + ys[1][0]]
    even, odd = [], []
    for k in range(m // 2 + 1):
        (ar, ai), (br, bi) = ys[k], ys[m - k]
        if k == 0:
            even.append((ar + br, None))
            odd.append((ar - br, None))
        elif 2 * k == m:
            even.append((ar, None))
            odd.append((-ai, None))
        else:
            c, s = root(k, m)
            dr, di = ar - br, ai + bi
            even.append((ar + br, ai - bi))
            odd.append((dr * c - di * s, dr * s + di * c))
    out = [None] * m
    out[0::2], out[1::2] = folded_sum(even), folded_sum(odd)
    return out


def split_pair(values):
    high = values.astype(ml_dtypes.bfloat16)
    low = (values - high.astype(np.float64)).astype(ml_dtypes.bfloat16)
    return np.concatenate([high, low], axis=-1)


def dft_tables(blocks, tokens):
    period = 2 * blocks * tokens
    k1 = np.arange(blocks + 1)[:, None, None]
    k2 = np.arange(tokens)[None, :, None]
    place = np.arange(tokens)[None, None, :]
    angle = (2.0 * math.pi / period) * ((place * (k1 + 2 * blocks * k2)) % period)
    c, s = np.cos(angle), np.sin(angle)
    weight = np.where((k1 == 0) | (k1 == blocks), 1.0, 2.0) / period
    forward = np.concatenate([c, s], 2)
    inverse = np.concatenate([c.transpose(0, 2, 1), -s.transpose(0, 2, 1)], 2) * weight
    return split_pair(forward), split_pair(inverse)


def halves_swapped(values):
    return pltpu.roll(values, HALF, 1)


def interleave(first, second):
    low = lax.broadcasted_iota(jnp.int32, first.shape, 1) < HALF
    return (
        jnp.where(low, first, halves_swapped(second)),
        jnp.where(low, halves_swapped(first), second),
    )


def pack_kernel(one, two, value, filt, grad, out):
    tokens = one.shape[0]
    half = tokens // 2
    for pair in range(one.shape[1] // LANES):
        cols = slice(pair * LANES, (pair + 1) * LANES)
        tile = [ref[:, cols] for ref in (two, one, value, grad, filt)]
        parts = (
            (0, tokens, tile[0], tile[1]),
            (tokens, tokens, tile[2], tile[3]),
            (2 * tokens, half, tile[4][:half], tile[4][half:]),
        )
        for start, rows, first, second in parts:
            for side, piece in enumerate(interleave(first, second)):
                out[2 * pair + side, start : start + rows] = piece.astype(out.dtype)


def window_conv(window, weights, tokens):
    total = weights[0] * window[8 : 8 + tokens]
    for j in (1, 2):
        total = total + weights[j] * window[8 - j : 8 - j + tokens]
    return total


def owner_kernel(blocks, chunk, weights, ftab, itab, out, ug_ref, spec_ref, lg_ref, gf_ref, acc_ref):
    step = pl.program_id(0)
    tokens = ftab.shape[1]
    half = tokens // 2
    f32 = jnp.float32

    def block_rows(a, start):
        return chunk[a, start : start + tokens].astype(f32)

    def window(a, start):
        before = chunk[jnp.maximum(a - 1, 0), start + tokens - 16 : start + tokens].astype(f32)[8:]
        return jnp.concatenate([jnp.where(a > 0, before, 0.0), block_rows(a, start)], axis=0)

    w1 = [weights[j : j + 1] for j in range(3)]
    w2 = [weights[3 + j : 4 + j] for j in range(3)]

    @pl.when(step == 0)
    def _():
        @pl.loop(0, blocks)
        def _(a):
            c1 = window_conv(window(a, 0), w1, tokens)
            c2 = window_conv(window(a, tokens), w2, tokens)
            ug_ref[a] = (c1 * c2).astype(jnp.bfloat16).astype(f32)

        @pl.loop(0, tokens // 8)
        def _(r):
            at = pl.multiple_of(r * 8, 8)
            spectrum = padded_dft([ug_ref[a, pl.ds(at, 8)] for a in range(blocks)])
            for k, (real, imag) in enumerate(spectrum):
                spec_ref[k, pl.ds(at, 8), :LANES] = real
                spec_ref[k, pl.ds(tokens + at, 8), :LANES] = (
                    jnp.zeros_like(real) if imag is None else imag
                )

        @pl.loop(0, half // 16)
        def _(r):
            at = pl.multiple_of(r * 16, 16)
            tiles = [chunk[a, pl.ds(2 * tokens + at, 16)].astype(f32) for a in range(blocks)]
            low = lax.broadcasted_iota(jnp.int32, (8, LANES), 1) < HALF
            for sub in range(2):
                spectrum = padded_dft([t[8 * sub : 8 * sub + 8] for t in tiles])
                for k, pair in enumerate(spectrum):
                    for place, part in enumerate(pair):
                        part = jnp.zeros_like(pair[0]) if part is None else part
                        turned = halves_swapped(part)
                        row = place * tokens + at + 8 * sub
                        spec_ref[k, pl.ds(row, 8), LANES:] = jnp.where(low, part, turned)
                        spec_ref[k, pl.ds(row + half, 8), LANES:] = jnp.where(low, turned, part)

    def transform(table, values):
        high = values.astype(jnp.bfloat16)
        rest = (values - high.astype(f32)).astype(jnp.bfloat16)
        cos_high, sin_high, cos_low, sin_low = [
            table[0, :, i * tokens : (i + 1) * tokens] for i in range(4)
        ]
        left = jnp.concatenate(
            [
                jnp.concatenate([cos_high, sin_high, cos_low, sin_low], 1),
                jnp.concatenate([-sin_high, cos_high, -sin_low, cos_low], 1),
            ],
            0,
        )
        return jnp.dot(
            left, jnp.concatenate([high, high], 0), preferred_element_type=f32
        ) + jnp.dot(left[:, : 2 * tokens], rest, preferred_element_type=f32)

    spectral = transform(ftab, spec_ref[step])
    sign = jnp.where(lax.broadcasted_iota(jnp.int32, (tokens, LANES), 1) < HALF, 1.0, -1.0)
    ur, ui = spectral[:tokens, :LANES], spectral[tokens:, :LANES]
    hr, hi = spectral[:tokens, LANES:], spectral[tokens:, LANES:] * sign
    vr, vi = halves_swapped(ur), halves_swapped(ui)
    products = jnp.concatenate(
        [
            jnp.concatenate([ur * hr - ui * hi, ur * vr + ui * vi], 1),
            jnp.concatenate([ui * hr + ur * hi, vi * ur - vr * ui], 1),
        ],
        0,
    )
    spec_ref[step] = transform(itab, products)

    @pl.when(step == blocks)
    def _():
        skip = weights[6:7]
        low = lax.broadcasted_iota(jnp.int32, (8, LANES), 1) < HALF

        @pl.loop(0, tokens // 8)
        def _(r):
            at = pl.multiple_of(r * 8, 8)
            ys = [
                (spec_ref[k, pl.ds(at, 8), :LANES], spec_ref[k, pl.ds(tokens + at, 8), :LANES])
                for k in range(blocks + 1)
            ]
            for a, total in enumerate(folded_sum(ys)):
                lg_ref[a, pl.ds(at, 8)] = total + skip * ug_ref[a, pl.ds(at, 8)]

        @pl.loop(0, half // 8)
        def _(r):
            at = pl.multiple_of(r * 8, 8)
            ys = []
            for k in range(blocks + 1):
                pair = []
                for place in range(2):
                    row = place * tokens + at
                    top = spec_ref[k, pl.ds(row, 8), LANES:]
                    bottom = spec_ref[k, pl.ds(row + half, 8), LANES:]
                    pair.append(jnp.where(low, top, halves_swapped(bottom)))
                ys.append(tuple(pair))
            for a, total in enumerate(folded_sum(ys)):
                gf_ref[a, pl.ds(at, 8)] = total

        acc_ref[...] = jnp.zeros_like(acc_ref)

        def folded(values):
            total = values[:8]
            for r in range(1, tokens // 8):
                total = total + values[8 * r : 8 * r + 8]
            return total

        @pl.loop(0, blocks)
        def _(i):
            a = blocks - 1 - i
            one, two = window(a, 0), window(a, tokens)
            c1, c2 = window_conv(one, w1, tokens), window_conv(two, w2, tokens)
            lg = lg_ref[a]
            turned = halves_swapped(lg)
            x1, x2 = c2 * turned, c1 * turned
            ug = ug_ref[a]
            for j in range(3):
                acc_ref[j] += folded(x1 * one[8 - j : 8 - j + tokens])
                acc_ref[3 + j] += folded(x2 * two[8 - j : 8 - j + tokens])
            acc_ref[6] += folded(ug * halves_swapped(ug))
            after = acc_ref[7]
            out[a, :tokens] = lg.astype(out.dtype)
            out[a, tokens : tokens + half] = gf_ref[a].astype(out.dtype)
            out[a, tokens + half :] = jnp.concatenate(
                [after[:4], one[6:8], two[6:8], jnp.zeros((8, LANES), f32)], 0
            ).astype(out.dtype)
            acc_ref[7] = jnp.concatenate([x1[:2], x2[:2], jnp.zeros((4, LANES), f32)], 0)

        lower = lax.broadcasted_iota(jnp.int32, (1, LANES), 1) < HALF
        sums = [jnp.sum(acc_ref[j], axis=0, keepdims=True) for j in range(7)]
        sums[3] = jnp.where(lower, sums[3], sums[6])
        tail = jnp.concatenate(sums[:6] + [jnp.zeros((2, LANES), f32)], 0)

        @pl.loop(0, blocks)
        def _(a):
            rows = out[a, tokens + half :].astype(f32)
            out[a, tokens + half :] = jnp.concatenate([rows[:8], tail], 0).astype(out.dtype)


def resident_kernel(
    blocks, chunk, weights, tables_hbm, out,
    tables, high_ref, low_ref, zh_ref, zl_ref, spec_ref,
    s1_ref, s2_ref, c1_ref, c2_ref, ug_ref, lg_ref, gf_ref, acc_ref, sems,
):
    tokens = tables.shape[2]
    size = 2 * tokens
    half = tokens // 2
    f32, bf16 = jnp.float32, jnp.bfloat16
    copies = [
        pltpu.make_async_copy(tables_hbm.at[i], tables.at[i], sems.at[i]) for i in range(2)
    ]
    for copy in copies:
        copy.start()

    w1 = [weights[j : j + 1] for j in range(3)]
    w2 = [weights[3 + j : 4 + j] for j in range(3)]

    s1_ref[:8] = jnp.zeros((8, LANES), f32)
    s2_ref[:8] = jnp.zeros((8, LANES), f32)

    def earlier(ref, a, j):
        return ref[pl.ds(a * tokens + (8 - j), tokens)]

    def conv(ref, a, own, w):
        return w[0] * own + w[1] * earlier(ref, a, 1) + w[2] * earlier(ref, a, 2)

    acc_ref[...] = jnp.zeros_like(acc_ref)

    def folded(values):
        rows = [values[r : r + 8] for r in range(0, tokens, 8)]
        while len(rows) > 1:
            rows = [sum(rows[r : r + 2]) for r in range(0, len(rows), 2)]
        return rows[0]

    @pl.loop(0, blocks, unroll=blocks)
    def _(a):
        at = pl.multiple_of(a * tokens + 8, 8)
        one, two = chunk[a, :tokens].astype(f32), chunk[a, tokens : 2 * tokens].astype(f32)
        s1_ref[pl.ds(at, tokens)], s2_ref[pl.ds(at, tokens)] = one, two
        c1, c2 = conv(s1_ref, a, one, w1), conv(s2_ref, a, two, w2)
        c1_ref[a], c2_ref[a] = c1, c2
        ug = (c1 * c2).astype(bf16)
        ug_ref[a] = ug
        ug = ug.astype(f32)
        acc_ref[6] += folded(ug * halves_swapped(ug))

    def put(k, row, cols, values):
        high = values.astype(bf16)
        high_ref[k, pl.ds(row, 16), cols] = high
        low_ref[k, pl.ds(row, 16), cols] = (values - high.astype(f32)).astype(bf16)

    left, right = slice(0, LANES), slice(LANES, 2 * LANES)

    @pl.loop(0, tokens // 16, unroll=2)
    def _(r):
        at = pl.multiple_of(r * 16, 16)
        spectrum = padded_dft([ug_ref[a, pl.ds(at, 16)].astype(f32) for a in range(blocks)])
        for k, (real, imag) in enumerate(spectrum):
            put(k, at, left, real)
            put(k, tokens + at, left, jnp.zeros_like(real) if imag is None else imag)

    @pl.loop(0, half // 16, unroll=2)
    def _(r):
        at = pl.multiple_of(r * 16, 16)
        low = lax.broadcasted_iota(jnp.int32, (16, LANES), 1) < HALF
        spectrum = padded_dft(
            [chunk[a, pl.ds(2 * tokens + at, 16)].astype(f32) for a in range(blocks)]
        )
        for k, pair in enumerate(spectrum):
            for place, part in enumerate(pair):
                part = jnp.zeros_like(pair[0]) if part is None else part
                turned = halves_swapped(part)
                put(k, place * tokens + at, right, jnp.where(low, part, turned))
                put(k, place * tokens + half + at, right, jnp.where(low, turned, part))

    def whole_map(table, k, start):
        pair = tables[table, k, :, start : start + size]
        return jnp.concatenate(
            [pair, jnp.concatenate([-pair[:, tokens:], pair[:, :tokens]], 1)], 0
        )

    def apply(table, k, high, rest):
        first = whole_map(table, k, 0)
        total = jnp.dot(first, high, preferred_element_type=f32)
        total = total + jnp.dot(whole_map(table, k, size), high, preferred_element_type=f32)
        return total + jnp.dot(first, rest, preferred_element_type=f32)

    sign = jnp.where(lax.broadcasted_iota(jnp.int32, (1, LANES), 1) < HALF, 1.0, -1.0)

    def into_products(k, slot):
        spectral = apply(0, k, high_ref[k], low_ref[k])
        ur, ui = spectral[:tokens, :LANES], spectral[tokens:, :LANES]
        hr, hi = spectral[:tokens, LANES:], spectral[tokens:, LANES:] * sign
        vr, vi = halves_swapped(ur), halves_swapped(ui)
        for place, cols, values in (
            (0, left, ur * hr - ui * hi),
            (1, left, ui * hr + ur * hi),
            (0, right, ur * vr + ui * vi),
            (1, right, vi * ur - vr * ui),
        ):
            rows = slice(place * tokens, (place + 1) * tokens)
            high = values.astype(bf16)
            zh_ref[slot, rows, cols] = high
            zl_ref[slot, rows, cols] = (values - high.astype(f32)).astype(bf16)

    def out_of_products(k, slot):
        spec_ref[k] = apply(1, k, zh_ref[slot], zl_ref[slot])

    copies[0].wait()

    group = zh_ref.shape[0] // 2
    whole = (blocks + 1) // group
    rest = range(whole * group, blocks + 1)
    for j in range(group):
        into_products(j, j)
    copies[1].wait()

    @pl.loop(1, whole)
    def _(i):
        now = lax.rem(i, 2) * group
        for j in range(group):
            out_of_products((i - 1) * group + j, group - now + j)
        for j in range(group):
            into_products(i * group + j, now + j)

    last = (whole - 1) % 2 * group
    for j, k in enumerate(rest):
        into_products(k, group - last + j)
    for j in range(group):
        out_of_products((whole - 1) * group + j, last + j)
    for j, k in enumerate(rest):
        out_of_products(k, group - last + j)

    skip = weights[6:7]
    low8 = lax.broadcasted_iota(jnp.int32, (8, LANES), 1) < HALF

    @pl.loop(0, tokens // 16, unroll=tokens // 16)
    def _(r):
        at = pl.multiple_of(r * 16, 16)
        ug = [ug_ref[a, pl.ds(at, 16)].astype(f32) for a in range(blocks)]
        for sub in range(2):
            row = pl.multiple_of(at + 8 * sub, 8)
            ys = [
                (spec_ref[k, pl.ds(row, 8), left], spec_ref[k, pl.ds(tokens + row, 8), left])
                for k in range(blocks + 1)
            ]
            for a, total in enumerate(folded_sum(ys)):
                lg_ref[a, pl.ds(row, 8)] = total + skip * ug[a][8 * sub : 8 * sub + 8]

    @pl.loop(0, half // 8, unroll=half // 8)
    def _(r):
        at = pl.multiple_of(r * 8, 8)
        ys = []
        for k in range(blocks + 1):
            pair = []
            for place in range(2):
                row = place * tokens + at
                top = spec_ref[k, pl.ds(row, 8), right]
                bottom = spec_ref[k, pl.ds(row + half, 8), right]
                pair.append(jnp.where(low8, top, halves_swapped(bottom)))
            ys.append(tuple(pair))
        for a, total in enumerate(folded_sum(ys)):
            gf_ref[a, pl.ds(at, 8)] = total

    @pl.loop(0, blocks, unroll=blocks)
    def _(i):
        a = blocks - 1 - i
        lg = lg_ref[a]
        turned = halves_swapped(lg)
        x1, x2 = c2_ref[a] * turned, c1_ref[a] * turned
        for j in range(3):
            acc_ref[j] += folded(x1 * earlier(s1_ref, a, j))
            acc_ref[3 + j] += folded(x2 * earlier(s2_ref, a, j))
        after = acc_ref[7]
        before = pl.multiple_of(a * tokens, 8)
        out[a, :tokens] = lg.astype(out.dtype)
        out[a, tokens : tokens + half] = gf_ref[a].astype(out.dtype)
        out[a, tokens + half :] = jnp.concatenate(
            [after[:4], s1_ref[pl.ds(before, 8)][6:], s2_ref[pl.ds(before, 8)][6:], jnp.zeros((8, LANES), f32)], 0
        ).astype(out.dtype)
        acc_ref[7] = jnp.concatenate([x1[:2], x2[:2], jnp.zeros((4, LANES), f32)], 0)

    lower = lax.broadcasted_iota(jnp.int32, (1, LANES), 1) < HALF
    sums = [jnp.sum(acc_ref[j], axis=0, keepdims=True) for j in range(7)]
    sums[3] = jnp.where(lower, sums[3], sums[6])
    tail = jnp.concatenate(sums[:6] + [jnp.zeros((2, LANES), f32)], 0)

    @pl.loop(0, blocks, unroll=blocks)
    def _(a):
        rows = out[a, tokens + half :].astype(f32)
        out[a, tokens + half :] = jnp.concatenate([rows[:8], tail], 0).astype(out.dtype)


def local_gates(streams, weights):
    tokens = streams[0].shape[0]
    gates = []
    for s, stream in enumerate(streams):
        window = jnp.concatenate([jnp.zeros_like(stream[:8]), stream], 0)
        gates.append(window_conv(window, weights[3 * s : 3 * s + 3], tokens))
    return gates


def finish(gates, cotangent, weights, low, high):
    tokens = cotangent.shape[0]
    half = tokens // 2
    at = tokens + half
    long_out, grad_mixed = low[:tokens], high[:tokens]
    grad_filter = jnp.concatenate([low[tokens:at], high[tokens:at]], 0)
    before = (high[at + 4 : at + 6], low[at + 4 : at + 6], low[at + 6 : at + 8])
    after = (high[at : at + 2], low[at : at + 2], low[at + 2 : at + 4])
    whole = []
    for s in range(3):
        older, newer = before[s][:1], before[s][1:]
        w1, w2 = weights[3 * s + 1], weights[3 * s + 2]
        missing = jnp.concatenate(
            [w1 * newer + w2 * older, w2 * newer, jnp.zeros((6, older.shape[1]), jnp.float32)], 0
        )
        whole.append(jnp.concatenate([gates[s][:8] + missing, gates[s][8:]], 0))
    mixed_out = whole[0] * long_out
    conv_grads = (cotangent * long_out, grad_mixed * whole[2], grad_mixed * whole[1])
    grads = []
    for s in range(3):
        trailing = jnp.concatenate([conv_grads[s], after[s], jnp.zeros_like(low[:6])], 0)
        total = weights[3 * s] * trailing[:tokens]
        for j in (1, 2):
            total = total + weights[3 * s + j] * trailing[j : j + tokens]
        grads.append(total)
    return [mixed_out] + grads + [grad_filter]


def token_sums(low, high):
    return [high[:3], low[:3], low[3:6], high[3:4]]


def gates_kernel(one, two, value, weights, after, gates):
    del after
    for pair in range(one.shape[1] // LANES):
        cols = slice(pair * LANES, (pair + 1) * LANES)
        results = local_gates(
            [ref[:, cols].astype(jnp.float32) for ref in (one, two, value)],
            [weights[i // 3, i % 3 : i % 3 + 1, cols] for i in range(9)],
        )
        for s, result in enumerate(results):
            gates[s, :, cols] = result


def finish_kernel(gates, grad, weights, back, *refs):
    targets, buffers, sems, sum_sems = refs[:7], refs[7:14], refs[14], refs[15]
    grad_taps, grad_skip = buffers[5:]
    pieces = sems.shape[1]
    width = grad.shape[1] // pieces

    def copy(i, piece):
        cols = pl.ds(piece * width, width)
        return pltpu.make_async_copy(buffers[i].at[:, cols], targets[i].at[:, cols], sems.at[i, piece])

    for owner in range(0, back.shape[0], 2):
        cols = slice(owner * HALF, (owner + 2) * HALF)
        last = [back[owner + side, -16:].astype(jnp.float32)[8:] for side in range(2)]
        totals = token_sums(*interleave(*last))
        for s in range(3):
            grad_taps[s, :, cols] = totals[s]
        grad_skip[:, cols] = totals[3]
    sum_copies = [
        pltpu.make_async_copy(buffers[5 + i], targets[5 + i], sum_sems.at[i]) for i in range(2)
    ]
    for small_copy in sum_copies:
        small_copy.start()

    for piece in range(pieces):
        for start in range(piece * width, (piece + 1) * width, LANES):
            cols = slice(start, start + LANES)
            owner = start // HALF
            low, high = interleave(
                back[owner].astype(jnp.float32), back[owner + 1].astype(jnp.float32)
            )
            results = finish(
                [gates[s, :, cols] for s in range(3)],
                grad[:, cols].astype(jnp.float32),
                [weights[i // 3, i % 3 : i % 3 + 1, cols] for i in range(9)],
                low,
                high,
            )
            for ref, result in zip(buffers, results[:5]):
                ref[:, cols] = result.astype(ref.dtype)
        for i in range(5):
            copy(i, piece).start()
    for piece in range(pieces):
        for i in range(5):
            copy(i, piece).wait()
    for small_copy in sum_copies:
        small_copy.wait()


VMEM = pl.BlockSpec(memory_space=pltpu.VMEM)
ANY = pl.BlockSpec(memory_space=pl.ANY)
HBM = pl.BlockSpec(memory_space=pltpu.HBM)


def per_device(stream_one, stream_two, stream_value, long_filter, short_taps, skip_gain, out_grad):
    blocks = lax.axis_size("seq")
    me = lax.axis_index("seq")
    tokens, channels = stream_one.shape
    half = tokens // 2
    owned = channels // blocks
    exact = owned == HALF
    bf16, f32 = jnp.bfloat16, jnp.float32
    rows_in = 2 * tokens + half
    rows_out = tokens + half + EXTRA
    taps_flat = short_taps.reshape(9, channels)

    def by_owner(array):
        split = array.reshape(array.shape[0], blocks, owned).transpose(1, 0, 2)
        return jnp.pad(split, ((0, 0), (0, 0), (0, HALF - owned)))

    def side_by_side(first, second):
        return jnp.concatenate([by_owner(first), by_owner(second)], 2)

    small = pltpu.CompilerParams(vmem_limit_bytes=16 * 1024 * 1024)
    steps = 2 if channels % 512 == 0 else 1
    by_columns = pl.BlockSpec((tokens, channels // steps), lambda i: (0, i))

    if exact:
        packed = pl.pallas_call(
            pack_kernel,
            out_shape=jax.ShapeDtypeStruct((blocks, rows_in, LANES), bf16),
            grid=(steps,),
            in_specs=[by_columns] * 5,
            out_specs=pl.BlockSpec((blocks // steps, rows_in, LANES), lambda i: (i, 0, 0)),
            name="pack",
        )(stream_one, stream_two, stream_value, long_filter, out_grad)
    else:
        packed = jnp.concatenate(
            [
                side_by_side(stream_two, stream_one),
                side_by_side(stream_value, out_grad),
                side_by_side(long_filter[:half], long_filter[half:]),
            ],
            1,
        )

    unit = jnp.zeros((3, channels), f32).at[0].set(1.0)
    lower = jnp.concatenate([taps_flat[3:9], skip_gain[None], skip_gain[None]], 0)
    upper = jnp.concatenate([taps_flat[:3], unit, skip_gain[None], skip_gain[None]], 0)
    weights = lax.dynamic_index_in_dim(side_by_side(lower, upper), me, 0, keepdims=False)

    owned_chunk = lax.all_to_all(packed, "seq", 0, 0, tiled=True)

    forward, inverse = dft_tables(blocks, tokens)
    size = 2 * tokens
    table_spec = pl.BlockSpec((1, tokens, 2 * size), lambda k: (k, 0, 0))

    if exact and blocks <= 16:
        group = 6

        def resident(*refs):
            resident_kernel(blocks, *refs)

        returned = pl.pallas_call(
            resident,
            out_shape=jax.ShapeDtypeStruct((blocks, rows_out, LANES), bf16),
            in_specs=[VMEM, VMEM, HBM],
            out_specs=VMEM,
            scratch_shapes=[
                pltpu.VMEM((2, blocks + 1, tokens, 2 * size), bf16),
                pltpu.VMEM((blocks + 1, size, 2 * LANES), bf16),
                pltpu.VMEM((blocks + 1, size, 2 * LANES), bf16),
                pltpu.VMEM((2 * group, size, 2 * LANES), bf16),
                pltpu.VMEM((2 * group, size, 2 * LANES), bf16),
                pltpu.VMEM((blocks + 1, size, 2 * LANES), f32),
                pltpu.VMEM((blocks * tokens + 8, LANES), f32),
                pltpu.VMEM((blocks * tokens + 8, LANES), f32),
                pltpu.VMEM((blocks, tokens, LANES), f32),
                pltpu.VMEM((blocks, tokens, LANES), f32),
                pltpu.VMEM((blocks, tokens, LANES), bf16),
                pltpu.VMEM((blocks, tokens, LANES), f32),
                pltpu.VMEM((blocks, half, LANES), f32),
                pltpu.VMEM((8, 8, LANES), f32),
                pltpu.SemaphoreType.DMA((2,)),
            ],
            compiler_params=pltpu.CompilerParams(vmem_limit_bytes=48 * 1024 * 1024),
            name="owner",
        )(owned_chunk, weights, jnp.asarray(np.stack([forward, inverse])))
    else:

        def owner(*refs):
            owner_kernel(blocks, *refs)

        returned = pl.pallas_call(
            owner,
            out_shape=jax.ShapeDtypeStruct((blocks, rows_out, LANES), bf16),
            grid=(blocks + 1,),
            in_specs=[VMEM, VMEM, table_spec, table_spec],
            out_specs=VMEM,
            scratch_shapes=[
                pltpu.VMEM((blocks, tokens, LANES), f32),
                pltpu.VMEM((blocks + 1, size, 2 * LANES), f32),
                pltpu.VMEM((blocks, tokens, LANES), f32),
                pltpu.VMEM((blocks, half, LANES), f32),
                pltpu.VMEM((8, 8, LANES), f32),
            ],
            compiler_params=pltpu.CompilerParams(vmem_limit_bytes=58 * 1024 * 1024),
            name="owner",
        )(owned_chunk, weights, jnp.asarray(forward), jnp.asarray(inverse))

    back = lax.all_to_all(returned, "seq", 0, 0, tiled=True)

    if exact:
        shape = (tokens, channels)
        taps_spec = pl.BlockSpec((3, 3, channels // steps), lambda i: (0, 0, i))
        gates_spec = pl.BlockSpec((3, tokens, channels // steps), lambda i: (0, 0, i))
        gates = pl.pallas_call(
            gates_kernel,
            out_shape=jax.ShapeDtypeStruct((3,) + shape, f32),
            grid=(steps,),
            in_specs=[by_columns] * 3 + [taps_spec, ANY],
            out_specs=gates_spec,
            compiler_params=small,
            name="gates",
        )(stream_one, stream_two, stream_value, short_taps, returned)
        results = pl.pallas_call(
            finish_kernel,
            out_shape=[jax.ShapeDtypeStruct(shape, bf16)] * 4
            + [
                jax.ShapeDtypeStruct(shape, f32),
                jax.ShapeDtypeStruct(short_taps.shape, f32),
                jax.ShapeDtypeStruct((1, channels), f32),
            ],
            in_specs=[VMEM] * 4,
            out_specs=[ANY] * 7,
            scratch_shapes=[pltpu.VMEM(shape, bf16)] * 4
            + [
                pltpu.VMEM(shape, f32),
                pltpu.VMEM(short_taps.shape, f32),
                pltpu.VMEM((1, channels), f32),
                pltpu.SemaphoreType.DMA((5, 4)),
                pltpu.SemaphoreType.DMA((2,)),
            ],
            compiler_params=small,
            name="finish",
        )(gates, out_grad, short_taps, back)
    else:
        wide = back.astype(f32)

        def joined(part):
            return part[:, :, :owned].transpose(1, 0, 2).reshape(rows_out, channels)

        low, high = joined(wide[:, :, :HALF]), joined(wide[:, :, HALF:])
        rows = [taps_flat[i : i + 1] for i in range(9)]
        streams = [s.astype(f32) for s in (stream_one, stream_two, stream_value)]
        results = finish(local_gates(streams, rows), out_grad.astype(f32), rows, low, high)
        totals = token_sums(low[-8:], high[-8:])
        results = [r.astype(bf16) for r in results[:4]] + [
            results[4],
            jnp.stack(totals[:3]),
            totals[3],
        ]
    return tuple(results[:6]) + (results[6].reshape(channels),)


def solution(mesh):
    rows = P("seq", "ch")
    return jax.shard_map(
        per_device,
        mesh=mesh,
        in_specs=(rows, rows, rows, rows, P(None, None, "ch"), P("ch"), rows),
        out_specs=(rows, rows, rows, rows, rows, P(None, None, "ch"), P("ch")),
        check_vma=False,
    )
```

```python
import math

import jax
import jax.numpy as jnp
import ml_dtypes
import numpy as np
from jax import lax
from jax.experimental import pallas as pl
from jax.experimental.pallas import tpu as pltpu
from jax.sharding import PartitionSpec as P

HALF = 64
LANES = 2 * HALF
EXTRA = 16


def root(top, bottom):
    angle = math.pi * top / bottom
    return math.cos(angle), math.sin(angle)


def padded_dft(xs):
    m = len(xs)
    if m == 1:
        return [(xs[0], None), (xs[0], None)]
    even, odd = padded_dft(xs[0::2]), padded_dft(xs[1::2])
    out = [None] * (m + 1)
    for k in range(m // 2 + 1):
        (ar, ai), (br, bi) = even[k], odd[k]
        if k == 0:
            out[0], out[m] = (ar + br, None), (ar - br, None)
        elif 2 * k == m:
            out[k] = (ar, -br)
        else:
            c, s = root(k, m)
            if bi is None:
                tr, ti = br * c, br * -s
            else:
                tr, ti = br * c + bi * s, bi * c - br * s
            out[k] = (ar + tr, ti if ai is None else ai + ti)
            out[m - k] = (ar - tr, ti if ai is None else ti - ai)
    return out


def folded_sum(ys):
    m = len(ys) - 1
    if m == 1:
        return [ys[0][0] + ys[1][0]]
    even, odd = [], []
    for k in range(m // 2 + 1):
        (ar, ai), (br, bi) = ys[k], ys[m - k]
        if k == 0:
            even.append((ar + br, None))
            odd.append((ar - br, None))
        elif 2 * k == m:
            even.append((ar, None))
            odd.append((-ai, None))
        else:
            c, s = root(k, m)
            dr, di = ar - br, ai + bi
            even.append((ar + br, ai - bi))
            odd.append((dr * c - di * s, dr * s + di * c))
    out = [None] * m
    out[0::2], out[1::2] = folded_sum(even), folded_sum(odd)
    return out


def split_pair(values):
    high = values.astype(ml_dtypes.bfloat16)
    low = (values - high.astype(np.float64)).astype(ml_dtypes.bfloat16)
    return np.concatenate([high, low], axis=-1)


def dft_tables(blocks, tokens):
    period = 2 * blocks * tokens
    k1 = np.arange(blocks + 1)[:, None, None]
    k2 = np.arange(tokens)[None, :, None]
    place = np.arange(tokens)[None, None, :]
    angle = (2.0 * math.pi / period) * ((place * (k1 + 2 * blocks * k2)) % period)
    c, s = np.cos(angle), np.sin(angle)
    weight = np.where((k1 == 0) | (k1 == blocks), 1.0, 2.0) / period
    forward = np.concatenate([c, s], 2)
    inverse = np.concatenate([c.transpose(0, 2, 1), -s.transpose(0, 2, 1)], 2) * weight
    return split_pair(forward), split_pair(inverse)


def halves_swapped(values):
    return pltpu.roll(values, HALF, 1)


def interleave(first, second):
    low = lax.broadcasted_iota(jnp.int32, first.shape, 1) < HALF
    return (
        jnp.where(low, first, halves_swapped(second)),
        jnp.where(low, halves_swapped(first), second),
    )


def pack_kernel(one, two, value, filt, grad, out):
    tokens = one.shape[0]
    half = tokens // 2
    for pair in range(one.shape[1] // LANES):
        cols = slice(pair * LANES, (pair + 1) * LANES)
        tile = [ref[:, cols] for ref in (two, one, value, grad, filt)]
        parts = (
            (0, tokens, tile[0], tile[1]),
            (tokens, tokens, tile[2], tile[3]),
            (2 * tokens, half, tile[4][:half], tile[4][half:]),
        )
        for start, rows, first, second in parts:
            for side, piece in enumerate(interleave(first, second)):
                out[2 * pair + side, start : start + rows] = piece.astype(out.dtype)


def window_conv(window, weights, tokens):
    total = weights[0] * window[8 : 8 + tokens]
    for j in (1, 2):
        total = total + weights[j] * window[8 - j : 8 - j + tokens]
    return total


def owner_kernel(blocks, chunk, weights, ftab, itab, out, ug_ref, spec_ref, lg_ref, gf_ref, acc_ref):
    step = pl.program_id(0)
    tokens = ftab.shape[1]
    half = tokens // 2
    f32 = jnp.float32

    def block_rows(a, start):
        return chunk[a, start : start + tokens].astype(f32)

    def window(a, start):
        before = chunk[jnp.maximum(a - 1, 0), start + tokens - 16 : start + tokens].astype(f32)[8:]
        return jnp.concatenate([jnp.where(a > 0, before, 0.0), block_rows(a, start)], axis=0)

    w1 = [weights[j : j + 1] for j in range(3)]
    w2 = [weights[3 + j : 4 + j] for j in range(3)]

    @pl.when(step == 0)
    def _():
        @pl.loop(0, blocks)
        def _(a):
            c1 = window_conv(window(a, 0), w1, tokens)
            c2 = window_conv(window(a, tokens), w2, tokens)
            ug_ref[a] = (c1 * c2).astype(jnp.bfloat16).astype(f32)

        @pl.loop(0, tokens // 8)
        def _(r):
            at = pl.multiple_of(r * 8, 8)
            spectrum = padded_dft([ug_ref[a, pl.ds(at, 8)] for a in range(blocks)])
            for k, (real, imag) in enumerate(spectrum):
                spec_ref[k, pl.ds(at, 8), :LANES] = real
                spec_ref[k, pl.ds(tokens + at, 8), :LANES] = (
                    jnp.zeros_like(real) if imag is None else imag
                )

        @pl.loop(0, half // 16)
        def _(r):
            at = pl.multiple_of(r * 16, 16)
            tiles = [chunk[a, pl.ds(2 * tokens + at, 16)].astype(f32) for a in range(blocks)]
            low = lax.broadcasted_iota(jnp.int32, (8, LANES), 1) < HALF
            for sub in range(2):
                spectrum = padded_dft([t[8 * sub : 8 * sub + 8] for t in tiles])
                for k, pair in enumerate(spectrum):
                    for place, part in enumerate(pair):
                        part = jnp.zeros_like(pair[0]) if part is None else part
                        turned = halves_swapped(part)
                        row = place * tokens + at + 8 * sub
                        spec_ref[k, pl.ds(row, 8), LANES:] = jnp.where(low, part, turned)
                        spec_ref[k, pl.ds(row + half, 8), LANES:] = jnp.where(low, turned, part)

    def transform(table, values):
        high = values.astype(jnp.bfloat16)
        rest = (values - high.astype(f32)).astype(jnp.bfloat16)
        cos_high, sin_high, cos_low, sin_low = [
            table[0, :, i * tokens : (i + 1) * tokens] for i in range(4)
        ]
        left = jnp.concatenate(
            [
                jnp.concatenate([cos_high, sin_high, cos_low, sin_low], 1),
                jnp.concatenate([-sin_high, cos_high, -sin_low, cos_low], 1),
            ],
            0,
        )
        return jnp.dot(
            left, jnp.concatenate([high, high], 0), preferred_element_type=f32
        ) + jnp.dot(left[:, : 2 * tokens], rest, preferred_element_type=f32)

    spectral = transform(ftab, spec_ref[step])
    sign = jnp.where(lax.broadcasted_iota(jnp.int32, (tokens, LANES), 1) < HALF, 1.0, -1.0)
    ur, ui = spectral[:tokens, :LANES], spectral[tokens:, :LANES]
    hr, hi = spectral[:tokens, LANES:], spectral[tokens:, LANES:] * sign
    vr, vi = halves_swapped(ur), halves_swapped(ui)
    products = jnp.concatenate(
        [
            jnp.concatenate([ur * hr - ui * hi, ur * vr + ui * vi], 1),
            jnp.concatenate([ui * hr + ur * hi, vi * ur - vr * ui], 1),
        ],
        0,
    )
    spec_ref[step] = transform(itab, products)

    @pl.when(step == blocks)
    def _():
        skip = weights[6:7]
        low = lax.broadcasted_iota(jnp.int32, (8, LANES), 1) < HALF

        @pl.loop(0, tokens // 8)
        def _(r):
            at = pl.multiple_of(r * 8, 8)
            ys = [
                (spec_ref[k, pl.ds(at, 8), :LANES], spec_ref[k, pl.ds(tokens + at, 8), :LANES])
                for k in range(blocks + 1)
            ]
            for a, total in enumerate(folded_sum(ys)):
                lg_ref[a, pl.ds(at, 8)] = total + skip * ug_ref[a, pl.ds(at, 8)]

        @pl.loop(0, half // 8)
        def _(r):
            at = pl.multiple_of(r * 8, 8)
            ys = []
            for k in range(blocks + 1):
                pair = []
                for place in range(2):
                    row = place * tokens + at
                    top = spec_ref[k, pl.ds(row, 8), LANES:]
                    bottom = spec_ref[k, pl.ds(row + half, 8), LANES:]
                    pair.append(jnp.where(low, top, halves_swapped(bottom)))
                ys.append(tuple(pair))
            for a, total in enumerate(folded_sum(ys)):
                gf_ref[a, pl.ds(at, 8)] = total

        acc_ref[...] = jnp.zeros_like(acc_ref)

        def folded(values):
            total = values[:8]
            for r in range(1, tokens // 8):
                total = total + values[8 * r : 8 * r + 8]
            return total

        @pl.loop(0, blocks)
        def _(i):
            a = blocks - 1 - i
            one, two = window(a, 0), window(a, tokens)
            c1, c2 = window_conv(one, w1, tokens), window_conv(two, w2, tokens)
            lg = lg_ref[a]
            turned = halves_swapped(lg)
            x1, x2 = c2 * turned, c1 * turned
            ug = ug_ref[a]
            for j in range(3):
                acc_ref[j] += folded(x1 * one[8 - j : 8 - j + tokens])
                acc_ref[3 + j] += folded(x2 * two[8 - j : 8 - j + tokens])
            acc_ref[6] += folded(ug * halves_swapped(ug))
            after = acc_ref[7]
            out[a, :tokens] = lg.astype(out.dtype)
            out[a, tokens : tokens + half] = gf_ref[a].astype(out.dtype)
            out[a, tokens + half :] = jnp.concatenate(
                [after[:4], one[6:8], two[6:8], jnp.zeros((8, LANES), f32)], 0
            ).astype(out.dtype)
            acc_ref[7] = jnp.concatenate([x1[:2], x2[:2], jnp.zeros((4, LANES), f32)], 0)

        lower = lax.broadcasted_iota(jnp.int32, (1, LANES), 1) < HALF
        sums = [jnp.sum(acc_ref[j], axis=0, keepdims=True) for j in range(7)]
        sums[3] = jnp.where(lower, sums[3], sums[6])
        tail = jnp.concatenate(sums[:6] + [jnp.zeros((2, LANES), f32)], 0)

        @pl.loop(0, blocks)
        def _(a):
            rows = out[a, tokens + half :].astype(f32)
            out[a, tokens + half :] = jnp.concatenate([rows[:8], tail], 0).astype(out.dtype)


def resident_kernel(
    blocks, chunk, weights, tables_hbm, out,
    tables, raw_ref, zh_ref, zl_ref, spec_ref,
    s1_ref, s2_ref, c1_ref, c2_ref, ug_ref, lg_ref, gf_ref, acc_ref, sems,
):
    tokens = tables.shape[2]
    size = 2 * tokens
    half = tokens // 2
    f32, bf16 = jnp.float32, jnp.bfloat16
    copies = [
        pltpu.make_async_copy(tables_hbm.at[i], tables.at[i], sems.at[i]) for i in range(2)
    ]
    for copy in copies:
        copy.start()

    w1 = [weights[j : j + 1] for j in range(3)]
    w2 = [weights[3 + j : 4 + j] for j in range(3)]

    s1_ref[:8] = jnp.zeros((8, LANES), f32)
    s2_ref[:8] = jnp.zeros((8, LANES), f32)

    def earlier(ref, a, j):
        return ref[pl.ds(a * tokens + (8 - j), tokens)]

    def conv(ref, a, own, w):
        return w[0] * own + w[1] * earlier(ref, a, 1) + w[2] * earlier(ref, a, 2)

    acc_ref[...] = jnp.zeros_like(acc_ref)

    def folded(values):
        rows = [values[r : r + 8] for r in range(0, tokens, 8)]
        while len(rows) > 1:
            rows = [sum(rows[r : r + 2]) for r in range(0, len(rows), 2)]
        return rows[0]

    @pl.loop(0, blocks, unroll=blocks)
    def _(a):
        at = pl.multiple_of(a * tokens + 8, 8)
        one, two = chunk[a, :tokens].astype(f32), chunk[a, tokens : 2 * tokens].astype(f32)
        s1_ref[pl.ds(at, tokens)], s2_ref[pl.ds(at, tokens)] = one, two
        c1, c2 = conv(s1_ref, a, one, w1), conv(s2_ref, a, two, w2)
        c1_ref[a], c2_ref[a] = c1, c2
        ug = (c1 * c2).astype(bf16)
        ug_ref[a] = ug
        ug = ug.astype(f32)
        acc_ref[6] += folded(ug * halves_swapped(ug))

    def put(k, row, cols, values):
        raw_ref[k, pl.ds(row, 16), cols] = values

    left, right = slice(0, LANES), slice(LANES, 2 * LANES)

    @pl.loop(0, tokens // 16, unroll=2)
    def _(r):
        at = pl.multiple_of(r * 16, 16)
        spectrum = padded_dft([ug_ref[a, pl.ds(at, 16)].astype(f32) for a in range(blocks)])
        for k, (real, imag) in enumerate(spectrum):
            put(k, at, left, real)
            put(k, tokens + at, left, jnp.zeros_like(real) if imag is None else imag)

    @pl.loop(0, half // 16, unroll=2)
    def _(r):
        at = pl.multiple_of(r * 16, 16)
        low = lax.broadcasted_iota(jnp.int32, (16, LANES), 1) < HALF
        spectrum = padded_dft(
            [chunk[a, pl.ds(2 * tokens + at, 16)].astype(f32) for a in range(blocks)]
        )
        for k, pair in enumerate(spectrum):
            for place, part in enumerate(pair):
                part = jnp.zeros_like(pair[0]) if part is None else part
                turned = halves_swapped(part)
                put(k, place * tokens + at, right, jnp.where(low, part, turned))
                put(k, place * tokens + half + at, right, jnp.where(low, turned, part))

    def whole_map(table, k, start):
        pair = tables[table, k, :, start : start + size]
        return jnp.concatenate(
            [pair, jnp.concatenate([-pair[:, tokens:], pair[:, :tokens]], 1)], 0
        )

    def apply(table, k, high, rest):
        first = whole_map(table, k, 0)
        total = jnp.dot(first, high, preferred_element_type=f32)
        total = total + jnp.dot(whole_map(table, k, size), high, preferred_element_type=f32)
        return total + jnp.dot(first, rest, preferred_element_type=f32)

    sign = jnp.where(lax.broadcasted_iota(jnp.int32, (1, LANES), 1) < HALF, 1.0, -1.0)

    def into_products(k, slot):
        raw = raw_ref[k]
        coarse = raw.astype(bf16)
        spectral = apply(0, k, coarse, (raw - coarse.astype(f32)).astype(bf16))
        ur, ui = spectral[:tokens, :LANES], spectral[tokens:, :LANES]
        hr, hi = spectral[:tokens, LANES:], spectral[tokens:, LANES:] * sign
        vr, vi = halves_swapped(ur), halves_swapped(ui)
        for place, cols, values in (
            (0, left, ur * hr - ui * hi),
            (1, left, ui * hr + ur * hi),
            (0, right, ur * vr + ui * vi),
            (1, right, vi * ur - vr * ui),
        ):
            rows = slice(place * tokens, (place + 1) * tokens)
            high = values.astype(bf16)
            zh_ref[slot, rows, cols] = high
            zl_ref[slot, rows, cols] = (values - high.astype(f32)).astype(bf16)

    def out_of_products(k, slot):
        spec_ref[k] = apply(1, k, zh_ref[slot], zl_ref[slot])

    copies[0].wait()

    group = zh_ref.shape[0] // 2
    whole = (blocks + 1) // group
    rest = range(whole * group, blocks + 1)
    for j in range(group):
        into_products(j, j)
    copies[1].wait()

    @pl.loop(1, whole)
    def _(i):
        now = lax.rem(i, 2) * group
        for j in range(group):
            out_of_products((i - 1) * group + j, group - now + j)
        for j in range(group):
            into_products(i * group + j, now + j)

    last = (whole - 1) % 2 * group
    for j, k in enumerate(rest):
        into_products(k, group - last + j)
    for j in range(group):
        out_of_products((whole - 1) * group + j, last + j)
    for j, k in enumerate(rest):
        out_of_products(k, group - last + j)

    skip = weights[6:7]
    low8 = lax.broadcasted_iota(jnp.int32, (8, LANES), 1) < HALF

    @pl.loop(0, tokens // 16, unroll=tokens // 16)
    def _(r):
        at = pl.multiple_of(r * 16, 16)
        ug = [ug_ref[a, pl.ds(at, 16)].astype(f32) for a in range(blocks)]
        for sub in range(2):
            row = pl.multiple_of(at + 8 * sub, 8)
            ys = [
                (spec_ref[k, pl.ds(row, 8), left], spec_ref[k, pl.ds(tokens + row, 8), left])
                for k in range(blocks + 1)
            ]
            for a, total in enumerate(folded_sum(ys)):
                lg_ref[a, pl.ds(row, 8)] = total + skip * ug[a][8 * sub : 8 * sub + 8]

    @pl.loop(0, half // 8, unroll=half // 8)
    def _(r):
        at = pl.multiple_of(r * 8, 8)
        ys = []
        for k in range(blocks + 1):
            pair = []
            for place in range(2):
                row = place * tokens + at
                top = spec_ref[k, pl.ds(row, 8), right]
                bottom = spec_ref[k, pl.ds(row + half, 8), right]
                pair.append(jnp.where(low8, top, halves_swapped(bottom)))
            ys.append(tuple(pair))
        for a, total in enumerate(folded_sum(ys)):
            gf_ref[a, pl.ds(at, 8)] = total

    @pl.loop(0, blocks, unroll=blocks)
    def _(i):
        a = blocks - 1 - i
        lg = lg_ref[a]
        turned = halves_swapped(lg)
        x1, x2 = c2_ref[a] * turned, c1_ref[a] * turned
        for j in range(3):
            acc_ref[j] += folded(x1 * earlier(s1_ref, a, j))
            acc_ref[3 + j] += folded(x2 * earlier(s2_ref, a, j))
        after = acc_ref[7]
        before = pl.multiple_of(a * tokens, 8)
        out[a, :tokens] = lg.astype(out.dtype)
        out[a, tokens : tokens + half] = gf_ref[a].astype(out.dtype)
        out[a, tokens + half :] = jnp.concatenate(
            [after[:4], s1_ref[pl.ds(before, 8)][6:], s2_ref[pl.ds(before, 8)][6:], jnp.zeros((8, LANES), f32)], 0
        ).astype(out.dtype)
        acc_ref[7] = jnp.concatenate([x1[:2], x2[:2], jnp.zeros((4, LANES), f32)], 0)

    lower = lax.broadcasted_iota(jnp.int32, (1, LANES), 1) < HALF
    sums = [jnp.sum(acc_ref[j], axis=0, keepdims=True) for j in range(7)]
    sums[3] = jnp.where(lower, sums[3], sums[6])
    tail = jnp.concatenate(sums[:6] + [jnp.zeros((2, LANES), f32)], 0)

    @pl.loop(0, blocks, unroll=blocks)
    def _(a):
        rows = out[a, tokens + half :].astype(f32)
        out[a, tokens + half :] = jnp.concatenate([rows[:8], tail], 0).astype(out.dtype)


def local_gates(streams, weights):
    tokens = streams[0].shape[0]
    gates = []
    for s, stream in enumerate(streams):
        window = jnp.concatenate([jnp.zeros_like(stream[:8]), stream], 0)
        gates.append(window_conv(window, weights[3 * s : 3 * s + 3], tokens))
    return gates


def finish(gates, cotangent, weights, low, high):
    tokens = cotangent.shape[0]
    half = tokens // 2
    at = tokens + half
    long_out, grad_mixed = low[:tokens], high[:tokens]
    grad_filter = jnp.concatenate([low[tokens:at], high[tokens:at]], 0)
    before = (high[at + 4 : at + 6], low[at + 4 : at + 6], low[at + 6 : at + 8])
    after = (high[at : at + 2], low[at : at + 2], low[at + 2 : at + 4])
    whole = []
    for s in range(3):
        older, newer = before[s][:1], before[s][1:]
        w1, w2 = weights[3 * s + 1], weights[3 * s + 2]
        missing = jnp.concatenate(
            [w1 * newer + w2 * older, w2 * newer, jnp.zeros((6, older.shape[1]), jnp.float32)], 0
        )
        whole.append(jnp.concatenate([gates[s][:8] + missing, gates[s][8:]], 0))
    mixed_out = whole[0] * long_out
    conv_grads = (cotangent * long_out, grad_mixed * whole[2], grad_mixed * whole[1])
    grads = []
    for s in range(3):
        trailing = jnp.concatenate([conv_grads[s], after[s], jnp.zeros_like(low[:6])], 0)
        total = weights[3 * s] * trailing[:tokens]
        for j in (1, 2):
            total = total + weights[3 * s + j] * trailing[j : j + tokens]
        grads.append(total)
    return [mixed_out] + grads + [grad_filter]


def token_sums(low, high):
    return [high[:3], low[:3], low[3:6], high[3:4]]


def gates_kernel(one, two, value, weights, after, gates):
    del after
    for pair in range(one.shape[1] // LANES):
        cols = slice(pair * LANES, (pair + 1) * LANES)
        results = local_gates(
            [ref[:, cols].astype(jnp.float32) for ref in (one, two, value)],
            [weights[i // 3, i % 3 : i % 3 + 1, cols] for i in range(9)],
        )
        for s, result in enumerate(results):
            gates[s, :, cols] = result


def finish_kernel(gates, grad, weights, back, *refs):
    targets, buffers, sems, sum_sems = refs[:7], refs[7:14], refs[14], refs[15]
    grad_taps, grad_skip = buffers[5:]
    pieces = sems.shape[1]
    width = grad.shape[1] // pieces

    def copy(i, piece):
        cols = pl.ds(piece * width, width)
        return pltpu.make_async_copy(buffers[i].at[:, cols], targets[i].at[:, cols], sems.at[i, piece])

    for owner in range(0, back.shape[0], 2):
        cols = slice(owner * HALF, (owner + 2) * HALF)
        last = [back[owner + side, -16:].astype(jnp.float32)[8:] for side in range(2)]
        totals = token_sums(*interleave(*last))
        for s in range(3):
            grad_taps[s, :, cols] = totals[s]
        grad_skip[:, cols] = totals[3]
    sum_copies = [
        pltpu.make_async_copy(buffers[5 + i], targets[5 + i], sum_sems.at[i]) for i in range(2)
    ]
    for small_copy in sum_copies:
        small_copy.start()

    for piece in range(pieces):
        for start in range(piece * width, (piece + 1) * width, LANES):
            cols = slice(start, start + LANES)
            owner = start // HALF
            low, high = interleave(
                back[owner].astype(jnp.float32), back[owner + 1].astype(jnp.float32)
            )
            results = finish(
                [gates[s, :, cols] for s in range(3)],
                grad[:, cols].astype(jnp.float32),
                [weights[i // 3, i % 3 : i % 3 + 1, cols] for i in range(9)],
                low,
                high,
            )
            for ref, result in zip(buffers, results[:5]):
                ref[:, cols] = result.astype(ref.dtype)
        for i in range(5):
            copy(i, piece).start()
    for piece in range(pieces):
        for i in range(5):
            copy(i, piece).wait()
    for small_copy in sum_copies:
        small_copy.wait()


VMEM = pl.BlockSpec(memory_space=pltpu.VMEM)
ANY = pl.BlockSpec(memory_space=pl.ANY)
HBM = pl.BlockSpec(memory_space=pltpu.HBM)


def per_device(stream_one, stream_two, stream_value, long_filter, short_taps, skip_gain, out_grad):
    blocks = lax.axis_size("seq")
    me = lax.axis_index("seq")
    tokens, channels = stream_one.shape
    half = tokens // 2
    owned = channels // blocks
    exact = owned == HALF
    bf16, f32 = jnp.bfloat16, jnp.float32
    rows_in = 2 * tokens + half
    rows_out = tokens + half + EXTRA
    taps_flat = short_taps.reshape(9, channels)

    def by_owner(array):
        split = array.reshape(array.shape[0], blocks, owned).transpose(1, 0, 2)
        return jnp.pad(split, ((0, 0), (0, 0), (0, HALF - owned)))

    def side_by_side(first, second):
        return jnp.concatenate([by_owner(first), by_owner(second)], 2)

    small = pltpu.CompilerParams(vmem_limit_bytes=16 * 1024 * 1024)
    steps = 2 if channels % 512 == 0 else 1
    by_columns = pl.BlockSpec((tokens, channels // steps), lambda i: (0, i))

    if exact:
        packed = pl.pallas_call(
            pack_kernel,
            out_shape=jax.ShapeDtypeStruct((blocks, rows_in, LANES), bf16),
            grid=(steps,),
            in_specs=[by_columns] * 5,
            out_specs=pl.BlockSpec((blocks // steps, rows_in, LANES), lambda i: (i, 0, 0)),
            name="pack",
        )(stream_one, stream_two, stream_value, long_filter, out_grad)
    else:
        packed = jnp.concatenate(
            [
                side_by_side(stream_two, stream_one),
                side_by_side(stream_value, out_grad),
                side_by_side(long_filter[:half], long_filter[half:]),
            ],
            1,
        )

    unit = jnp.zeros((3, channels), f32).at[0].set(1.0)
    lower = jnp.concatenate([taps_flat[3:9], skip_gain[None], skip_gain[None]], 0)
    upper = jnp.concatenate([taps_flat[:3], unit, skip_gain[None], skip_gain[None]], 0)
    weights = lax.dynamic_index_in_dim(side_by_side(lower, upper), me, 0, keepdims=False)

    owned_chunk = lax.all_to_all(packed, "seq", 0, 0, tiled=True)

    forward, inverse = dft_tables(blocks, tokens)
    size = 2 * tokens
    table_spec = pl.BlockSpec((1, tokens, 2 * size), lambda k: (k, 0, 0))

    if exact and blocks <= 16:
        group = 6

        def resident(*refs):
            resident_kernel(blocks, *refs)

        returned = pl.pallas_call(
            resident,
            out_shape=jax.ShapeDtypeStruct((blocks, rows_out, LANES), bf16),
            in_specs=[VMEM, VMEM, HBM],
            out_specs=VMEM,
            scratch_shapes=[
                pltpu.VMEM((2, blocks + 1, tokens, 2 * size), bf16),
                pltpu.VMEM((blocks + 1, size, 2 * LANES), f32),
                pltpu.VMEM((2 * group, size, 2 * LANES), bf16),
                pltpu.VMEM((2 * group, size, 2 * LANES), bf16),
                pltpu.VMEM((blocks + 1, size, 2 * LANES), f32),
                pltpu.VMEM((blocks * tokens + 8, LANES), f32),
                pltpu.VMEM((blocks * tokens + 8, LANES), f32),
                pltpu.VMEM((blocks, tokens, LANES), f32),
                pltpu.VMEM((blocks, tokens, LANES), f32),
                pltpu.VMEM((blocks, tokens, LANES), bf16),
                pltpu.VMEM((blocks, tokens, LANES), f32),
                pltpu.VMEM((blocks, half, LANES), f32),
                pltpu.VMEM((8, 8, LANES), f32),
                pltpu.SemaphoreType.DMA((2,)),
            ],
            compiler_params=pltpu.CompilerParams(vmem_limit_bytes=48 * 1024 * 1024),
            name="owner",
        )(owned_chunk, weights, jnp.asarray(np.stack([forward, inverse])))
    else:

        def owner(*refs):
            owner_kernel(blocks, *refs)

        returned = pl.pallas_call(
            owner,
            out_shape=jax.ShapeDtypeStruct((blocks, rows_out, LANES), bf16),
            grid=(blocks + 1,),
            in_specs=[VMEM, VMEM, table_spec, table_spec],
            out_specs=VMEM,
            scratch_shapes=[
                pltpu.VMEM((blocks, tokens, LANES), f32),
                pltpu.VMEM((blocks + 1, size, 2 * LANES), f32),
                pltpu.VMEM((blocks, tokens, LANES), f32),
                pltpu.VMEM((blocks, half, LANES), f32),
                pltpu.VMEM((8, 8, LANES), f32),
            ],
            compiler_params=pltpu.CompilerParams(vmem_limit_bytes=58 * 1024 * 1024),
            name="owner",
        )(owned_chunk, weights, jnp.asarray(forward), jnp.asarray(inverse))

    back = lax.all_to_all(returned, "seq", 0, 0, tiled=True)

    if exact:
        shape = (tokens, channels)
        taps_spec = pl.BlockSpec((3, 3, channels // steps), lambda i: (0, 0, i))
        gates_spec = pl.BlockSpec((3, tokens, channels // steps), lambda i: (0, 0, i))
        gates = pl.pallas_call(
            gates_kernel,
            out_shape=jax.ShapeDtypeStruct((3,) + shape, f32),
            grid=(steps,),
            in_specs=[by_columns] * 3 + [taps_spec, ANY],
            out_specs=gates_spec,
            compiler_params=small,
            name="gates",
        )(stream_one, stream_two, stream_value, short_taps, returned)
        results = pl.pallas_call(
            finish_kernel,
            out_shape=[jax.ShapeDtypeStruct(shape, bf16)] * 4
            + [
                jax.ShapeDtypeStruct(shape, f32),
                jax.ShapeDtypeStruct(short_taps.shape, f32),
                jax.ShapeDtypeStruct((1, channels), f32),
            ],
            in_specs=[VMEM] * 4,
            out_specs=[ANY] * 7,
            scratch_shapes=[pltpu.VMEM(shape, bf16)] * 4
            + [
                pltpu.VMEM(shape, f32),
                pltpu.VMEM(short_taps.shape, f32),
                pltpu.VMEM((1, channels), f32),
                pltpu.SemaphoreType.DMA((5, 4)),
                pltpu.SemaphoreType.DMA((2,)),
            ],
            compiler_params=small,
            name="finish",
        )(gates, out_grad, short_taps, back)
    else:
        wide = back.astype(f32)

        def joined(part):
            return part[:, :, :owned].transpose(1, 0, 2).reshape(rows_out, channels)

        low, high = joined(wide[:, :, :HALF]), joined(wide[:, :, HALF:])
        rows = [taps_flat[i : i + 1] for i in range(9)]
        streams = [s.astype(f32) for s in (stream_one, stream_two, stream_value)]
        results = finish(local_gates(streams, rows), out_grad.astype(f32), rows, low, high)
        totals = token_sums(low[-8:], high[-8:])
        results = [r.astype(bf16) for r in results[:4]] + [
            results[4],
            jnp.stack(totals[:3]),
            totals[3],
        ]
    return tuple(results[:6]) + (results[6].reshape(channels),)


def solution(mesh):
    rows = P("seq", "ch")
    return jax.shard_map(
        per_device,
        mesh=mesh,
        in_specs=(rows, rows, rows, rows, P(None, None, "ch"), P("ch"), rows),
        out_specs=(rows, rows, rows, rows, rows, P(None, None, "ch"), P("ch")),
        check_vma=False,
    )
```

```python
import math

import jax
import jax.numpy as jnp
import ml_dtypes
import numpy as np
from jax import lax
from jax.experimental import pallas as pl
from jax.experimental.pallas import tpu as pltpu
from jax.sharding import PartitionSpec as P

HALF = 64
LANES = 2 * HALF
EXTRA = 16


def root(top, bottom):
    angle = math.pi * top / bottom
    return math.cos(angle), math.sin(angle)


def padded_dft(xs):
    m = len(xs)
    if m == 1:
        return [(xs[0], None), (xs[0], None)]
    even, odd = padded_dft(xs[0::2]), padded_dft(xs[1::2])
    out = [None] * (m + 1)
    for k in range(m // 2 + 1):
        (ar, ai), (br, bi) = even[k], odd[k]
        if k == 0:
            out[0], out[m] = (ar + br, None), (ar - br, None)
        elif 2 * k == m:
            out[k] = (ar, -br)
        else:
            c, s = root(k, m)
            if bi is None:
                tr, ti = br * c, br * -s
            else:
                tr, ti = br * c + bi * s, bi * c - br * s
            out[k] = (ar + tr, ti if ai is None else ai + ti)
            out[m - k] = (ar - tr, ti if ai is None else ti - ai)
    return out


def folded_sum(ys):
    m = len(ys) - 1
    if m == 1:
        return [ys[0][0] + ys[1][0]]
    even, odd = [], []
    for k in range(m // 2 + 1):
        (ar, ai), (br, bi) = ys[k], ys[m - k]
        if k == 0:
            even.append((ar + br, None))
            odd.append((ar - br, None))
        elif 2 * k == m:
            even.append((ar, None))
            odd.append((-ai, None))
        else:
            c, s = root(k, m)
            dr, di = ar - br, ai + bi
            even.append((ar + br, ai - bi))
            odd.append((dr * c - di * s, dr * s + di * c))
    out = [None] * m
    out[0::2], out[1::2] = folded_sum(even), folded_sum(odd)
    return out


def split_pair(values):
    high = values.astype(ml_dtypes.bfloat16)
    low = (values - high.astype(np.float64)).astype(ml_dtypes.bfloat16)
    return np.concatenate([high, low], axis=-1)


def dft_tables(blocks, tokens):
    period = 2 * blocks * tokens
    k1 = np.arange(blocks + 1)[:, None, None]
    k2 = np.arange(tokens)[None, :, None]
    place = np.arange(tokens)[None, None, :]
    angle = (2.0 * math.pi / period) * ((place * (k1 + 2 * blocks * k2)) % period)
    c, s = np.cos(angle), np.sin(angle)
    weight = np.where((k1 == 0) | (k1 == blocks), 1.0, 2.0) / period
    forward = np.concatenate([c, s], 2)
    inverse = np.concatenate([c.transpose(0, 2, 1), -s.transpose(0, 2, 1)], 2) * weight
    return split_pair(forward), split_pair(inverse)


def halves_swapped(values):
    return pltpu.roll(values, HALF, 1)


def interleave(first, second):
    low = lax.broadcasted_iota(jnp.int32, first.shape, 1) < HALF
    return (
        jnp.where(low, first, halves_swapped(second)),
        jnp.where(low, halves_swapped(first), second),
    )


def pack_kernel(one, two, value, filt, grad, out):
    tokens = one.shape[0]
    half = tokens // 2
    for pair in range(one.shape[1] // LANES):
        cols = slice(pair * LANES, (pair + 1) * LANES)
        tile = [ref[:, cols] for ref in (two, one, value, grad, filt)]
        parts = (
            (0, tokens, tile[0], tile[1]),
            (tokens, tokens, tile[2], tile[3]),
            (2 * tokens, half, tile[4][:half], tile[4][half:]),
        )
        for start, rows, first, second in parts:
            for side, piece in enumerate(interleave(first, second)):
                out[2 * pair + side, start : start + rows] = piece.astype(out.dtype)


def window_conv(window, weights, tokens):
    total = weights[0] * window[8 : 8 + tokens]
    for j in (1, 2):
        total = total + weights[j] * window[8 - j : 8 - j + tokens]
    return total


def owner_kernel(blocks, chunk, weights, ftab, itab, out, ug_ref, spec_ref, lg_ref, gf_ref, acc_ref):
    step = pl.program_id(0)
    tokens = ftab.shape[1]
    half = tokens // 2
    f32 = jnp.float32

    def block_rows(a, start):
        return chunk[a, start : start + tokens].astype(f32)

    def window(a, start):
        before = chunk[jnp.maximum(a - 1, 0), start + tokens - 16 : start + tokens].astype(f32)[8:]
        return jnp.concatenate([jnp.where(a > 0, before, 0.0), block_rows(a, start)], axis=0)

    w1 = [weights[j : j + 1] for j in range(3)]
    w2 = [weights[3 + j : 4 + j] for j in range(3)]

    @pl.when(step == 0)
    def _():
        @pl.loop(0, blocks)
        def _(a):
            c1 = window_conv(window(a, 0), w1, tokens)
            c2 = window_conv(window(a, tokens), w2, tokens)
            ug_ref[a] = (c1 * c2).astype(jnp.bfloat16).astype(f32)

        @pl.loop(0, tokens // 8)
        def _(r):
            at = pl.multiple_of(r * 8, 8)
            spectrum = padded_dft([ug_ref[a, pl.ds(at, 8)] for a in range(blocks)])
            for k, (real, imag) in enumerate(spectrum):
                spec_ref[k, pl.ds(at, 8), :LANES] = real
                spec_ref[k, pl.ds(tokens + at, 8), :LANES] = (
                    jnp.zeros_like(real) if imag is None else imag
                )

        @pl.loop(0, half // 16)
        def _(r):
            at = pl.multiple_of(r * 16, 16)
            tiles = [chunk[a, pl.ds(2 * tokens + at, 16)].astype(f32) for a in range(blocks)]
            low = lax.broadcasted_iota(jnp.int32, (8, LANES), 1) < HALF
            for sub in range(2):
                spectrum = padded_dft([t[8 * sub : 8 * sub + 8] for t in tiles])
                for k, pair in enumerate(spectrum):
                    for place, part in enumerate(pair):
                        part = jnp.zeros_like(pair[0]) if part is None else part
                        turned = halves_swapped(part)
                        row = place * tokens + at + 8 * sub
                        spec_ref[k, pl.ds(row, 8), LANES:] = jnp.where(low, part, turned)
                        spec_ref[k, pl.ds(row + half, 8), LANES:] = jnp.where(low, turned, part)

    def transform(table, values):
        high = values.astype(jnp.bfloat16)
        rest = (values - high.astype(f32)).astype(jnp.bfloat16)
        cos_high, sin_high, cos_low, sin_low = [
            table[0, :, i * tokens : (i + 1) * tokens] for i in range(4)
        ]
        left = jnp.concatenate(
            [
                jnp.concatenate([cos_high, sin_high, cos_low, sin_low], 1),
                jnp.concatenate([-sin_high, cos_high, -sin_low, cos_low], 1),
            ],
            0,
        )
        return jnp.dot(
            left, jnp.concatenate([high, high], 0), preferred_element_type=f32
        ) + jnp.dot(left[:, : 2 * tokens], rest, preferred_element_type=f32)

    spectral = transform(ftab, spec_ref[step])
    sign = jnp.where(lax.broadcasted_iota(jnp.int32, (tokens, LANES), 1) < HALF, 1.0, -1.0)
    ur, ui = spectral[:tokens, :LANES], spectral[tokens:, :LANES]
    hr, hi = spectral[:tokens, LANES:], spectral[tokens:, LANES:] * sign
    vr, vi = halves_swapped(ur), halves_swapped(ui)
    products = jnp.concatenate(
        [
            jnp.concatenate([ur * hr - ui * hi, ur * vr + ui * vi], 1),
            jnp.concatenate([ui * hr + ur * hi, vi * ur - vr * ui], 1),
        ],
        0,
    )
    spec_ref[step] = transform(itab, products)

    @pl.when(step == blocks)
    def _():
        skip = weights[6:7]
        low = lax.broadcasted_iota(jnp.int32, (8, LANES), 1) < HALF

        @pl.loop(0, tokens // 8)
        def _(r):
            at = pl.multiple_of(r * 8, 8)
            ys = [
                (spec_ref[k, pl.ds(at, 8), :LANES], spec_ref[k, pl.ds(tokens + at, 8), :LANES])
                for k in range(blocks + 1)
            ]
            for a, total in enumerate(folded_sum(ys)):
                lg_ref[a, pl.ds(at, 8)] = total + skip * ug_ref[a, pl.ds(at, 8)]

        @pl.loop(0, half // 8)
        def _(r):
            at = pl.multiple_of(r * 8, 8)
            ys = []
            for k in range(blocks + 1):
                pair = []
                for place in range(2):
                    row = place * tokens + at
                    top = spec_ref[k, pl.ds(row, 8), LANES:]
                    bottom = spec_ref[k, pl.ds(row + half, 8), LANES:]
                    pair.append(jnp.where(low, top, halves_swapped(bottom)))
                ys.append(tuple(pair))
            for a, total in enumerate(folded_sum(ys)):
                gf_ref[a, pl.ds(at, 8)] = total

        acc_ref[...] = jnp.zeros_like(acc_ref)

        def folded(values):
            total = values[:8]
            for r in range(1, tokens // 8):
                total = total + values[8 * r : 8 * r + 8]
            return total

        @pl.loop(0, blocks)
        def _(i):
            a = blocks - 1 - i
            one, two = window(a, 0), window(a, tokens)
            c1, c2 = window_conv(one, w1, tokens), window_conv(two, w2, tokens)
            lg = lg_ref[a]
            turned = halves_swapped(lg)
            x1, x2 = c2 * turned, c1 * turned
            ug = ug_ref[a]
            for j in range(3):
                acc_ref[j] += folded(x1 * one[8 - j : 8 - j + tokens])
                acc_ref[3 + j] += folded(x2 * two[8 - j : 8 - j + tokens])
            acc_ref[6] += folded(ug * halves_swapped(ug))
            after = acc_ref[7]
            out[a, :tokens] = lg.astype(out.dtype)
            out[a, tokens : tokens + half] = gf_ref[a].astype(out.dtype)
            out[a, tokens + half :] = jnp.concatenate(
                [after[:4], one[6:8], two[6:8], jnp.zeros((8, LANES), f32)], 0
            ).astype(out.dtype)
            acc_ref[7] = jnp.concatenate([x1[:2], x2[:2], jnp.zeros((4, LANES), f32)], 0)

        lower = lax.broadcasted_iota(jnp.int32, (1, LANES), 1) < HALF
        sums = [jnp.sum(acc_ref[j], axis=0, keepdims=True) for j in range(7)]
        sums[3] = jnp.where(lower, sums[3], sums[6])
        tail = jnp.concatenate(sums[:6] + [jnp.zeros((2, LANES), f32)], 0)

        @pl.loop(0, blocks)
        def _(a):
            rows = out[a, tokens + half :].astype(f32)
            out[a, tokens + half :] = jnp.concatenate([rows[:8], tail], 0).astype(out.dtype)


def resident_kernel(
    blocks, chunk, weights, tables_hbm, out,
    tables, raw_ref, zh_ref, zl_ref, spec_ref,
    s1_ref, s2_ref, c1_ref, c2_ref, ug_ref, lg_ref, gf_ref, acc_ref, sems,
):
    tokens = tables.shape[2]
    size = 2 * tokens
    half = tokens // 2
    f32, bf16 = jnp.float32, jnp.bfloat16
    copies = [
        pltpu.make_async_copy(tables_hbm.at[i], tables.at[i], sems.at[i]) for i in range(2)
    ]
    for copy in copies:
        copy.start()

    w1 = [weights[j : j + 1] for j in range(3)]
    w2 = [weights[3 + j : 4 + j] for j in range(3)]

    s1_ref[:8] = jnp.zeros((8, LANES), f32)
    s2_ref[:8] = jnp.zeros((8, LANES), f32)

    def earlier(ref, a, j):
        return ref[pl.ds(a * tokens + (8 - j), tokens)]

    def conv(ref, a, own, w):
        return w[0] * own + w[1] * earlier(ref, a, 1) + w[2] * earlier(ref, a, 2)

    acc_ref[...] = jnp.zeros_like(acc_ref)

    def folded(values):
        rows = [values[r : r + 8] for r in range(0, tokens, 8)]
        while len(rows) > 1:
            rows = [sum(rows[r : r + 2]) for r in range(0, len(rows), 2)]
        return rows[0]

    @pl.loop(0, blocks, unroll=blocks)
    def _(a):
        at = pl.multiple_of(a * tokens + 8, 8)
        one, two = chunk[a, :tokens].astype(f32), chunk[a, tokens : 2 * tokens].astype(f32)
        s1_ref[pl.ds(at, tokens)], s2_ref[pl.ds(at, tokens)] = one, two
        c1, c2 = conv(s1_ref, a, one, w1), conv(s2_ref, a, two, w2)
        c1_ref[a], c2_ref[a] = c1, c2
        ug = (c1 * c2).astype(bf16)
        ug_ref[a] = ug
        ug = ug.astype(f32)
        acc_ref[6] += folded(ug * halves_swapped(ug))

    def put(k, row, cols, values):
        raw_ref[k, pl.ds(row, 16), cols] = values

    left, right = slice(0, LANES), slice(LANES, 2 * LANES)

    @pl.loop(0, tokens // 16, unroll=2)
    def _(r):
        at = pl.multiple_of(r * 16, 16)
        spectrum = padded_dft([ug_ref[a, pl.ds(at, 16)].astype(f32) for a in range(blocks)])
        for k, (real, imag) in enumerate(spectrum):
            put(k, at, left, real)
            if imag is not None:
                put(k, tokens + at, left, imag)

    @pl.loop(0, half // 16, unroll=2)
    def _(r):
        at = pl.multiple_of(r * 16, 16)
        low = lax.broadcasted_iota(jnp.int32, (16, LANES), 1) < HALF
        spectrum = padded_dft(
            [chunk[a, pl.ds(2 * tokens + at, 16)].astype(f32) for a in range(blocks)]
        )
        for k, pair in enumerate(spectrum):
            for place, part in enumerate(pair):
                if part is None:
                    continue
                turned = halves_swapped(part)
                put(k, place * tokens + at, right, jnp.where(low, part, turned))
                put(k, place * tokens + half + at, right, jnp.where(low, turned, part))

    def whole_map(table, k, start):
        pair = tables[table, k, :, start : start + size]
        return jnp.concatenate(
            [pair, jnp.concatenate([-pair[:, tokens:], pair[:, :tokens]], 1)], 0
        )

    def is_real(k):
        return isinstance(k, int) and k in (0, blocks)

    def apply(table, k, high, rest):
        rows = tokens if is_real(k) and table == 1 else size
        depth = high.shape[0]
        first = whole_map(table, k, 0)[:rows, :depth]
        total = jnp.dot(first, high, preferred_element_type=f32)
        second = whole_map(table, k, size)[:rows, :depth]
        total = total + jnp.dot(second, high, preferred_element_type=f32)
        return total + jnp.dot(first, rest, preferred_element_type=f32)

    sign = jnp.where(lax.broadcasted_iota(jnp.int32, (1, LANES), 1) < HALF, 1.0, -1.0)

    def into_products(k, slot):
        raw = raw_ref[k, :tokens] if is_real(k) else raw_ref[k]
        coarse = raw.astype(bf16)
        spectral = apply(0, k, coarse, (raw - coarse.astype(f32)).astype(bf16))
        ur, ui = spectral[:tokens, :LANES], spectral[tokens:, :LANES]
        hr, hi = spectral[:tokens, LANES:], spectral[tokens:, LANES:] * sign
        vr, vi = halves_swapped(ur), halves_swapped(ui)
        for place, cols, values in (
            (0, left, ur * hr - ui * hi),
            (1, left, ui * hr + ur * hi),
            (0, right, ur * vr + ui * vi),
            (1, right, vi * ur - vr * ui),
        ):
            rows = slice(place * tokens, (place + 1) * tokens)
            high = values.astype(bf16)
            zh_ref[slot, rows, cols] = high
            zl_ref[slot, rows, cols] = (values - high.astype(f32)).astype(bf16)

    def out_of_products(k, slot):
        values = apply(1, k, zh_ref[slot], zl_ref[slot])
        spec_ref[k, : values.shape[0]] = values

    copies[0].wait()

    group = zh_ref.shape[0] // 2
    whole = (blocks + 1) // group
    rest = range(whole * group, blocks + 1)
    for j in range(group):
        into_products(j, j)
    copies[1].wait()

    for i in range(1, whole):
        now = i % 2 * group
        for j in range(group):
            out_of_products((i - 1) * group + j, group - now + j)
        for j in range(group):
            into_products(i * group + j, now + j)

    last = (whole - 1) % 2 * group
    for j, k in enumerate(rest):
        into_products(k, group - last + j)
    for j in range(group):
        out_of_products((whole - 1) * group + j, last + j)
    for j, k in enumerate(rest):
        out_of_products(k, group - last + j)

    skip = weights[6:7]
    low8 = lax.broadcasted_iota(jnp.int32, (8, LANES), 1) < HALF

    @pl.loop(0, tokens // 16, unroll=tokens // 16)
    def _(r):
        at = pl.multiple_of(r * 16, 16)
        ug = [ug_ref[a, pl.ds(at, 16)].astype(f32) for a in range(blocks)]
        for sub in range(2):
            row = pl.multiple_of(at + 8 * sub, 8)
            ys = [
                (spec_ref[k, pl.ds(row, 8), left], spec_ref[k, pl.ds(tokens + row, 8), left])
                for k in range(blocks + 1)
            ]
            for a, total in enumerate(folded_sum(ys)):
                lg_ref[a, pl.ds(row, 8)] = total + skip * ug[a][8 * sub : 8 * sub + 8]

    @pl.loop(0, half // 8, unroll=half // 8)
    def _(r):
        at = pl.multiple_of(r * 8, 8)
        ys = []
        for k in range(blocks + 1):
            pair = []
            for place in range(2):
                row = place * tokens + at
                top = spec_ref[k, pl.ds(row, 8), right]
                bottom = spec_ref[k, pl.ds(row + half, 8), right]
                pair.append(jnp.where(low8, top, halves_swapped(bottom)))
            ys.append(tuple(pair))
        for a, total in enumerate(folded_sum(ys)):
            gf_ref[a, pl.ds(at, 8)] = total

    @pl.loop(0, blocks, unroll=blocks)
    def _(i):
        a = blocks - 1 - i
        lg = lg_ref[a]
        turned = halves_swapped(lg)
        x1, x2 = c2_ref[a] * turned, c1_ref[a] * turned
        for j in range(3):
            acc_ref[j] += folded(x1 * earlier(s1_ref, a, j))
            acc_ref[3 + j] += folded(x2 * earlier(s2_ref, a, j))
        after = acc_ref[7]
        before = pl.multiple_of(a * tokens, 8)
        out[a, :tokens] = lg.astype(out.dtype)
        out[a, tokens : tokens + half] = gf_ref[a].astype(out.dtype)
        out[a, tokens + half :] = jnp.concatenate(
            [after[:4], s1_ref[pl.ds(before, 8)][6:], s2_ref[pl.ds(before, 8)][6:], jnp.zeros((8, LANES), f32)], 0
        ).astype(out.dtype)
        acc_ref[7] = jnp.concatenate([x1[:2], x2[:2], jnp.zeros((4, LANES), f32)], 0)

    lower = lax.broadcasted_iota(jnp.int32, (1, LANES), 1) < HALF
    sums = [jnp.sum(acc_ref[j], axis=0, keepdims=True) for j in range(7)]
    sums[3] = jnp.where(lower, sums[3], sums[6])
    tail = jnp.concatenate(sums[:6] + [jnp.zeros((2, LANES), f32)], 0)

    @pl.loop(0, blocks, unroll=blocks)
    def _(a):
        rows = out[a, tokens + half :].astype(f32)
        out[a, tokens + half :] = jnp.concatenate([rows[:8], tail], 0).astype(out.dtype)


def local_gates(streams, weights):
    tokens = streams[0].shape[0]
    gates = []
    for s, stream in enumerate(streams):
        window = jnp.concatenate([jnp.zeros_like(stream[:8]), stream], 0)
        gates.append(window_conv(window, weights[3 * s : 3 * s + 3], tokens))
    return gates


def finish(gates, cotangent, weights, low, high):
    tokens = cotangent.shape[0]
    half = tokens // 2
    at = tokens + half
    long_out, grad_mixed = low[:tokens], high[:tokens]
    grad_filter = jnp.concatenate([low[tokens:at], high[tokens:at]], 0)
    before = (high[at + 4 : at + 6], low[at + 4 : at + 6], low[at + 6 : at + 8])
    after = (high[at : at + 2], low[at : at + 2], low[at + 2 : at + 4])
    whole = []
    for s in range(3):
        older, newer = before[s][:1], before[s][1:]
        w1, w2 = weights[3 * s + 1], weights[3 * s + 2]
        missing = jnp.concatenate(
            [w1 * newer + w2 * older, w2 * newer, jnp.zeros((6, older.shape[1]), jnp.float32)], 0
        )
        whole.append(jnp.concatenate([gates[s][:8] + missing, gates[s][8:]], 0))
    mixed_out = whole[0] * long_out
    conv_grads = (cotangent * long_out, grad_mixed * whole[2], grad_mixed * whole[1])
    grads = []
    for s in range(3):
        trailing = jnp.concatenate([conv_grads[s], after[s], jnp.zeros_like(low[:6])], 0)
        total = weights[3 * s] * trailing[:tokens]
        for j in (1, 2):
            total = total + weights[3 * s + j] * trailing[j : j + tokens]
        grads.append(total)
    return [mixed_out] + grads + [grad_filter]


def token_sums(low, high):
    return [high[:3], low[:3], low[3:6], high[3:4]]


def gates_kernel(one, two, value, weights, after, gates):
    del after
    for pair in range(one.shape[1] // LANES):
        cols = slice(pair * LANES, (pair + 1) * LANES)
        results = local_gates(
            [ref[:, cols].astype(jnp.float32) for ref in (one, two, value)],
            [weights[i // 3, i % 3 : i % 3 + 1, cols] for i in range(9)],
        )
        for s, result in enumerate(results):
            gates[s, :, cols] = result


def finish_kernel(gates, grad, weights, back, *refs):
    targets, buffers, sems, sum_sems = refs[:7], refs[7:14], refs[14], refs[15]
    grad_taps, grad_skip = buffers[5:]
    pieces = sems.shape[1]
    width = grad.shape[1] // pieces

    def copy(i, piece):
        cols = pl.ds(piece * width, width)
        return pltpu.make_async_copy(buffers[i].at[:, cols], targets[i].at[:, cols], sems.at[i, piece])

    for owner in range(0, back.shape[0], 2):
        cols = slice(owner * HALF, (owner + 2) * HALF)
        last = [back[owner + side, -16:].astype(jnp.float32)[8:] for side in range(2)]
        totals = token_sums(*interleave(*last))
        for s in range(3):
            grad_taps[s, :, cols] = totals[s]
        grad_skip[:, cols] = totals[3]
    sum_copies = [
        pltpu.make_async_copy(buffers[5 + i], targets[5 + i], sum_sems.at[i]) for i in range(2)
    ]
    for small_copy in sum_copies:
        small_copy.start()

    for piece in range(pieces):
        for start in range(piece * width, (piece + 1) * width, LANES):
            cols = slice(start, start + LANES)
            owner = start // HALF
            low, high = interleave(
                back[owner].astype(jnp.float32), back[owner + 1].astype(jnp.float32)
            )
            results = finish(
                [gates[s, :, cols] for s in range(3)],
                grad[:, cols].astype(jnp.float32),
                [weights[i // 3, i % 3 : i % 3 + 1, cols] for i in range(9)],
                low,
                high,
            )
            for ref, result in zip(buffers, results[:5]):
                ref[:, cols] = result.astype(ref.dtype)
        for i in range(5):
            copy(i, piece).start()
    for piece in range(pieces):
        for i in range(5):
            copy(i, piece).wait()
    for small_copy in sum_copies:
        small_copy.wait()


VMEM = pl.BlockSpec(memory_space=pltpu.VMEM)
ANY = pl.BlockSpec(memory_space=pl.ANY)
HBM = pl.BlockSpec(memory_space=pltpu.HBM)


def per_device(stream_one, stream_two, stream_value, long_filter, short_taps, skip_gain, out_grad):
    blocks = lax.axis_size("seq")
    me = lax.axis_index("seq")
    tokens, channels = stream_one.shape
    half = tokens // 2
    owned = channels // blocks
    exact = owned == HALF
    bf16, f32 = jnp.bfloat16, jnp.float32
    rows_in = 2 * tokens + half
    rows_out = tokens + half + EXTRA
    taps_flat = short_taps.reshape(9, channels)

    def by_owner(array):
        split = array.reshape(array.shape[0], blocks, owned).transpose(1, 0, 2)
        return jnp.pad(split, ((0, 0), (0, 0), (0, HALF - owned)))

    def side_by_side(first, second):
        return jnp.concatenate([by_owner(first), by_owner(second)], 2)

    small = pltpu.CompilerParams(vmem_limit_bytes=16 * 1024 * 1024)
    steps = 2 if channels % 512 == 0 else 1
    by_columns = pl.BlockSpec((tokens, channels // steps), lambda i: (0, i))

    if exact:
        packed = pl.pallas_call(
            pack_kernel,
            out_shape=jax.ShapeDtypeStruct((blocks, rows_in, LANES), bf16),
            grid=(steps,),
            in_specs=[by_columns] * 5,
            out_specs=pl.BlockSpec((blocks // steps, rows_in, LANES), lambda i: (i, 0, 0)),
            name="pack",
        )(stream_one, stream_two, stream_value, long_filter, out_grad)
    else:
        packed = jnp.concatenate(
            [
                side_by_side(stream_two, stream_one),
                side_by_side(stream_value, out_grad),
                side_by_side(long_filter[:half], long_filter[half:]),
            ],
            1,
        )

    unit = jnp.zeros((3, channels), f32).at[0].set(1.0)
    lower = jnp.concatenate([taps_flat[3:9], skip_gain[None], skip_gain[None]], 0)
    upper = jnp.concatenate([taps_flat[:3], unit, skip_gain[None], skip_gain[None]], 0)
    weights = lax.dynamic_index_in_dim(side_by_side(lower, upper), me, 0, keepdims=False)

    owned_chunk = lax.all_to_all(packed, "seq", 0, 0, tiled=True)

    forward, inverse = dft_tables(blocks, tokens)
    size = 2 * tokens
    table_spec = pl.BlockSpec((1, tokens, 2 * size), lambda k: (k, 0, 0))

    if exact and blocks <= 16:
        group = 6

        def resident(*refs):
            resident_kernel(blocks, *refs)

        returned = pl.pallas_call(
            resident,
            out_shape=jax.ShapeDtypeStruct((blocks, rows_out, LANES), bf16),
            in_specs=[VMEM, VMEM, HBM],
            out_specs=VMEM,
            scratch_shapes=[
                pltpu.VMEM((2, blocks + 1, tokens, 2 * size), bf16),
                pltpu.VMEM((blocks + 1, size, 2 * LANES), f32),
                pltpu.VMEM((2 * group, size, 2 * LANES), bf16),
                pltpu.VMEM((2 * group, size, 2 * LANES), bf16),
                pltpu.VMEM((blocks + 1, size, 2 * LANES), f32),
                pltpu.VMEM((blocks * tokens + 8, LANES), f32),
                pltpu.VMEM((blocks * tokens + 8, LANES), f32),
                pltpu.VMEM((blocks, tokens, LANES), f32),
                pltpu.VMEM((blocks, tokens, LANES), f32),
                pltpu.VMEM((blocks, tokens, LANES), bf16),
                pltpu.VMEM((blocks, tokens, LANES), f32),
                pltpu.VMEM((blocks, half, LANES), f32),
                pltpu.VMEM((8, 8, LANES), f32),
                pltpu.SemaphoreType.DMA((2,)),
            ],
            compiler_params=pltpu.CompilerParams(vmem_limit_bytes=48 * 1024 * 1024),
            name="owner",
        )(owned_chunk, weights, jnp.asarray(np.stack([forward, inverse])))
    else:

        def owner(*refs):
            owner_kernel(blocks, *refs)

        returned = pl.pallas_call(
            owner,
            out_shape=jax.ShapeDtypeStruct((blocks, rows_out, LANES), bf16),
            grid=(blocks + 1,),
            in_specs=[VMEM, VMEM, table_spec, table_spec],
            out_specs=VMEM,
            scratch_shapes=[
                pltpu.VMEM((blocks, tokens, LANES), f32),
                pltpu.VMEM((blocks + 1, size, 2 * LANES), f32),
                pltpu.VMEM((blocks, tokens, LANES), f32),
                pltpu.VMEM((blocks, half, LANES), f32),
                pltpu.VMEM((8, 8, LANES), f32),
            ],
            compiler_params=pltpu.CompilerParams(vmem_limit_bytes=58 * 1024 * 1024),
            name="owner",
        )(owned_chunk, weights, jnp.asarray(forward), jnp.asarray(inverse))

    back = lax.all_to_all(returned, "seq", 0, 0, tiled=True)

    if exact:
        shape = (tokens, channels)
        taps_spec = pl.BlockSpec((3, 3, channels // steps), lambda i: (0, 0, i))
        gates_spec = pl.BlockSpec((3, tokens, channels // steps), lambda i: (0, 0, i))
        gates = pl.pallas_call(
            gates_kernel,
            out_shape=jax.ShapeDtypeStruct((3,) + shape, f32),
            grid=(steps,),
            in_specs=[by_columns] * 3 + [taps_spec, ANY],
            out_specs=gates_spec,
            compiler_params=small,
            name="gates",
        )(stream_one, stream_two, stream_value, short_taps, returned)
        results = pl.pallas_call(
            finish_kernel,
            out_shape=[jax.ShapeDtypeStruct(shape, bf16)] * 4
            + [
                jax.ShapeDtypeStruct(shape, f32),
                jax.ShapeDtypeStruct(short_taps.shape, f32),
                jax.ShapeDtypeStruct((1, channels), f32),
            ],
            in_specs=[VMEM] * 4,
            out_specs=[ANY] * 7,
            scratch_shapes=[pltpu.VMEM(shape, bf16)] * 4
            + [
                pltpu.VMEM(shape, f32),
                pltpu.VMEM(short_taps.shape, f32),
                pltpu.VMEM((1, channels), f32),
                pltpu.SemaphoreType.DMA((5, 4)),
                pltpu.SemaphoreType.DMA((2,)),
            ],
            compiler_params=small,
            name="finish",
        )(gates, out_grad, short_taps, back)
    else:
        wide = back.astype(f32)

        def joined(part):
            return part[:, :, :owned].transpose(1, 0, 2).reshape(rows_out, channels)

        low, high = joined(wide[:, :, :HALF]), joined(wide[:, :, HALF:])
        rows = [taps_flat[i : i + 1] for i in range(9)]
        streams = [s.astype(f32) for s in (stream_one, stream_two, stream_value)]
        results = finish(local_gates(streams, rows), out_grad.astype(f32), rows, low, high)
        totals = token_sums(low[-8:], high[-8:])
        results = [r.astype(bf16) for r in results[:4]] + [
            results[4],
            jnp.stack(totals[:3]),
            totals[3],
        ]
    return tuple(results[:6]) + (results[6].reshape(channels),)


def solution(mesh):
    rows = P("seq", "ch")
    return jax.shard_map(
        per_device,
        mesh=mesh,
        in_specs=(rows, rows, rows, rows, P(None, None, "ch"), P("ch"), rows),
        out_specs=(rows, rows, rows, rows, rows, P(None, None, "ch"), P("ch")),
        check_vma=False,
    )
```
